256 devices in a mesh: grp: 16 (over x_hi, z), blk: 16 (over x_lo, y, core).
Axes of the slice: x: 4 (x_hi: 2, x_lo: 2; x = x_hi * 2 + x_lo), y: 4, z: 8, core: 2. Of those that a mesh axis runs over, the one named last changes fastest.
Arguments:
- prompt_of: int32 [2048], P(('grp', 'blk')), may hold values from 0 to 31, as said below
- suffix_len: int32 [2048], P(('grp', 'blk')), may hold values from 1 to 256, as said below
- query: bfloat16 [2048, 4096], P(('grp', 'blk')), may hold values from -8 to 23
- new_key: bfloat16 [2048, 512], P(('grp', 'blk')), may hold values from -5 to 6
- new_value: bfloat16 [2048, 512], P(('grp', 'blk')), may hold values from -6 to 6
- suffix_key: bfloat16 [2048, 256, 512], P(('grp', 'blk')), may hold values from -5 to 6
- suffix_value: bfloat16 [2048, 256, 512], P(('grp', 'blk')), may hold values from -6 to 6
- prefix_key: bfloat16 [32, 4096, 512], P('grp', 'blk'), may hold values from -5 to 6
- prefix_value: bfloat16 [32, 4096, 512], P('grp', 'blk'), may hold values from -6 to 6
Outputs:
- attended: bfloat16 [2048, 4096], P(('grp', 'blk'))
The draws below stay inside these ranges and needn't reach their ends.
Inputs may be any that keep to these rules, and one draw needn't show every extreme that they name: `prompt_of`: on every device at most 2 of its completions name prompts of one group (the group of a prompt is prompt // 2); one group gets exactly 2 from every device. `suffix_len`: some completion has exactly 256 cached suffix tokens.
All inputs are finite; a program needn't handle non-finite values.
Results may differ from the reference program's by a relative error of at most 0.0037.
Values may be sent and summed in bfloat16 or wider, within the bound.
No kernel may reach another device: no remote copies, remote signals or barrier semaphores. Data moves between devices by JAX's collectives and lax.ppermute only.
A program may use at most 128 MiB of HBM per device.

```python
from functools import partial
import jax
import jax.numpy as jnp
from jax import lax

QH = 32
KVH = 4
HD = 128
C_DEV = 8
CAP = 2
PR_GRP = 2
SUF = 256
PROMPTS = 32
PLEN = 4096
COMPL = 2048
N_GRP = 16
N_BLK = 16


def clipped_normal(key, dims):
    values = jnp.clip(jax.random.normal(key, dims, jnp.float32), -5.0, 5.0)
    return values


def draw_prompt_of(key, part):
    key = jax.random.fold_in(key, 11)
    blocks = N_GRP * N_BLK
    hot_key, spread_key, shuffle_key, pick_key = jax.random.split(key, 4)
    hot_group = jax.random.randint(hot_key, (), 0, N_GRP)
    spread_keys = jax.random.split(spread_key, blocks)
    pooled = jax.vmap(lambda sub_key: jax.random.permutation(sub_key, 2 * (N_GRP - 1)))(spread_keys)
    others = (hot_group + 1 + pooled[:, :C_DEV - CAP] % (N_GRP - 1)) % N_GRP
    groups = jnp.concatenate([jnp.full((blocks, CAP), hot_group, jnp.int32), others.astype(jnp.int32)], axis=1)
    shuffle = jax.vmap(lambda sub_key: jax.random.permutation(sub_key, C_DEV))(jax.random.split(shuffle_key, blocks))
    groups = jnp.take_along_axis(groups, shuffle, axis=1)
    within = jax.random.randint(pick_key, (blocks, C_DEV), 0, PR_GRP)
    return (groups * PR_GRP + within).reshape(blocks * C_DEV).astype(jnp.int32)


def draw_suffix_len(key, part):
    key = jax.random.fold_in(key, 12)
    length_key, spot_key = jax.random.split(key)
    lengths = jax.random.randint(length_key, (COMPL,), 1, SUF + 1)
    longest = jax.random.randint(spot_key, (), 0, COMPL)
    return lengths.at[longest].set(SUF).astype(jnp.int32)


def draw_query(key, part):
    key = jax.random.fold_in(key, 31)
    noise_key = jax.random.fold_in(key, 0)
    array_dims = (COMPL, QH, HD)
    values = jnp.clip(2.0 * jax.random.normal(noise_key, array_dims, jnp.float32), -8.0, 8.0)
    return values.reshape(COMPL, QH * HD).astype(jnp.bfloat16)


def draw_new_key(key, part):
    key = jax.random.fold_in(key, 41)
    return clipped_normal(key, (COMPL, KVH * HD)).astype(jnp.bfloat16)


def draw_suffix_key(key, part):
    key = jax.random.fold_in(key, 42)
    return clipped_normal(key, (COMPL, SUF, KVH * HD)).astype(jnp.bfloat16)


def draw_prefix_key(key, part):
    key = jax.random.fold_in(key, 43)
    return clipped_normal(key, (PROMPTS, PLEN, KVH * HD)).astype(jnp.bfloat16)


def steps_of(key, extent, shards, low, top_value):
    def one(dim, blocks):
        draws = jax.random.uniform(jax.random.fold_in(jax.random.fold_in(key, 6), dim), (blocks,), jnp.float32, low / len(shards), top_value / len(shards))
        return jnp.repeat(jnp.exp(draws), extent[dim] // blocks).reshape((-1,) + (1,) * (len(extent) - dim - 1))

    loudness = one(*shards[0])
    for cut in shards[1:]:
        loudness = loudness * one(*cut)
    return loudness


def normal_values(stream_key, extent, deviation, reach, pieces=(), kind=jnp.bfloat16):
    result = jax.random.normal(stream_key, extent, jnp.float32) * deviation
    if len(pieces) > 0:
        result = steps_of(stream_key, extent, pieces, -0.22, 0.18) * result
    return jnp.clip(result, min=-reach, max=reach).astype(kind)


def setup_inputs(seed: int = 0) -> dict:
    streams_of = jax.random.split(jax.random.key(seed), 10)
    prompt_of = draw_prompt_of(jax.random.fold_in(streams_of[9], 71), 0)
    suffix_len = draw_suffix_len(jax.random.fold_in(streams_of[9], 71), 0)
    query = draw_query(jax.random.fold_in(streams_of[9], 71), 0)
    new_key = draw_new_key(jax.random.fold_in(streams_of[9], 71), 0)
    new_value = normal_values(streams_of[4], (COMPL, KVH * HD), 1.0, 6.0, ((0, 256),))
    suffix_key = draw_suffix_key(jax.random.fold_in(streams_of[9], 71), 0)
    suffix_value = normal_values(streams_of[6], (COMPL, SUF, KVH * HD), 1.0, 6.0, ((0, 256),))
    prefix_key = draw_prefix_key(jax.random.fold_in(streams_of[9], 71), 0)
    prefix_value = normal_values(streams_of[8], (PROMPTS, PLEN, KVH * HD), 1.0, 6.0, ((0, 16), (1, 16)))
    return dict(prompt_of=prompt_of, suffix_len=suffix_len, query=query, new_key=new_key, new_value=new_value, suffix_key=suffix_key, suffix_value=suffix_value, prefix_key=prefix_key, prefix_value=prefix_value)


NEG = -1.0e30


def rounded(values):
    return lax.optimization_barrier(values.astype(jnp.bfloat16)).astype(jnp.float32)


def attend(prefix_key, prefix_value, inputs):
    prompt_id, length, query_row, own_key, own_value, cache_key, cache_value = inputs
    group_ratio = QH // KVH
    scaling = HD ** -0.5
    query_heads = query_row.astype(jnp.float32).reshape(KVH, group_ratio, HD)
    far_keys = lax.dynamic_index_in_dim(prefix_key, prompt_id.astype(jnp.int32), 0, keepdims=False).astype(jnp.float32).reshape(PLEN, KVH, HD)
    far_values = lax.dynamic_index_in_dim(prefix_value, prompt_id.astype(jnp.int32), 0, keepdims=False).astype(jnp.float32).reshape(PLEN, KVH, HD)
    far_scores = jnp.einsum("kgd,tkd->kgt", query_heads, far_keys) * scaling
    far_max = jnp.max(far_scores, axis=2)
    far_weights = jnp.exp(far_scores - far_max[:, :, None])
    far_total = jnp.sum(far_weights, axis=2)
    far_out = jnp.einsum("kgt,tkd->kgd", rounded(far_weights), far_values)
    near_keys = cache_key.astype(jnp.float32).reshape(SUF, KVH, HD)
    near_values = cache_value.astype(jnp.float32).reshape(SUF, KVH, HD)
    near_scores = jnp.einsum("kgd,tkd->kgt", query_heads, near_keys) * scaling
    live_mask = jnp.arange(SUF, dtype=jnp.int32) < length.astype(jnp.int32)
    near_scores = jnp.where(live_mask[None, None, :], near_scores, NEG)
    own_score = jnp.einsum("kgd,kd->kg", query_heads, own_key.astype(jnp.float32).reshape(KVH, HD)) * scaling
    near_max = jnp.maximum(jnp.max(near_scores, axis=2), own_score)
    near_weights = jnp.where(live_mask[None, None, :], jnp.exp(near_scores - near_max[:, :, None]), 0.0)
    own_weight = jnp.exp(own_score - near_max)
    near_total = jnp.sum(near_weights, axis=2) + own_weight
    near_out = jnp.einsum("kgt,tkd->kgd", rounded(near_weights), near_values)
    near_out = near_out + rounded(own_weight)[:, :, None] * own_value.astype(jnp.float32).reshape(KVH, 1, HD)
    top_max = jnp.maximum(far_max, near_max)
    far_scale = jnp.exp(far_max - top_max)
    near_scale = jnp.exp(near_max - top_max)
    numerator = far_out * far_scale[:, :, None] + near_out * near_scale[:, :, None]
    denominator = far_total * far_scale + near_total * near_scale
    return (numerator / denominator[:, :, None]).reshape(QH * HD).astype(jnp.bfloat16)


def reference(prompt_of, suffix_len, query, new_key, new_value, suffix_key, suffix_value, prefix_key, prefix_value):
    return lax.map(partial(attend, prefix_key, prefix_value), (prompt_of, suffix_len, query, new_key, new_value, suffix_key, suffix_value))
```

```python
import jax
import jax.numpy as jnp
from jax import lax
from jax.experimental import pallas as pl
from jax.experimental.pallas import tpu as pltpu
from jax.sharding import Mesh, PartitionSpec as P

HD = 128
CAP = 2
HELD = 8
HEADS = 32
KVH = 4
RATIO = 8
PROMPTS = 32
PARTS = 8
PART_HEADS = 4
DEVICES = 256
SUF = 256
PIECE = 256
ROWS = DEVICES * CAP * PART_HEADS
NEG = -1e30
SCALE = HD ** (-0.5)
LOG2E = 1.4426950408889634
LN2 = 0.6931471805599453
ALL = ("xh", "z", "xl", "y", "c")
NEAR = ("xl", "y")


def slots_of(prompt_ref):
    prompts = [prompt_ref[i] for i in range(HELD)]
    slots = []
    for i in range(HELD):
        rank = jnp.int32(0)
        for j in range(i):
            rank = rank + jnp.where(prompts[j] == prompts[i], 1, 0)
        slots.append(prompts[i] * CAP + rank)
    return slots


def spread(values, index):
    picked = jnp.zeros(index.shape, jnp.int32)
    for i, value in enumerate(values):
        picked = jnp.where(index == i, value, picked)
    return picked


def pack_kernel(prompt_ref, query_ref, out_ref):
    slots = slots_of(prompt_ref)
    held = jnp.concatenate(
        [query_ref[:, h * HD : (h + 1) * HD].astype(jnp.float32) for h in range(HEADS)], axis=0
    ).astype(jnp.bfloat16)
    lane = lax.broadcasted_iota(jnp.int32, (1, HEADS * HELD), 1)
    lane_key = (lane >> 3) * 64 + spread(slots, lane & 7)
    chunk = 512
    for start in range(0, ROWS, chunk):
        row = lax.broadcasted_iota(jnp.int32, (chunk, 1), 0) + start
        head = ((row >> 3) & 7) * 4 + (row & 3)
        slot = (row >> 6) * 2 + ((row >> 2) & 1)
        select = (head * 64 + slot == lane_key).astype(jnp.float32).astype(jnp.bfloat16)
        out_ref[start : start + chunk, :] = jnp.dot(
            select, held, preferred_element_type=jnp.float32
        ).astype(jnp.bfloat16)


def cut_kernel(place_ref, key_ref, value_ref, *out_refs):
    place = place_ref[0]
    for step, out_ref in enumerate(out_refs):
        target = place ^ step
        prompt = target >> 2
        column = pl.multiple_of((target & 3) * HD, HD)
        out_ref[0] = key_ref[prompt, :, pl.ds(column, HD)]
        out_ref[1] = value_ref[prompt, :, pl.ds(column, HD)]


def near_kernel(len_ref, query_ref, new_key_ref, new_value_ref, key_ref, value_ref, out_ref, lse_ref):
    step = pl.program_id(0)
    length = len_ref[step]
    query = query_ref[0]
    keys = key_ref[0]
    values = value_ref[0]
    new_key = new_key_ref[pl.ds(step, 1), :]
    new_value = new_value_ref[pl.ds(step, 1), :]

    def spread_heads(row):
        return jnp.concatenate(
            [jnp.broadcast_to(row[:, k * HD : (k + 1) * HD], (RATIO, HD)) for k in range(KVH)], axis=0
        )

    scores = jnp.concatenate(
        [
            lax.dot_general(
                query,
                keys[:, k * HD : (k + 1) * HD],
                (((1,), (1,)), ((), ())),
                preferred_element_type=jnp.float32,
            )[k * RATIO : (k + 1) * RATIO]
            for k in range(KVH)
        ],
        axis=0,
    ) * SCALE
    own = jnp.sum(query.astype(jnp.float32) * spread_heads(new_key), axis=1, keepdims=True) * SCALE
    live = lax.broadcasted_iota(jnp.int32, (1, SUF), 1) < length
    scores = jnp.where(live, scores, NEG)
    top = jnp.maximum(jnp.max(scores, axis=1, keepdims=True), own)
    weights = jnp.where(live, jnp.exp(scores - top), 0.0)
    own_weight = jnp.exp(own - top)
    total = jnp.sum(weights, axis=1, keepdims=True) + own_weight
    rounded = weights.astype(jnp.bfloat16)
    mixed = jnp.concatenate(
        [
            jnp.dot(rounded, values[:, k * HD : (k + 1) * HD], preferred_element_type=jnp.float32)[
                k * RATIO : (k + 1) * RATIO
            ]
            for k in range(KVH)
        ],
        axis=0,
    )
    mixed = mixed + own_weight.astype(jnp.bfloat16).astype(jnp.float32) * spread_heads(new_value)
    out_ref[:, pl.ds(step, 1), :] = (mixed / total).reshape(HEADS, 1, HD)
    lse_ref[:, pl.ds(step, 1), :] = jnp.broadcast_to(top + jnp.log(total), (HEADS, HD)).reshape(
        HEADS, 1, HD
    )


def far_kernel(query_ref, *refs):
    pieces = refs[:-3]
    out_ref, stat_ref, score_ref = refs[-3:]
    block = 256

    @pl.loop(0, ROWS // block)
    def _(index):
        start = pl.multiple_of(index * block, block)
        query = query_ref[pl.ds(start, block), :]
        peak = jnp.full((block, HD), -jnp.inf, jnp.float32)
        for n, piece in enumerate(pieces):
            scores = lax.dot_general(
                query, piece[0], (((1,), (1,)), ((), ())), preferred_element_type=jnp.float32
            )
            score_ref[n] = scores
            peak = jnp.maximum(peak, jnp.maximum(scores[:, :HD], scores[:, HD:]))
        peak = jnp.max(peak, axis=1, keepdims=True)
        total = jnp.zeros((block, HD), jnp.float32)
        mixed = jnp.zeros((block, HD), jnp.float32)
        for n, piece in enumerate(pieces):
            weights = jnp.exp2((score_ref[n] - peak) * (SCALE * LOG2E))
            total = total + (weights[:, :HD] + weights[:, HD:])
            mixed = mixed + jnp.dot(
                weights.astype(jnp.bfloat16), piece[1], preferred_element_type=jnp.float32
            )
        total = jnp.sum(total, axis=1, keepdims=True)
        out_ref[pl.ds(start, block), :] = (mixed / total).astype(jnp.bfloat16)
        lse = peak * SCALE + jnp.log(total)
        high = lse.astype(jnp.bfloat16).astype(jnp.float32)
        rest = lse - high
        middle = rest.astype(jnp.bfloat16).astype(jnp.float32)
        low = rest - middle
        lane = lax.broadcasted_iota(jnp.int32, (block, HD), 1)
        row = lax.broadcasted_iota(jnp.int32, (block, HD), 0) & 7
        stat = jnp.where(
            lane == row,
            high,
            jnp.where(lane == row + 8, middle, jnp.where(lane == row + 16, low, 0.0)),
        )
        stat = jnp.sum(stat.reshape(block // 8, 8, HD), axis=1)
        stat_ref[pl.ds(pl.multiple_of(index * (block // 8), block // 8), block // 8), :] = stat.astype(
            jnp.bfloat16
        )


def merge_kernel(prompt_ref, back_ref, near_ref, near_lse_ref, out_ref):
    slots = slots_of(prompt_ref)
    count = HEADS * HELD
    row = lax.broadcasted_iota(jnp.int32, (count, 1), 0)
    slot = spread(slots, row & 7)
    head = row >> 3
    lane = lax.broadcasted_iota(jnp.int32, (1, ROWS), 1)
    source = (lane >> 1) & 255
    inner = (lane >> 9) * 2 + (lane & 1)
    lane_key = ((source & 7) * 4 + (inner & 3)) * 64 + (source >> 3) * 2 + (inner >> 2)
    select = (head * 64 + slot == lane_key).astype(jnp.float32).astype(jnp.bfloat16)
    far = jnp.dot(select, back_ref[:ROWS, :], preferred_element_type=jnp.float32)
    stat_lane = lax.broadcasted_iota(jnp.int32, (1, 2 * DEVICES), 1)
    stat_select = (((slot >> 1) * 8 + (head >> 2)) * 2 == stat_lane).astype(jnp.float32).astype(jnp.bfloat16)
    stat = jnp.dot(stat_select, back_ref[ROWS:, :], preferred_element_type=jnp.float32)
    wide = lax.broadcasted_iota(jnp.int32, (count, HD), 1)
    mine = ((wide & 7) == (slot & 1) * 4 + (head & 3)) & (wide < 24)
    far_lse = jnp.sum(jnp.where(mine, stat, 0.0), axis=1, keepdims=True)
    near_lse = near_lse_ref[...].reshape(count, HD)
    top = jnp.maximum(far_lse, near_lse)
    far_scale = jnp.exp(far_lse - top)
    near_scale = jnp.exp(near_lse - top)
    merged = (far * far_scale + near_ref[...].reshape(count, HD) * near_scale) / (far_scale + near_scale)
    for h in range(HEADS):
        out_ref[:, h * HD : (h + 1) * HD] = merged[h * HELD : (h + 1) * HELD].astype(jnp.bfloat16)


VMEM = pl.BlockSpec(memory_space=pltpu.VMEM)
SMEM = pl.BlockSpec(memory_space=pltpu.SMEM)


def params(mib):
    return pltpu.CompilerParams(vmem_limit_bytes=mib << 20)


def shards(
    prompt_of,
    suffix_len,
    query,
    new_key,
    new_value,
    suffix_key,
    suffix_value,
    prefix_key,
    prefix_value,
):
    place = lax.axis_index(NEAR).astype(jnp.int32).reshape(1)
    cuts = pl.pallas_call(
        cut_kernel,
        out_shape=[jax.ShapeDtypeStruct((2, PIECE, HD), jnp.bfloat16)] * 8,
        in_specs=[SMEM, VMEM, VMEM],
        out_specs=[VMEM] * 8,
        compiler_params=params(16),
        name="cut",
    )(place, prefix_key, prefix_value)
    outgoing = pl.pallas_call(
        pack_kernel,
        out_shape=jax.ShapeDtypeStruct((ROWS, HD), jnp.bfloat16),
        in_specs=[SMEM, VMEM],
        out_specs=VMEM,
        compiler_params=params(16),
        name="pack",
    )(prompt_of, query)
    arrived = lax.all_to_all(outgoing.reshape(DEVICES, 8, HD), ALL, 0, 0, tiled=True)
    held = [cuts[0]]
    for step in range(1, 8):
        held.append(lax.ppermute(cuts[step], NEAR, [(i, i ^ step) for i in range(8)]))
    swapped = [lax.ppermute(piece, "c", [(0, 1), (1, 0)]) for piece in held]

    near_out, near_lse = pl.pallas_call(
        near_kernel,
        grid=(HELD,),
        out_shape=[jax.ShapeDtypeStruct((HEADS, HELD, HD), jnp.float32)] * 2,
        in_specs=[
            SMEM,
            pl.BlockSpec((1, HEADS, HD), lambda i: (i, 0, 0)),
            pl.BlockSpec((HELD, KVH * HD), lambda i: (0, 0)),
            pl.BlockSpec((HELD, KVH * HD), lambda i: (0, 0)),
            pl.BlockSpec((1, SUF, KVH * HD), lambda i: (i, 0, 0)),
            pl.BlockSpec((1, SUF, KVH * HD), lambda i: (i, 0, 0)),
        ],
        out_specs=[pl.BlockSpec((HEADS, HELD, HD), lambda i: (0, 0, 0))] * 2,
        compiler_params=params(16),
        cost_estimate=pl.CostEstimate(flops=300_000_000, bytes_accessed=4_500_000, transcendentals=65536),
        name="near",
    )(
        suffix_len,
        query.reshape(HELD, HEADS, HD),
        new_key.astype(jnp.float32),
        new_value.astype(jnp.float32),
        suffix_key,
        suffix_value,
    )

    far_out, far_stat = pl.pallas_call(
        far_kernel,
        out_shape=[
            jax.ShapeDtypeStruct((ROWS, HD), jnp.bfloat16),
            jax.ShapeDtypeStruct((DEVICES, HD), jnp.bfloat16),
        ],
        in_specs=[VMEM] * 17,
        out_specs=[VMEM] * 2,
        scratch_shapes=[pltpu.VMEM((16, 256, PIECE), jnp.float32)],
        compiler_params=params(32),
        name="far",
    )(arrived.reshape(ROWS, HD), *held, *swapped)
    parcel = jnp.concatenate(
        [
            far_out.reshape(DEVICES, 4, 2, HD),
            jnp.broadcast_to(far_stat.reshape(DEVICES, 1, 1, HD), (DEVICES, 1, 2, HD)),
        ],
        axis=1,
    )
    back = lax.all_to_all(parcel, ALL, 0, 0, tiled=True)
    back = back.transpose(1, 0, 2, 3).reshape(10 * DEVICES, HD)
    return pl.pallas_call(
        merge_kernel,
        out_shape=jax.ShapeDtypeStruct((HELD, HEADS * HD), jnp.bfloat16),
        in_specs=[SMEM, VMEM, VMEM, VMEM],
        out_specs=VMEM,
        compiler_params=params(16),
        name="merge",
    )(prompt_of, back, near_out, near_lse)


def solution(mesh):
    fine = Mesh(mesh.devices.reshape(2, 8, 2, 4, 2), ALL)
    grp = ("xh", "z")
    blk = ("xl", "y", "c")
    in_specs = (
        P(ALL),
        P(ALL),
        P(ALL, None),
        P(ALL, None),
        P(ALL, None),
        P(ALL, None, None),
        P(ALL, None, None),
        P(grp, blk, None),
        P(grp, blk, None),
    )
    return jax.shard_map(
        shards, mesh=fine, in_specs=in_specs, out_specs=P(ALL, None), check_vma=False
    )
```

```python
import math

import jax
import jax.numpy as jnp
from jax import lax
from jax.experimental import pallas as pl
from jax.experimental.pallas import tpu as pltpu
from jax.sharding import Mesh, PartitionSpec as P

HD = 128
CAP = 2
HELD = 8
HEADS = 32
KVH = 4
RATIO = 8
PROMPTS = 32
SUF = 256
PIECE = 256
SLOTS = 256
ROWS = SLOTS * RATIO
NEG = -1e30
SCALE = HD ** (-0.5)
LOG2E = 1.4426950408889634
ALL = ("xh", "z", "xl", "y", "c")
NEAR = ("xl", "y")
FAR = ("xh", "z", "xl")


def slots_of(prompt_ref):
    prompts = [prompt_ref[i] for i in range(HELD)]
    slots = []
    for i in range(HELD):
        rank = jnp.int32(0)
        for j in range(i):
            rank = rank + jnp.where(prompts[j] == prompts[i], 1, 0)
        slots.append(prompts[i] * CAP + rank)
    return slots


def spread(values, index):
    picked = jnp.zeros(index.shape, jnp.int32)
    for i, value in enumerate(values):
        picked = jnp.where(index == i, value, picked)
    return picked


def prep_kernel(place_ref, prompt_ref, query_ref, key_ref, value_ref, send_ref, *cut_refs):
    slots = slots_of(prompt_ref)
    lane = lax.broadcasted_iota(jnp.int32, (HELD, HD), 1)
    row = lax.broadcasted_iota(jnp.int32, (HELD, HD), 0)
    tags = jnp.concatenate(
        [spread(slots, lane & 7).astype(jnp.float32), spread(slots, row).astype(jnp.float32)], axis=0
    ).astype(jnp.bfloat16)
    for y in range(KVH):
        send_ref[y, :64] = jnp.concatenate(
            [
                query_ref[:, h * HD : (h + 1) * HD].astype(jnp.float32)
                for h in range(y * RATIO, (y + 1) * RATIO)
            ],
            axis=0,
        ).astype(jnp.bfloat16)
        send_ref[y, 64:] = tags
    place = place_ref[0]
    for step, cut_ref in enumerate(cut_refs):
        target = place ^ step
        prompt = target >> 2
        column = pl.multiple_of((target & 3) * HD, HD)
        cut_ref[0] = key_ref[prompt, :, pl.ds(column, HD)]
        cut_ref[1] = value_ref[prompt, :, pl.ds(column, HD)]


def pack_kernel(got_ref, out_ref):
    held = got_ref[:, :64].reshape(256, HD)
    tags = [got_ref[y, 64:].astype(jnp.float32)[:1].astype(jnp.int32) for y in range(KVH)]
    half = lax.broadcasted_iota(jnp.int32, (1, HD), 1) < 64
    tag = jnp.concatenate([jnp.where(half, tags[0], tags[1]), jnp.where(half, tags[2], tags[3])], axis=1)
    lane_key = (lax.broadcasted_iota(jnp.int32, (1, 256), 1) >> 3) * 64 + tag
    chunk = 512
    for start in range(0, ROWS, chunk):
        row = lax.broadcasted_iota(jnp.int32, (chunk, 1), 0) + start
        row_key = ((row >> 1) & 3) * 512 + ((row >> 3) & 7) * 64 + (row >> 6) * 2 + (row & 1)
        select = (row_key == lane_key).astype(jnp.float32).astype(jnp.bfloat16)
        out_ref[start : start + chunk, :] = jnp.dot(
            select, held, preferred_element_type=jnp.float32
        ).astype(jnp.bfloat16)


def near_kernel(len_ref, query_ref, new_key_ref, new_value_ref, key_ref, value_ref, out_ref, lse_ref):
    step = pl.program_id(0)
    length = len_ref[step]
    query = query_ref[0]
    keys = key_ref[0]
    values = value_ref[0]
    new_key = new_key_ref[pl.ds(step, 1), :]
    new_value = new_value_ref[pl.ds(step, 1), :]

    def spread_heads(row):
        return jnp.concatenate(
            [jnp.broadcast_to(row[:, k * HD : (k + 1) * HD], (RATIO, HD)) for k in range(KVH)], axis=0
        )

    scores = jnp.concatenate(
        [
            lax.dot_general(
                query,
                keys[:, k * HD : (k + 1) * HD],
                (((1,), (1,)), ((), ())),
                preferred_element_type=jnp.float32,
            )[k * RATIO : (k + 1) * RATIO]
            for k in range(KVH)
        ],
        axis=0,
    ) * SCALE
    own = jnp.sum(query.astype(jnp.float32) * spread_heads(new_key), axis=1, keepdims=True) * SCALE
    live = lax.broadcasted_iota(jnp.int32, (1, SUF), 1) < length
    scores = jnp.where(live, scores, NEG)
    top = jnp.maximum(jnp.max(scores, axis=1, keepdims=True), own)
    weights = jnp.where(live, jnp.exp(scores - top), 0.0)
    own_weight = jnp.exp(own - top)
    total = jnp.sum(weights, axis=1, keepdims=True) + own_weight
    rounded = weights.astype(jnp.bfloat16)
    mixed = jnp.concatenate(
        [
            jnp.dot(rounded, values[:, k * HD : (k + 1) * HD], preferred_element_type=jnp.float32)[
                k * RATIO : (k + 1) * RATIO
            ]
            for k in range(KVH)
        ],
        axis=0,
    )
    mixed = mixed + own_weight.astype(jnp.bfloat16).astype(jnp.float32) * spread_heads(new_value)
    out_ref[:, pl.ds(step, 1), :] = (mixed / total).reshape(HEADS, 1, HD)
    lse_ref[:, pl.ds(step, 1), :] = jnp.broadcast_to(top + jnp.log(total), (HEADS, HD)).reshape(
        HEADS, 1, HD
    )


def far_kernel(query_ref, *refs):
    pieces = refs[:16]
    out_ref, score_ref, query_scr, mixed_scr, stat_scr = refs[16:]
    span = 32
    block = span * RATIO
    tokens = 16 * PIECE
    queries = query_ref[...].astype(jnp.float32).reshape(32, RATIO, 8, HD)
    biggest = jnp.max(jnp.max(jnp.abs(queries), axis=1).reshape(SLOTS, HD), axis=1, keepdims=True)
    valid = (biggest > 0).astype(jnp.float32)
    row = lax.broadcasted_iota(jnp.int32, (SLOTS, SLOTS), 0)
    lane = lax.broadcasted_iota(jnp.int32, (SLOTS, SLOTS), 1)
    wide = jnp.broadcast_to(valid, (SLOTS, SLOTS)).astype(jnp.bfloat16)
    before = jnp.dot(
        (lane < row).astype(jnp.float32).astype(jnp.bfloat16), wide, preferred_element_type=jnp.float32
    )
    order = jnp.where(valid > 0, before, -1.0).astype(jnp.int32)
    gather = (order == lane).astype(jnp.float32).astype(jnp.bfloat16)
    count = jnp.sum(valid).astype(jnp.int32)
    for h in range(RATIO):
        query_scr[h] = lax.dot_general(
            gather,
            queries[:, h].reshape(SLOTS, HD).astype(jnp.bfloat16),
            (((0,), (0,)), ((), ())),
            preferred_element_type=jnp.float32,
        ).astype(jnp.bfloat16)
    mixed_scr[...] = jnp.zeros_like(mixed_scr)
    stat_scr[...] = jnp.zeros_like(stat_scr)

    @pl.loop(0, (count + span - 1) // span)
    def _(index):
        start = pl.multiple_of(index * span, span)
        query = query_scr[:, pl.ds(start, span), :].reshape(block, HD)
        peak = jnp.full((block, HD), -jnp.inf, jnp.float32)
        for n, piece in enumerate(pieces):
            scores = lax.dot_general(
                query, piece[0], (((1,), (1,)), ((), ())), preferred_element_type=jnp.float32
            )
            score_ref[n] = scores
            peak = jnp.maximum(peak, jnp.maximum(scores[:, :HD], scores[:, HD:]))
        peak = jnp.max(peak, axis=1, keepdims=True)
        total = jnp.zeros((block, HD), jnp.float32)
        mixed = jnp.zeros((block, HD), jnp.float32)
        for n, piece in enumerate(pieces):
            weights = jnp.exp2((score_ref[n] - peak) * (SCALE * LOG2E))
            total = total + (weights[:, :HD] + weights[:, HD:])
            mixed = mixed + jnp.dot(
                weights.astype(jnp.bfloat16), piece[1], preferred_element_type=jnp.float32
            )
        total = jnp.sum(total, axis=1, keepdims=True)
        mixed_scr[:, pl.ds(start, span), :] = (mixed / total).astype(jnp.bfloat16).reshape(RATIO, span, HD)
        lse = peak * SCALE + jnp.log(total)
        stat_scr[pl.ds(start, span), :] = split_stat(lse.reshape(RATIO, span, 1), span).astype(jnp.bfloat16)

    idle = 1.0 - valid
    mean = sum(piece[1].astype(jnp.float32).reshape(PIECE // 8, 8, HD).sum(axis=0) for piece in pieces)
    mean = jnp.sum(mean, axis=0, keepdims=True) / tokens
    heads = []
    for h in range(RATIO):
        spread_out = jnp.dot(gather, mixed_scr[h], preferred_element_type=jnp.float32) + idle * mean
        heads.append(spread_out.reshape(32, 8, HD))
    for h in range(0, RATIO, 2):
        out_ref[:, h * 8 : h * 8 + 16] = jnp.concatenate(heads[h : h + 2], axis=1).astype(jnp.bfloat16)
    even = split_stat(jnp.full((RATIO, SLOTS, 1), math.log(tokens), jnp.float32), SLOTS)
    stat = jnp.dot(gather, stat_scr[...], preferred_element_type=jnp.float32) + idle * even
    stat = stat.reshape(32, 8, HD)
    out_ref[:, 64:] = jnp.concatenate([stat, jnp.zeros_like(stat)], axis=1).astype(jnp.bfloat16)


def split_stat(lse, span):
    high = lse.astype(jnp.bfloat16).astype(jnp.float32)
    rest = lse - high
    middle = rest.astype(jnp.bfloat16).astype(jnp.float32)
    low = rest - middle
    lane = lax.broadcasted_iota(jnp.int32, (span, HD), 1)
    stat = jnp.zeros((span, HD), jnp.float32)
    for h in range(RATIO):
        for n, part in enumerate((high, middle, low)):
            stat = jnp.where(lane == n * 8 + h, part[h], stat)
    return stat


def select_kernel(got_ref, back_ref, send_ref):
    tags = [got_ref[y, 64:].astype(jnp.float32)[8:, :1].astype(jnp.int32) for y in range(KVH)]
    lane = lax.broadcasted_iota(jnp.int32, (1, ROWS), 1)
    lane_key = ((lane >> 1) & 3) * 512 + ((lane >> 3) & 7) * 64 + (lane >> 6) * 2 + (lane & 1)
    tag = jnp.concatenate([tags[y] for y in range(KVH) for _ in range(RATIO)], axis=0)
    row_key = (lax.broadcasted_iota(jnp.int32, (256, 1), 0) >> 3) * 64 + tag
    select = (row_key == lane_key).astype(jnp.float32).astype(jnp.bfloat16)
    far = jnp.dot(select, back_ref[:, :64].reshape(ROWS, HD), preferred_element_type=jnp.float32)
    send_ref[:, :64] = far.astype(jnp.bfloat16).reshape(KVH, 64, HD)
    stats = back_ref[:, 64:].astype(jnp.float32)[:, :8].reshape(SLOTS, HD).astype(jnp.bfloat16)
    lane = lax.broadcasted_iota(jnp.int32, (1, SLOTS), 1)
    lane_key = ((lane >> 1) & 3) * 64 + (lane >> 3) * 2 + (lane & 1)
    row_key = (lax.broadcasted_iota(jnp.int32, (32, 1), 0) >> 3) * 64 + jnp.concatenate(tags, axis=0)
    select = (row_key == lane_key).astype(jnp.float32).astype(jnp.bfloat16)
    stat = jnp.dot(select, stats, preferred_element_type=jnp.float32).reshape(KVH, 8, HD)
    send_ref[:, 64:] = jnp.concatenate([stat, jnp.zeros_like(stat)], axis=1).astype(jnp.bfloat16)


def merge_kernel(back_ref, near_ref, near_lse_ref, out_ref):
    lane = lax.broadcasted_iota(jnp.int32, (HELD, HD), 1)
    for y in range(KVH):
        far = back_ref[y, :64].astype(jnp.float32)
        stat = jnp.where(lane < 24, back_ref[y, 64:].astype(jnp.float32)[:8], 0.0)
        for h in range(RATIO):
            head = y * RATIO + h
            far_lse = jnp.sum(jnp.where((lane & 7) == h, stat, 0.0), axis=1, keepdims=True)
            near_lse = near_lse_ref[head]
            top = jnp.maximum(far_lse, near_lse)
            far_scale = jnp.exp(far_lse - top)
            near_scale = jnp.exp(near_lse - top)
            merged = far[h * 8 : (h + 1) * 8] * far_scale + near_ref[head] * near_scale
            out_ref[:, head * HD : (head + 1) * HD] = (merged / (far_scale + near_scale)).astype(
                jnp.bfloat16
            )


VMEM = pl.BlockSpec(memory_space=pltpu.VMEM)
SMEM = pl.BlockSpec(memory_space=pltpu.SMEM)


def params(mib):
    return pltpu.CompilerParams(vmem_limit_bytes=mib << 20)


def shards(
    prompt_of,
    suffix_len,
    query,
    new_key,
    new_value,
    suffix_key,
    suffix_value,
    prefix_key,
    prefix_value,
):
    place = lax.axis_index(NEAR).astype(jnp.int32).reshape(1)
    sent, *cuts = pl.pallas_call(
        prep_kernel,
        out_shape=[jax.ShapeDtypeStruct((KVH, 80, HD), jnp.bfloat16)]
        + [jax.ShapeDtypeStruct((2, PIECE, HD), jnp.bfloat16)] * 8,
        in_specs=[SMEM, SMEM, VMEM, VMEM, VMEM],
        out_specs=[VMEM] * 9,
        compiler_params=params(16),
        name="prep",
    )(place, prompt_of, query, prefix_key, prefix_value)
    held = [cuts[0]]
    for step in range(1, 8):
        held.append(lax.ppermute(cuts[step], NEAR, [(i, i ^ step) for i in range(8)]))
    swapped = [lax.ppermute(piece, "c", [(0, 1), (1, 0)]) for piece in held]
    got = lax.all_to_all(sent, "y", 0, 0, tiled=True)
    outgoing = pl.pallas_call(
        pack_kernel,
        out_shape=jax.ShapeDtypeStruct((ROWS, HD), jnp.bfloat16),
        in_specs=[VMEM],
        out_specs=VMEM,
        compiler_params=params(16),
        name="pack",
    )(got)
    arrived = lax.all_to_all(outgoing.reshape(PROMPTS, 64, HD), FAR, 0, 0, tiled=True)

    near_out, near_lse = pl.pallas_call(
        near_kernel,
        grid=(HELD,),
        out_shape=[jax.ShapeDtypeStruct((HEADS, HELD, HD), jnp.float32)] * 2,
        in_specs=[
            SMEM,
            pl.BlockSpec((1, HEADS, HD), lambda i: (i, 0, 0)),
            pl.BlockSpec((HELD, KVH * HD), lambda i: (0, 0)),
            pl.BlockSpec((HELD, KVH * HD), lambda i: (0, 0)),
            pl.BlockSpec((1, SUF, KVH * HD), lambda i: (i, 0, 0)),
            pl.BlockSpec((1, SUF, KVH * HD), lambda i: (i, 0, 0)),
        ],
        out_specs=[pl.BlockSpec((HEADS, HELD, HD), lambda i: (0, 0, 0))] * 2,
        compiler_params=params(16),
        cost_estimate=pl.CostEstimate(flops=300_000_000, bytes_accessed=4_500_000, transcendentals=65536),
        name="near",
    )(
        suffix_len,
        query.reshape(HELD, HEADS, HD),
        new_key.astype(jnp.float32),
        new_value.astype(jnp.float32),
        suffix_key,
        suffix_value,
    )

    parcel = pl.pallas_call(
        far_kernel,
        out_shape=jax.ShapeDtypeStruct((PROMPTS, 80, HD), jnp.bfloat16),
        in_specs=[VMEM] * 17,
        out_specs=VMEM,
        scratch_shapes=[
            pltpu.VMEM((16, 256, PIECE), jnp.float32),
            pltpu.VMEM((RATIO, SLOTS, HD), jnp.bfloat16),
            pltpu.VMEM((RATIO, SLOTS, HD), jnp.bfloat16),
            pltpu.VMEM((SLOTS, HD), jnp.bfloat16),
        ],
        compiler_params=params(32),
        name="far",
    )(arrived.reshape(ROWS, HD), *held, *swapped)
    back = lax.all_to_all(parcel, FAR, 0, 0, tiled=True)
    chosen = pl.pallas_call(
        select_kernel,
        out_shape=jax.ShapeDtypeStruct((KVH, 80, HD), jnp.bfloat16),
        in_specs=[VMEM] * 2,
        out_specs=VMEM,
        compiler_params=params(16),
        name="select",
    )(got, back)
    final = lax.all_to_all(chosen, "y", 0, 0, tiled=True)
    return pl.pallas_call(
        merge_kernel,
        out_shape=jax.ShapeDtypeStruct((HELD, HEADS * HD), jnp.bfloat16),
        in_specs=[VMEM] * 3,
        out_specs=VMEM,
        compiler_params=params(16),
        name="merge",
    )(final, near_out, near_lse)


def solution(mesh):
    fine = Mesh(mesh.devices.reshape(2, 8, 2, 4, 2), ALL)
    grp = ("xh", "z")
    blk = ("xl", "y", "c")
    in_specs = (
        P(ALL),
        P(ALL),
        P(ALL, None),
        P(ALL, None),
        P(ALL, None),
        P(ALL, None, None),
        P(ALL, None, None),
        P(grp, blk, None),
        P(grp, blk, None),
    )
    return jax.shard_map(
        shards, mesh=fine, in_specs=in_specs, out_specs=P(ALL, None), check_vma=False
    )
```

```python
import math

import jax
import jax.numpy as jnp
from jax import lax
from jax.experimental import pallas as pl
from jax.experimental.pallas import tpu as pltpu
from jax.sharding import Mesh, PartitionSpec as P

HD = 128
CAP = 2
HELD = 8
HEADS = 32
KVH = 4
RATIO = 8
PROMPTS = 32
SUF = 256
PIECE = 256
SLOTS = 256
ROWS = SLOTS * RATIO
NEG = -1e30
SCALE = HD ** (-0.5)
LOG2E = 1.4426950408889634
ALL = ("xh", "z", "xl", "y", "c")
NEAR = ("xl", "y")
FAR = ("xh", "z", "xl")


def slots_of(prompt_ref):
    prompts = [prompt_ref[i] for i in range(HELD)]
    slots = []
    for i in range(HELD):
        rank = jnp.int32(0)
        for j in range(i):
            rank = rank + jnp.where(prompts[j] == prompts[i], 1, 0)
        slots.append(prompts[i] * CAP + rank)
    return slots


def spread(values, index):
    picked = jnp.zeros(index.shape, jnp.int32)
    for i, value in enumerate(values):
        picked = jnp.where(index == i, value, picked)
    return picked


def prep_kernel(place_ref, prompt_hbm, query_hbm, key_ref, value_ref, send_ref, *refs):
    cut_refs = refs[:8]
    prompt_ref, query_ref, small_sem, cut_sem = refs[8:]
    small = [
        pltpu.make_async_copy(prompt_hbm, prompt_ref, small_sem.at[0]),
        pltpu.make_async_copy(query_hbm, query_ref, small_sem.at[1]),
    ]
    for copy in small:
        copy.start()
    place = place_ref[0]
    copies = []
    for step, cut_ref in enumerate(cut_refs):
        target = place ^ step
        prompt = target >> 2
        column = pl.multiple_of((target & 3) * HD, HD)
        for n, cache in enumerate((key_ref, value_ref)):
            copies.append(
                pltpu.make_async_copy(
                    cache.at[prompt, :, pl.ds(column, HD)], cut_ref.at[n], cut_sem.at[step, n]
                )
            )
            copies[-1].start()
    for copy in small:
        copy.wait()
    slots = slots_of(prompt_ref)
    lane = lax.broadcasted_iota(jnp.int32, (HELD, HD), 1)
    row = lax.broadcasted_iota(jnp.int32, (HELD, HD), 0)
    tags = jnp.concatenate(
        [spread(slots, lane & 7).astype(jnp.float32), spread(slots, row).astype(jnp.float32)], axis=0
    ).astype(jnp.bfloat16)
    for y in range(KVH):
        send_ref[y, :64] = jnp.concatenate(
            [
                query_ref[:, h * HD : (h + 1) * HD].astype(jnp.float32)
                for h in range(y * RATIO, (y + 1) * RATIO)
            ],
            axis=0,
        ).astype(jnp.bfloat16)
        send_ref[y, 64:] = tags
    for copy in copies:
        copy.wait()


def pack_kernel(got_ref, *refs):
    out_ref = refs[-1]
    held = got_ref[:, :64].reshape(256, HD)
    tags = [got_ref[y, 64:].astype(jnp.float32)[:1].astype(jnp.int32) for y in range(KVH)]
    half = lax.broadcasted_iota(jnp.int32, (1, HD), 1) < 64
    tag = jnp.concatenate([jnp.where(half, tags[0], tags[1]), jnp.where(half, tags[2], tags[3])], axis=1)
    lane_key = (lax.broadcasted_iota(jnp.int32, (1, 256), 1) >> 3) * 64 + tag
    chunk = 512
    for start in range(0, ROWS, chunk):
        row = lax.broadcasted_iota(jnp.int32, (chunk, 1), 0) + start
        row_key = ((row >> 1) & 3) * 512 + ((row >> 3) & 7) * 64 + (row >> 6) * 2 + (row & 1)
        select = (row_key == lane_key).astype(jnp.float32).astype(jnp.bfloat16)
        out_ref[start : start + chunk, :] = jnp.dot(
            select, held, preferred_element_type=jnp.float32
        ).astype(jnp.bfloat16)


def near_kernel(len_ref, query_ref, new_key_ref, new_value_ref, key_ref, value_ref, out_ref, lse_ref):
    step = pl.program_id(0)
    length = len_ref[step]
    query = query_ref[0]
    keys = key_ref[0]
    values = value_ref[0]
    new_key = new_key_ref[pl.ds(step, 1), :]
    new_value = new_value_ref[pl.ds(step, 1), :]

    def spread_heads(row):
        return jnp.concatenate(
            [jnp.broadcast_to(row[:, k * HD : (k + 1) * HD], (RATIO, HD)) for k in range(KVH)], axis=0
        )

    scores = jnp.concatenate(
        [
            lax.dot_general(
                query,
                keys[:, k * HD : (k + 1) * HD],
                (((1,), (1,)), ((), ())),
                preferred_element_type=jnp.float32,
            )[k * RATIO : (k + 1) * RATIO]
            for k in range(KVH)
        ],
        axis=0,
    ) * SCALE
    own = jnp.sum(query.astype(jnp.float32) * spread_heads(new_key), axis=1, keepdims=True) * SCALE
    live = lax.broadcasted_iota(jnp.int32, (1, SUF), 1) < length
    scores = jnp.where(live, scores, NEG)
    top = jnp.maximum(jnp.max(scores, axis=1, keepdims=True), own)
    weights = jnp.where(live, jnp.exp(scores - top), 0.0)
    own_weight = jnp.exp(own - top)
    total = jnp.sum(weights, axis=1, keepdims=True) + own_weight
    rounded = weights.astype(jnp.bfloat16)
    mixed = jnp.concatenate(
        [
            jnp.dot(rounded, values[:, k * HD : (k + 1) * HD], preferred_element_type=jnp.float32)[
                k * RATIO : (k + 1) * RATIO
            ]
            for k in range(KVH)
        ],
        axis=0,
    )
    mixed = mixed + own_weight.astype(jnp.bfloat16).astype(jnp.float32) * spread_heads(new_value)
    out_ref[:, pl.ds(step, 1), :] = (mixed / total).reshape(HEADS, 1, HD)
    lse_ref[:, pl.ds(step, 1), :] = jnp.broadcast_to(top + jnp.log(total), (HEADS, HD)).reshape(
        HEADS, 1, HD
    )


def far_kernel(query_ref, *refs):
    sources = refs[:16]
    out_ref, score_ref, query_scr, mixed_scr, stat_scr, cache_ref, sems = refs[16:]
    copies = [
        pltpu.make_async_copy(source, cache_ref.at[n], sems.at[n]) for n, source in enumerate(sources)
    ]
    for copy in copies:
        copy.start()
    pieces = [cache_ref.at[n] for n in range(16)]
    span = 32
    block = span * RATIO
    tokens = 16 * PIECE
    queries = query_ref[...].astype(jnp.float32).reshape(32, RATIO, 8, HD)
    biggest = jnp.max(jnp.max(jnp.abs(queries), axis=1).reshape(SLOTS, HD), axis=1, keepdims=True)
    valid = (biggest > 0).astype(jnp.float32)
    row = lax.broadcasted_iota(jnp.int32, (SLOTS, SLOTS), 0)
    lane = lax.broadcasted_iota(jnp.int32, (SLOTS, SLOTS), 1)
    wide = jnp.broadcast_to(valid, (SLOTS, SLOTS)).astype(jnp.bfloat16)
    before = jnp.dot(
        (lane < row).astype(jnp.float32).astype(jnp.bfloat16), wide, preferred_element_type=jnp.float32
    )
    order = jnp.where(valid > 0, before, -1.0).astype(jnp.int32)
    gather = (order == lane).astype(jnp.float32).astype(jnp.bfloat16)
    count = jnp.sum(valid).astype(jnp.int32)
    for h in range(RATIO):
        query_scr[h] = lax.dot_general(
            gather,
            queries[:, h].reshape(SLOTS, HD).astype(jnp.bfloat16),
            (((0,), (0,)), ((), ())),
            preferred_element_type=jnp.float32,
        ).astype(jnp.bfloat16)
    mixed_scr[...] = jnp.zeros_like(mixed_scr)
    stat_scr[...] = jnp.zeros_like(stat_scr)
    for copy in copies:
        copy.wait()

    @pl.loop(0, (count + span - 1) // span)
    def _(index):
        start = pl.multiple_of(index * span, span)
        query = query_scr[:, pl.ds(start, span), :].reshape(block, HD)
        peak = jnp.full((block, HD), -jnp.inf, jnp.float32)
        for n, piece in enumerate(pieces):
            scores = lax.dot_general(
                query, piece[0], (((1,), (1,)), ((), ())), preferred_element_type=jnp.float32
            )
            score_ref[n] = scores
            peak = jnp.maximum(peak, jnp.maximum(scores[:, :HD], scores[:, HD:]))
        peak = jnp.max(peak, axis=1, keepdims=True)
        total = jnp.zeros((block, HD), jnp.float32)
        mixed = jnp.zeros((block, HD), jnp.float32)
        for n, piece in enumerate(pieces):
            weights = jnp.exp2((score_ref[n] - peak) * (SCALE * LOG2E))
            total = total + (weights[:, :HD] + weights[:, HD:])
            mixed = mixed + jnp.dot(
                weights.astype(jnp.bfloat16), piece[1], preferred_element_type=jnp.float32
            )
        total = jnp.sum(total, axis=1, keepdims=True)
        mixed_scr[:, pl.ds(start, span), :] = (mixed / total).astype(jnp.bfloat16).reshape(RATIO, span, HD)
        lse = peak * SCALE + jnp.log(total)
        stat_scr[pl.ds(start, span), :] = split_stat(lse.reshape(RATIO, span, 1), span).astype(jnp.bfloat16)

    idle = 1.0 - valid
    mean = sum(piece[1].astype(jnp.float32).reshape(PIECE // 8, 8, HD).sum(axis=0) for piece in pieces)
    mean = jnp.sum(mean, axis=0, keepdims=True) / tokens
    heads = []
    for h in range(RATIO):
        spread_out = jnp.dot(gather, mixed_scr[h], preferred_element_type=jnp.float32) + idle * mean
        heads.append(spread_out.reshape(32, 8, HD))
    for h in range(0, RATIO, 2):
        out_ref[:, h * 8 : h * 8 + 16] = jnp.concatenate(heads[h : h + 2], axis=1).astype(jnp.bfloat16)
    even = split_stat(jnp.full((RATIO, SLOTS, 1), math.log(tokens), jnp.float32), SLOTS)
    stat = jnp.dot(gather, stat_scr[...], preferred_element_type=jnp.float32) + idle * even
    stat = stat.reshape(32, 8, HD)
    out_ref[:, 64:] = jnp.concatenate([stat, jnp.zeros_like(stat)], axis=1).astype(jnp.bfloat16)


def split_stat(lse, span):
    high = lse.astype(jnp.bfloat16).astype(jnp.float32)
    rest = lse - high
    middle = rest.astype(jnp.bfloat16).astype(jnp.float32)
    low = rest - middle
    lane = lax.broadcasted_iota(jnp.int32, (span, HD), 1)
    stat = jnp.zeros((span, HD), jnp.float32)
    for h in range(RATIO):
        for n, part in enumerate((high, middle, low)):
            stat = jnp.where(lane == n * 8 + h, part[h], stat)
    return stat


def select_kernel(got_ref, back_ref, *refs):
    send_ref = refs[-1]
    tags = [got_ref[y, 64:].astype(jnp.float32)[8:, :1].astype(jnp.int32) for y in range(KVH)]
    lane = lax.broadcasted_iota(jnp.int32, (1, ROWS), 1)
    lane_key = ((lane >> 1) & 3) * 512 + ((lane >> 3) & 7) * 64 + (lane >> 6) * 2 + (lane & 1)
    tag = jnp.concatenate([tags[y] for y in range(KVH) for _ in range(RATIO)], axis=0)
    row_key = (lax.broadcasted_iota(jnp.int32, (256, 1), 0) >> 3) * 64 + tag
    select = (row_key == lane_key).astype(jnp.float32).astype(jnp.bfloat16)
    far = jnp.dot(select, back_ref[:, :64].reshape(ROWS, HD), preferred_element_type=jnp.float32)
    send_ref[:, :64] = far.astype(jnp.bfloat16).reshape(KVH, 64, HD)
    stats = back_ref[:, 64:].astype(jnp.float32)[:, :8].reshape(SLOTS, HD).astype(jnp.bfloat16)
    lane = lax.broadcasted_iota(jnp.int32, (1, SLOTS), 1)
    lane_key = ((lane >> 1) & 3) * 64 + (lane >> 3) * 2 + (lane & 1)
    row_key = (lax.broadcasted_iota(jnp.int32, (32, 1), 0) >> 3) * 64 + jnp.concatenate(tags, axis=0)
    select = (row_key == lane_key).astype(jnp.float32).astype(jnp.bfloat16)
    stat = jnp.dot(select, stats, preferred_element_type=jnp.float32).reshape(KVH, 8, HD)
    send_ref[:, 64:] = jnp.concatenate([stat, jnp.zeros_like(stat)], axis=1).astype(jnp.bfloat16)


def merge_kernel(back_ref, near_ref, near_lse_ref, out_ref):
    lane = lax.broadcasted_iota(jnp.int32, (HELD, HD), 1)
    for y in range(KVH):
        far = back_ref[y, :64].astype(jnp.float32)
        stat = jnp.where(lane < 24, back_ref[y, 64:].astype(jnp.float32)[:8], 0.0)
        for h in range(RATIO):
            head = y * RATIO + h
            far_lse = jnp.sum(jnp.where((lane & 7) == h, stat, 0.0), axis=1, keepdims=True)
            near_lse = near_lse_ref[head]
            top = jnp.maximum(far_lse, near_lse)
            far_scale = jnp.exp(far_lse - top)
            near_scale = jnp.exp(near_lse - top)
            merged = far[h * 8 : (h + 1) * 8] * far_scale + near_ref[head] * near_scale
            out_ref[:, head * HD : (head + 1) * HD] = (merged / (far_scale + near_scale)).astype(
                jnp.bfloat16
            )


VMEM = pl.BlockSpec(memory_space=pltpu.VMEM)
SMEM = pl.BlockSpec(memory_space=pltpu.SMEM)
ANY = pl.BlockSpec(memory_space=pl.ANY)
HBM = pl.BlockSpec(memory_space=pltpu.HBM)


def params(mib):
    return pltpu.CompilerParams(vmem_limit_bytes=mib << 20)


def shards(
    prompt_of,
    suffix_len,
    query,
    new_key,
    new_value,
    suffix_key,
    suffix_value,
    prefix_key,
    prefix_value,
):
    place = lax.axis_index(NEAR).astype(jnp.int32).reshape(1)
    sent, *cuts = pl.pallas_call(
        prep_kernel,
        out_shape=[jax.ShapeDtypeStruct((KVH, 80, HD), jnp.bfloat16)]
        + [jax.ShapeDtypeStruct((2, PIECE, HD), jnp.bfloat16)] * 8,
        in_specs=[SMEM, HBM, HBM, HBM, HBM],
        out_specs=[VMEM] * 9,
        scratch_shapes=[
            pltpu.SMEM((HELD,), jnp.int32),
            pltpu.VMEM((HELD, HEADS * HD), jnp.bfloat16),
            pltpu.SemaphoreType.DMA((2,)),
            pltpu.SemaphoreType.DMA((8, 2)),
        ],
        compiler_params=params(12),
        name="prep",
    )(place, prompt_of, query, prefix_key, prefix_value)
    held = [cuts[0]]
    for step in range(1, 8):
        held.append(lax.ppermute(cuts[step], NEAR, [(i, i ^ step) for i in range(8)]))
    swapped = [lax.ppermute(piece, "c", [(0, 1), (1, 0)]) for piece in held]
    got = lax.all_to_all(sent, "y", 0, 0, tiled=True)
    outgoing = pl.pallas_call(
        pack_kernel,
        out_shape=jax.ShapeDtypeStruct((ROWS, HD), jnp.bfloat16),
        in_specs=[VMEM] + [ANY] * 4,
        out_specs=VMEM,
        compiler_params=params(8),
        name="pack",
    )(got, *held[4:])
    arrived = lax.all_to_all(outgoing.reshape(PROMPTS, 64, HD), FAR, 0, 0, tiled=True)

    near_out, near_lse = pl.pallas_call(
        near_kernel,
        grid=(HELD,),
        out_shape=[jax.ShapeDtypeStruct((HEADS, HELD, HD), jnp.float32)] * 2,
        in_specs=[
            SMEM,
            pl.BlockSpec((1, HEADS, HD), lambda i: (i, 0, 0)),
            pl.BlockSpec((HELD, KVH * HD), lambda i: (0, 0)),
            pl.BlockSpec((HELD, KVH * HD), lambda i: (0, 0)),
            pl.BlockSpec((1, SUF, KVH * HD), lambda i: (i, 0, 0)),
            pl.BlockSpec((1, SUF, KVH * HD), lambda i: (i, 0, 0)),
        ],
        out_specs=[pl.BlockSpec((HEADS, HELD, HD), lambda i: (0, 0, 0))] * 2,
        compiler_params=params(12),
        cost_estimate=pl.CostEstimate(flops=300_000_000, bytes_accessed=4_500_000, transcendentals=65536),
        name="near",
    )(
        suffix_len,
        query.reshape(HELD, HEADS, HD),
        new_key.astype(jnp.float32),
        new_value.astype(jnp.float32),
        suffix_key,
        suffix_value,
    )

    parcel = pl.pallas_call(
        far_kernel,
        out_shape=jax.ShapeDtypeStruct((PROMPTS, 80, HD), jnp.bfloat16),
        in_specs=[VMEM] + [ANY] * 16,
        out_specs=VMEM,
        scratch_shapes=[
            pltpu.VMEM((16, 256, PIECE), jnp.float32),
            pltpu.VMEM((RATIO, SLOTS, HD), jnp.bfloat16),
            pltpu.VMEM((RATIO, SLOTS, HD), jnp.bfloat16),
            pltpu.VMEM((SLOTS, HD), jnp.bfloat16),
            pltpu.VMEM((16, 2, PIECE, HD), jnp.bfloat16),
            pltpu.SemaphoreType.DMA((16,)),
        ],
        compiler_params=params(16),
        name="far",
    )(arrived.reshape(ROWS, HD), *held, *swapped)
    back = lax.all_to_all(parcel, FAR, 0, 0, tiled=True)
    chosen = pl.pallas_call(
        select_kernel,
        out_shape=jax.ShapeDtypeStruct((KVH, 80, HD), jnp.bfloat16),
        in_specs=[VMEM] * 2 + [ANY] * 2,
        out_specs=VMEM,
        compiler_params=params(8),
        name="select",
    )(got, back, near_out, near_lse)
    final = lax.all_to_all(chosen, "y", 0, 0, tiled=True)
    return pl.pallas_call(
        merge_kernel,
        out_shape=jax.ShapeDtypeStruct((HELD, HEADS * HD), jnp.bfloat16),
        in_specs=[VMEM] * 3,
        out_specs=VMEM,
        compiler_params=params(12),
        name="merge",
    )(final, near_out, near_lse)


def solution(mesh):
    fine = Mesh(mesh.devices.reshape(2, 8, 2, 4, 2), ALL)
    grp = ("xh", "z")
    blk = ("xl", "y", "c")
    in_specs = (
        P(ALL),
        P(ALL),
        P(ALL, None),
        P(ALL, None),
        P(ALL, None),
        P(ALL, None, None),
        P(ALL, None, None),
        P(grp, blk, None),
        P(grp, blk, None),
    )
    return jax.shard_map(
        shards, mesh=fine, in_specs=in_specs, out_specs=P(ALL, None), check_vma=False
    )
```

```python
import math

import jax
import jax.numpy as jnp
from jax import lax
from jax.experimental import pallas as pl
from jax.experimental.pallas import tpu as pltpu
from jax.sharding import Mesh, PartitionSpec as P

HD = 128
CAP = 2
HELD = 8
HEADS = 32
KVH = 4
RATIO = 8
PROMPTS = 32
SUF = 256
PIECE = 256
SLOTS = 256
ROWS = SLOTS * RATIO
NEG = -1e30
SCALE = HD ** (-0.5)
LOG2E = 1.4426950408889634
ALL = ("xh", "z", "xl", "y", "c")
NEAR = ("xl", "y")
FAR = ("xh", "z", "xl")


def slots_of(prompt_ref):
    prompts = [prompt_ref[i] for i in range(HELD)]
    slots = []
    for i in range(HELD):
        rank = jnp.int32(0)
        for j in range(i):
            rank = rank + jnp.where(prompts[j] == prompts[i], 1, 0)
        slots.append(prompts[i] * CAP + rank)
    return slots


def spread(values, index):
    picked = jnp.zeros(index.shape, jnp.int32)
    for i, value in enumerate(values):
        picked = jnp.where(index == i, value, picked)
    return picked


def prep_kernel(place_ref, prompt_hbm, query_hbm, key_ref, value_ref, send_ref, *refs):
    cut_refs = refs[:8]
    prompt_ref, query_ref, small_sem, cut_sem = refs[8:]
    small = [
        pltpu.make_async_copy(prompt_hbm, prompt_ref, small_sem.at[0]),
        pltpu.make_async_copy(query_hbm, query_ref, small_sem.at[1]),
    ]
    for copy in small:
        copy.start()
    place = place_ref[0]
    copies = []
    for step, cut_ref in enumerate(cut_refs):
        target = place ^ step
        prompt = target >> 2
        column = pl.multiple_of((target & 3) * HD, HD)
        for n, cache in enumerate((key_ref, value_ref)):
            copies.append(
                pltpu.make_async_copy(
                    cache.at[prompt, :, pl.ds(column, HD)], cut_ref.at[n], cut_sem.at[step, n]
                )
            )
            copies[-1].start()
    for copy in small:
        copy.wait()
    slots = slots_of(prompt_ref)
    lane = lax.broadcasted_iota(jnp.int32, (HELD, HD), 1)
    row = lax.broadcasted_iota(jnp.int32, (HELD, HD), 0)
    tags = jnp.concatenate(
        [spread(slots, lane & 7).astype(jnp.float32), spread(slots, row).astype(jnp.float32)], axis=0
    ).astype(jnp.bfloat16)
    for y in range(KVH):
        send_ref[y, :64] = jnp.concatenate(
            [
                query_ref[:, h * HD : (h + 1) * HD].astype(jnp.float32)
                for h in range(y * RATIO, (y + 1) * RATIO)
            ],
            axis=0,
        ).astype(jnp.bfloat16)
        send_ref[y, 64:] = tags
    for copy in copies:
        copy.wait()


def pack_kernel(got_ref, *refs):
    out_ref = refs[-1]
    held = got_ref[:, :64].reshape(256, HD)
    tags = [got_ref[y, 64:].astype(jnp.float32)[:1].astype(jnp.int32) for y in range(KVH)]
    half = lax.broadcasted_iota(jnp.int32, (1, HD), 1) < 64
    tag = jnp.concatenate([jnp.where(half, tags[0], tags[1]), jnp.where(half, tags[2], tags[3])], axis=1)
    lane_key = (lax.broadcasted_iota(jnp.int32, (1, 256), 1) >> 3) * 64 + tag
    chunk = 512
    for start in range(0, ROWS, chunk):
        row = lax.broadcasted_iota(jnp.int32, (chunk, 1), 0) + start
        row_key = ((row >> 1) & 3) * 512 + ((row >> 3) & 7) * 64 + (row >> 6) * 2 + (row & 1)
        select = (row_key == lane_key).astype(jnp.float32).astype(jnp.bfloat16)
        out_ref[start : start + chunk, :] = jnp.dot(
            select, held, preferred_element_type=jnp.float32
        ).astype(jnp.bfloat16)


def near_kernel(
    len_ref, query_ref, new_key_ref, new_value_ref, key_ref, value_ref, out_ref, lse_ref, heads_ref
):
    step = pl.program_id(0)

    @pl.when(step == 0)
    def _():
        for h in range(HEADS):
            heads_ref[h] = query_ref[:, h * HD : (h + 1) * HD].astype(jnp.float32)

    length = len_ref[step]
    query = heads_ref[:, pl.ds(step, 1), :].reshape(HEADS, HD)
    keys = key_ref[0]
    values = value_ref[0]
    held_row = lax.broadcasted_iota(jnp.int32, (HELD, 1), 0)

    def row_of(ref):
        rows = jnp.where(held_row == step, ref[...].astype(jnp.float32), 0.0)
        return jnp.sum(rows, axis=0, keepdims=True)

    new_key = row_of(new_key_ref)
    new_value = row_of(new_value_ref)

    def spread_heads(row):
        return jnp.concatenate(
            [jnp.broadcast_to(row[:, k * HD : (k + 1) * HD], (RATIO, HD)) for k in range(KVH)], axis=0
        )

    scores = jnp.concatenate(
        [
            lax.dot_general(
                query.astype(jnp.bfloat16),
                keys[:, k * HD : (k + 1) * HD],
                (((1,), (1,)), ((), ())),
                preferred_element_type=jnp.float32,
            )[k * RATIO : (k + 1) * RATIO]
            for k in range(KVH)
        ],
        axis=0,
    ) * SCALE
    own = jnp.sum(query * spread_heads(new_key), axis=1, keepdims=True) * SCALE
    live = lax.broadcasted_iota(jnp.int32, (1, SUF), 1) < length
    scores = jnp.where(live, scores, NEG)
    top = jnp.maximum(jnp.max(scores, axis=1, keepdims=True), own)
    weights = jnp.where(live, jnp.exp(scores - top), 0.0)
    own_weight = jnp.exp(own - top)
    total = jnp.sum(weights, axis=1, keepdims=True) + own_weight
    rounded = weights.astype(jnp.bfloat16)
    mixed = jnp.concatenate(
        [
            jnp.dot(rounded, values[:, k * HD : (k + 1) * HD], preferred_element_type=jnp.float32)[
                k * RATIO : (k + 1) * RATIO
            ]
            for k in range(KVH)
        ],
        axis=0,
    )
    mixed = mixed + own_weight.astype(jnp.bfloat16).astype(jnp.float32) * spread_heads(new_value)
    out_ref[:, pl.ds(step, 1), :] = (mixed / total).reshape(HEADS, 1, HD)
    lse_ref[:, pl.ds(step, 1), :] = jnp.broadcast_to(top + jnp.log(total), (HEADS, HD)).reshape(
        HEADS, 1, HD
    )


def far_kernel(query_ref, *refs):
    pieces = refs[:16]
    out_ref, score_ref, query_scr, mixed_scr, stat_scr = refs[16:]
    span = 32
    block = span * RATIO
    tokens = 16 * PIECE
    queries = query_ref[...].astype(jnp.float32).reshape(32, RATIO, 8, HD)
    biggest = jnp.max(jnp.max(jnp.abs(queries), axis=1).reshape(SLOTS, HD), axis=1, keepdims=True)
    valid = (biggest > 0).astype(jnp.float32)
    row = lax.broadcasted_iota(jnp.int32, (SLOTS, SLOTS), 0)
    lane = lax.broadcasted_iota(jnp.int32, (SLOTS, SLOTS), 1)
    wide = jnp.broadcast_to(valid, (SLOTS, SLOTS)).astype(jnp.bfloat16)
    before = jnp.dot(
        (lane < row).astype(jnp.float32).astype(jnp.bfloat16), wide, preferred_element_type=jnp.float32
    )
    order = jnp.where(valid > 0, before, -1.0).astype(jnp.int32)
    gather = (order == lane).astype(jnp.float32).astype(jnp.bfloat16)
    count = jnp.sum(valid).astype(jnp.int32)
    for h in range(RATIO):
        query_scr[h] = lax.dot_general(
            gather,
            queries[:, h].reshape(SLOTS, HD).astype(jnp.bfloat16),
            (((0,), (0,)), ((), ())),
            preferred_element_type=jnp.float32,
        ).astype(jnp.bfloat16)
    mixed_scr[...] = jnp.zeros_like(mixed_scr)
    stat_scr[...] = jnp.zeros_like(stat_scr)

    @pl.loop(0, (count + span - 1) // span)
    def _(index):
        start = pl.multiple_of(index * span, span)
        query = query_scr[:, pl.ds(start, span), :].reshape(block, HD)
        peak = jnp.full((block, HD), -jnp.inf, jnp.float32)
        for n, piece in enumerate(pieces):
            scores = lax.dot_general(
                query, piece[0], (((1,), (1,)), ((), ())), preferred_element_type=jnp.float32
            )
            score_ref[n] = scores
            peak = jnp.maximum(peak, jnp.maximum(scores[:, :HD], scores[:, HD:]))
        peak = jnp.max(peak, axis=1, keepdims=True)
        total = jnp.zeros((block, HD), jnp.float32)
        mixed = jnp.zeros((block, HD), jnp.float32)
        for n, piece in enumerate(pieces):
            weights = jnp.exp2((score_ref[n] - peak) * (SCALE * LOG2E))
            total = total + (weights[:, :HD] + weights[:, HD:])
            mixed = mixed + jnp.dot(
                weights.astype(jnp.bfloat16), piece[1], preferred_element_type=jnp.float32
            )
        total = jnp.sum(total, axis=1, keepdims=True)
        mixed_scr[:, pl.ds(start, span), :] = (mixed / total).astype(jnp.bfloat16).reshape(RATIO, span, HD)
        lse = peak * SCALE + jnp.log(total)
        stat_scr[pl.ds(start, span), :] = split_stat(lse.reshape(RATIO, span, 1), span).astype(jnp.bfloat16)

    idle = 1.0 - valid
    mean = sum(piece[1].astype(jnp.float32).reshape(PIECE // 8, 8, HD).sum(axis=0) for piece in pieces)
    mean = jnp.sum(mean, axis=0, keepdims=True) / tokens
    heads = []
    for h in range(RATIO):
        spread_out = jnp.dot(gather, mixed_scr[h], preferred_element_type=jnp.float32) + idle * mean
        heads.append(spread_out.reshape(32, 8, HD))
    for h in range(0, RATIO, 2):
        out_ref[:, h * 8 : h * 8 + 16] = jnp.concatenate(heads[h : h + 2], axis=1).astype(jnp.bfloat16)
    even = split_stat(jnp.full((RATIO, SLOTS, 1), math.log(tokens), jnp.float32), SLOTS)
    stat = jnp.dot(gather, stat_scr[...], preferred_element_type=jnp.float32) + idle * even
    stat = stat.reshape(32, 8, HD)
    out_ref[:, 64:] = jnp.concatenate([stat, jnp.zeros_like(stat)], axis=1).astype(jnp.bfloat16)


def split_stat(lse, span):
    high = lse.astype(jnp.bfloat16).astype(jnp.float32)
    rest = lse - high
    middle = rest.astype(jnp.bfloat16).astype(jnp.float32)
    low = rest - middle
    lane = lax.broadcasted_iota(jnp.int32, (span, HD), 1)
    stat = jnp.zeros((span, HD), jnp.float32)
    for h in range(RATIO):
        for n, part in enumerate((high, middle, low)):
            stat = jnp.where(lane == n * 8 + h, part[h], stat)
    return stat


def select_kernel(got_ref, back_ref, *refs):
    send_ref = refs[-1]
    tags = [got_ref[y, 64:].astype(jnp.float32)[8:, :1].astype(jnp.int32) for y in range(KVH)]
    lane = lax.broadcasted_iota(jnp.int32, (1, ROWS), 1)
    lane_key = ((lane >> 1) & 3) * 512 + ((lane >> 3) & 7) * 64 + (lane >> 6) * 2 + (lane & 1)
    tag = jnp.concatenate([tags[y] for y in range(KVH) for _ in range(RATIO)], axis=0)
    row_key = (lax.broadcasted_iota(jnp.int32, (256, 1), 0) >> 3) * 64 + tag
    select = (row_key == lane_key).astype(jnp.float32).astype(jnp.bfloat16)
    far = jnp.dot(select, back_ref[:, :64].reshape(ROWS, HD), preferred_element_type=jnp.float32)
    send_ref[:, :64] = far.astype(jnp.bfloat16).reshape(KVH, 64, HD)
    stats = back_ref[:, 64:].astype(jnp.float32)[:, :8].reshape(SLOTS, HD).astype(jnp.bfloat16)
    lane = lax.broadcasted_iota(jnp.int32, (1, SLOTS), 1)
    lane_key = ((lane >> 1) & 3) * 64 + (lane >> 3) * 2 + (lane & 1)
    row_key = (lax.broadcasted_iota(jnp.int32, (32, 1), 0) >> 3) * 64 + jnp.concatenate(tags, axis=0)
    select = (row_key == lane_key).astype(jnp.float32).astype(jnp.bfloat16)
    stat = jnp.dot(select, stats, preferred_element_type=jnp.float32).reshape(KVH, 8, HD)
    send_ref[:, 64:] = jnp.concatenate([stat, jnp.zeros_like(stat)], axis=1).astype(jnp.bfloat16)


def merge_kernel(back_ref, near_ref, near_lse_ref, out_ref):
    lane = lax.broadcasted_iota(jnp.int32, (HELD, HD), 1)
    for y in range(KVH):
        far = back_ref[y, :64].astype(jnp.float32)
        stat = jnp.where(lane < 24, back_ref[y, 64:].astype(jnp.float32)[:8], 0.0)
        for h in range(RATIO):
            head = y * RATIO + h
            far_lse = jnp.sum(jnp.where((lane & 7) == h, stat, 0.0), axis=1, keepdims=True)
            near_lse = near_lse_ref[head]
            top = jnp.maximum(far_lse, near_lse)
            far_scale = jnp.exp(far_lse - top)
            near_scale = jnp.exp(near_lse - top)
            merged = far[h * 8 : (h + 1) * 8] * far_scale + near_ref[head] * near_scale
            out_ref[:, head * HD : (head + 1) * HD] = (merged / (far_scale + near_scale)).astype(
                jnp.bfloat16
            )


VMEM = pl.BlockSpec(memory_space=pltpu.VMEM)
SMEM = pl.BlockSpec(memory_space=pltpu.SMEM)
ANY = pl.BlockSpec(memory_space=pl.ANY)
HBM = pl.BlockSpec(memory_space=pltpu.HBM)


def params(mib):
    return pltpu.CompilerParams(vmem_limit_bytes=mib << 20)


def shards(
    prompt_of,
    suffix_len,
    query,
    new_key,
    new_value,
    suffix_key,
    suffix_value,
    prefix_key,
    prefix_value,
):
    place = lax.axis_index(NEAR).astype(jnp.int32).reshape(1)
    sent, *cuts = pl.pallas_call(
        prep_kernel,
        out_shape=[jax.ShapeDtypeStruct((KVH, 80, HD), jnp.bfloat16)]
        + [jax.ShapeDtypeStruct((2, PIECE, HD), jnp.bfloat16)] * 8,
        in_specs=[SMEM, HBM, HBM, HBM, HBM],
        out_specs=[VMEM] * 9,
        scratch_shapes=[
            pltpu.SMEM((HELD,), jnp.int32),
            pltpu.VMEM((HELD, HEADS * HD), jnp.bfloat16),
            pltpu.SemaphoreType.DMA((2,)),
            pltpu.SemaphoreType.DMA((8, 2)),
        ],
        compiler_params=params(12),
        name="prep",
    )(place, prompt_of, query, prefix_key, prefix_value)
    held = [cuts[0]]
    for step in range(1, 8):
        held.append(lax.ppermute(cuts[step], NEAR, [(i, i ^ step) for i in range(8)]))
    swapped = [lax.ppermute(piece, "c", [(0, 1), (1, 0)]) for piece in held]
    got = lax.all_to_all(sent, "y", 0, 0, tiled=True)
    outgoing = pl.pallas_call(
        pack_kernel,
        out_shape=jax.ShapeDtypeStruct((ROWS, HD), jnp.bfloat16),
        in_specs=[VMEM] + [ANY] * 4,
        out_specs=VMEM,
        compiler_params=params(8),
        name="pack",
    )(got, *held[4:])
    arrived = lax.all_to_all(outgoing.reshape(PROMPTS, 64, HD), FAR, 0, 0, tiled=True)

    near_out, near_lse = pl.pallas_call(
        near_kernel,
        grid=(HELD,),
        out_shape=[jax.ShapeDtypeStruct((HEADS, HELD, HD), jnp.float32)] * 2,
        in_specs=[
            SMEM,
            pl.BlockSpec((HELD, HEADS * HD), lambda i: (0, 0)),
            pl.BlockSpec((HELD, KVH * HD), lambda i: (0, 0)),
            pl.BlockSpec((HELD, KVH * HD), lambda i: (0, 0)),
            pl.BlockSpec((1, SUF, KVH * HD), lambda i: (i, 0, 0)),
            pl.BlockSpec((1, SUF, KVH * HD), lambda i: (i, 0, 0)),
        ],
        out_specs=[pl.BlockSpec((HEADS, HELD, HD), lambda i: (0, 0, 0))] * 2,
        scratch_shapes=[pltpu.VMEM((HEADS, HELD, HD), jnp.float32)],
        compiler_params=params(12),
        cost_estimate=pl.CostEstimate(flops=300_000_000, bytes_accessed=4_500_000, transcendentals=65536),
        name="near",
    )(
        suffix_len,
        query,
        new_key,
        new_value,
        suffix_key,
        suffix_value,
    )

    parcel = pl.pallas_call(
        far_kernel,
        out_shape=jax.ShapeDtypeStruct((PROMPTS, 80, HD), jnp.bfloat16),
        in_specs=[VMEM] * 17,
        out_specs=VMEM,
        scratch_shapes=[
            pltpu.VMEM((16, 256, PIECE), jnp.float32),
            pltpu.VMEM((RATIO, SLOTS, HD), jnp.bfloat16),
            pltpu.VMEM((RATIO, SLOTS, HD), jnp.bfloat16),
            pltpu.VMEM((SLOTS, HD), jnp.bfloat16),
        ],
        compiler_params=params(16),
        name="far",
    )(arrived.reshape(ROWS, HD), *held, *swapped)
    back = lax.all_to_all(parcel, FAR, 0, 0, tiled=True)
    chosen = pl.pallas_call(
        select_kernel,
        out_shape=jax.ShapeDtypeStruct((KVH, 80, HD), jnp.bfloat16),
        in_specs=[VMEM] * 2 + [ANY] * 2,
        out_specs=VMEM,
        compiler_params=params(8),
        name="select",
    )(got, back, near_out, near_lse)
    final = lax.all_to_all(chosen, "y", 0, 0, tiled=True)
    return pl.pallas_call(
        merge_kernel,
        out_shape=jax.ShapeDtypeStruct((HELD, HEADS * HD), jnp.bfloat16),
        in_specs=[VMEM] * 3,
        out_specs=VMEM,
        compiler_params=params(12),
        name="merge",
    )(final, near_out, near_lse)


def solution(mesh):
    fine = Mesh(mesh.devices.reshape(2, 8, 2, 4, 2), ALL)
    grp = ("xh", "z")
    blk = ("xl", "y", "c")
    in_specs = (
        P(ALL),
        P(ALL),
        P(ALL, None),
        P(ALL, None),
        P(ALL, None),
        P(ALL, None, None),
        P(ALL, None, None),
        P(grp, blk, None),
        P(grp, blk, None),
    )
    return jax.shard_map(
        shards, mesh=fine, in_specs=in_specs, out_specs=P(ALL, None), check_vma=False
    )
```

```python
import math

import jax
import jax.numpy as jnp
from jax import lax
from jax.experimental import pallas as pl
from jax.experimental.pallas import tpu as pltpu
from jax.sharding import Mesh, PartitionSpec as P

HD = 128
CAP = 2
HELD = 8
HEADS = 32
KVH = 4
RATIO = 8
PROMPTS = 32
SUF = 256
PIECE = 256
SLOTS = 256
ROWS = SLOTS * RATIO
NEG = -1e30
SCALE = HD ** (-0.5)
LOG2E = 1.4426950408889634
ALL = ("xh", "z", "xl", "y", "c")
NEAR = ("xl", "y")
FAR = ("xh", "z", "xl")


def slots_of(prompt_ref):
    prompts = [prompt_ref[i] for i in range(HELD)]
    slots = []
    for i in range(HELD):
        rank = jnp.int32(0)
        for j in range(i):
            rank = rank + jnp.where(prompts[j] == prompts[i], 1, 0)
        slots.append(prompts[i] * CAP + rank)
    return slots


def spread(values, index):
    picked = jnp.zeros(index.shape, jnp.int32)
    for i, value in enumerate(values):
        picked = jnp.where(index == i, value, picked)
    return picked


def prep_kernel(place_ref, prompt_hbm, query_hbm, key_ref, value_ref, send_ref, *refs):
    cut_refs = refs[:8]
    prompt_ref, query_ref, small_sem, cut_sem = refs[8:]
    small = [
        pltpu.make_async_copy(prompt_hbm, prompt_ref, small_sem.at[0]),
        pltpu.make_async_copy(query_hbm, query_ref, small_sem.at[1]),
    ]
    for copy in small:
        copy.start()
    place = place_ref[0]
    copies = []
    for step, cut_ref in enumerate(cut_refs):
        target = place ^ step
        prompt = target >> 2
        column = pl.multiple_of((target & 3) * HD, HD)
        for n, cache in enumerate((key_ref, value_ref)):
            copies.append(
                pltpu.make_async_copy(
                    cache.at[prompt, :, pl.ds(column, HD)], cut_ref.at[n], cut_sem.at[step, n]
                )
            )
            copies[-1].start()
    for copy in small:
        copy.wait()
    slots = slots_of(prompt_ref)
    lane = lax.broadcasted_iota(jnp.int32, (HELD, HD), 1)
    row = lax.broadcasted_iota(jnp.int32, (HELD, HD), 0)
    tags = jnp.concatenate(
        [spread(slots, lane & 7).astype(jnp.float32), spread(slots, row).astype(jnp.float32)], axis=0
    ).astype(jnp.bfloat16)
    for y in range(KVH):
        send_ref[y, :64] = jnp.concatenate(
            [
                query_ref[:, h * HD : (h + 1) * HD].astype(jnp.float32)
                for h in range(y * RATIO, (y + 1) * RATIO)
            ],
            axis=0,
        ).astype(jnp.bfloat16)
        send_ref[y, 64:] = tags
    for copy in copies:
        copy.wait()


def pack_kernel(got_ref, *refs):
    out_ref = refs[-1]
    held = got_ref[:, :64].reshape(256, HD)
    tags = [got_ref[y, 64:].astype(jnp.float32)[:1].astype(jnp.int32) for y in range(KVH)]
    half = lax.broadcasted_iota(jnp.int32, (1, HD), 1) < 64
    tag = jnp.concatenate([jnp.where(half, tags[0], tags[1]), jnp.where(half, tags[2], tags[3])], axis=1)
    lane_key = (lax.broadcasted_iota(jnp.int32, (1, 256), 1) >> 3) * 64 + tag
    chunk = 512
    for start in range(0, ROWS, chunk):
        row = lax.broadcasted_iota(jnp.int32, (chunk, 1), 0) + start
        row_key = ((row >> 1) & 3) * 512 + ((row >> 3) & 7) * 64 + (row >> 6) * 2 + (row & 1)
        select = (row_key == lane_key).astype(jnp.float32).astype(jnp.bfloat16)
        out_ref[start : start + chunk, :] = jnp.dot(
            select, held, preferred_element_type=jnp.float32
        ).astype(jnp.bfloat16)


def near_kernel(
    len_ref, query_ref, new_key_ref, new_value_ref, key_ref, value_ref, out_ref, lse_ref, heads_ref
):
    step = pl.program_id(0)

    @pl.when(step == 0)
    def _():
        for h in range(HEADS):
            heads_ref[h] = query_ref[:, h * HD : (h + 1) * HD].astype(jnp.float32)

    length = len_ref[step]
    query = heads_ref[:, pl.ds(step, 1), :].reshape(HEADS, HD)
    keys = key_ref[0]
    values = value_ref[0]
    held_row = lax.broadcasted_iota(jnp.int32, (HELD, 1), 0)

    def row_of(ref):
        rows = jnp.where(held_row == step, ref[...].astype(jnp.float32), 0.0)
        return jnp.sum(rows, axis=0, keepdims=True)

    new_key = row_of(new_key_ref)
    new_value = row_of(new_value_ref)

    def spread_heads(row):
        return jnp.concatenate(
            [jnp.broadcast_to(row[:, k * HD : (k + 1) * HD], (RATIO, HD)) for k in range(KVH)], axis=0
        )

    scores = jnp.concatenate(
        [
            lax.dot_general(
                query.astype(jnp.bfloat16),
                keys[:, k * HD : (k + 1) * HD],
                (((1,), (1,)), ((), ())),
                preferred_element_type=jnp.float32,
            )[k * RATIO : (k + 1) * RATIO]
            for k in range(KVH)
        ],
        axis=0,
    ) * SCALE
    own = jnp.sum(query * spread_heads(new_key), axis=1, keepdims=True) * SCALE
    live = lax.broadcasted_iota(jnp.int32, (1, SUF), 1) < length
    scores = jnp.where(live, scores, NEG)
    top = jnp.maximum(jnp.max(scores, axis=1, keepdims=True), own)
    weights = jnp.where(live, jnp.exp(scores - top), 0.0)
    own_weight = jnp.exp(own - top)
    total = jnp.sum(weights, axis=1, keepdims=True) + own_weight
    rounded = weights.astype(jnp.bfloat16)
    mixed = jnp.concatenate(
        [
            jnp.dot(rounded, values[:, k * HD : (k + 1) * HD], preferred_element_type=jnp.float32)[
                k * RATIO : (k + 1) * RATIO
            ]
            for k in range(KVH)
        ],
        axis=0,
    )
    mixed = mixed + own_weight.astype(jnp.bfloat16).astype(jnp.float32) * spread_heads(new_value)
    out_ref[:, pl.ds(step, 1), :] = (mixed / total).reshape(HEADS, 1, HD)
    lse_ref[:, pl.ds(step, 1), :] = jnp.broadcast_to(top + jnp.log(total), (HEADS, HD)).reshape(
        HEADS, 1, HD
    )


def far_kernel(query_ref, *refs):
    sources = refs[:16]
    out_ref, score_ref, query_scr, mixed_scr, stat_scr, cache_ref, sems = refs[16:]
    copies = [
        pltpu.make_async_copy(source, cache_ref.at[n], sems.at[n]) for n, source in enumerate(sources)
    ]
    for copy in copies:
        copy.start()
    pieces = [cache_ref.at[n] for n in range(16)]
    span = 32
    block = span * RATIO
    tokens = 16 * PIECE
    queries = query_ref[...].astype(jnp.float32).reshape(32, RATIO, 8, HD)
    biggest = jnp.max(jnp.max(jnp.abs(queries), axis=1).reshape(SLOTS, HD), axis=1, keepdims=True)
    valid = (biggest > 0).astype(jnp.float32)
    row = lax.broadcasted_iota(jnp.int32, (SLOTS, SLOTS), 0)
    lane = lax.broadcasted_iota(jnp.int32, (SLOTS, SLOTS), 1)
    wide = jnp.broadcast_to(valid, (SLOTS, SLOTS)).astype(jnp.bfloat16)
    before = jnp.dot(
        (lane < row).astype(jnp.float32).astype(jnp.bfloat16), wide, preferred_element_type=jnp.float32
    )
    order = jnp.where(valid > 0, before, -1.0).astype(jnp.int32)
    gather = (order == lane).astype(jnp.float32).astype(jnp.bfloat16)
    count = jnp.sum(valid).astype(jnp.int32)
    for h in range(RATIO):
        query_scr[h] = lax.dot_general(
            gather,
            queries[:, h].reshape(SLOTS, HD).astype(jnp.bfloat16),
            (((0,), (0,)), ((), ())),
            preferred_element_type=jnp.float32,
        ).astype(jnp.bfloat16)
    mixed_scr[...] = jnp.zeros_like(mixed_scr)
    stat_scr[...] = jnp.zeros_like(stat_scr)
    for copy in copies:
        copy.wait()

    @pl.loop(0, (count + span - 1) // span)
    def _(index):
        start = pl.multiple_of(index * span, span)
        query = query_scr[:, pl.ds(start, span), :].reshape(block, HD)
        peak = jnp.full((block, HD), -jnp.inf, jnp.float32)
        for n, piece in enumerate(pieces):
            scores = lax.dot_general(
                query, piece[0], (((1,), (1,)), ((), ())), preferred_element_type=jnp.float32
            )
            score_ref[n] = scores
            peak = jnp.maximum(peak, jnp.maximum(scores[:, :HD], scores[:, HD:]))
        peak = jnp.max(peak, axis=1, keepdims=True)
        total = jnp.zeros((block, HD), jnp.float32)
        mixed = jnp.zeros((block, HD), jnp.float32)
        for n, piece in enumerate(pieces):
            weights = jnp.exp2((score_ref[n] - peak) * (SCALE * LOG2E))
            total = total + (weights[:, :HD] + weights[:, HD:])
            mixed = mixed + jnp.dot(
                weights.astype(jnp.bfloat16), piece[1], preferred_element_type=jnp.float32
            )
        total = jnp.sum(total, axis=1, keepdims=True)
        mixed_scr[:, pl.ds(start, span), :] = (mixed / total).astype(jnp.bfloat16).reshape(RATIO, span, HD)
        lse = peak * SCALE + jnp.log(total)
        stat_scr[pl.ds(start, span), :] = split_stat(lse.reshape(RATIO, span, 1), span).astype(jnp.bfloat16)

    idle = 1.0 - valid
    mean = sum(piece[1].astype(jnp.float32).reshape(PIECE // 8, 8, HD).sum(axis=0) for piece in pieces)
    mean = jnp.sum(mean, axis=0, keepdims=True) / tokens
    heads = []
    for h in range(RATIO):
        spread_out = jnp.dot(gather, mixed_scr[h], preferred_element_type=jnp.float32) + idle * mean
        heads.append(spread_out.reshape(32, 8, HD))
    for h in range(0, RATIO, 2):
        out_ref[:, h * 8 : h * 8 + 16] = jnp.concatenate(heads[h : h + 2], axis=1).astype(jnp.bfloat16)
    even = split_stat(jnp.full((RATIO, SLOTS, 1), math.log(tokens), jnp.float32), SLOTS)
    stat = jnp.dot(gather, stat_scr[...], preferred_element_type=jnp.float32) + idle * even
    stat = stat.reshape(32, 8, HD)
    out_ref[:, 64:] = jnp.concatenate([stat, jnp.zeros_like(stat)], axis=1).astype(jnp.bfloat16)


def split_stat(lse, span):
    high = lse.astype(jnp.bfloat16).astype(jnp.float32)
    rest = lse - high
    middle = rest.astype(jnp.bfloat16).astype(jnp.float32)
    low = rest - middle
    lane = lax.broadcasted_iota(jnp.int32, (span, HD), 1)
    stat = jnp.zeros((span, HD), jnp.float32)
    for h in range(RATIO):
        for n, part in enumerate((high, middle, low)):
            stat = jnp.where(lane == n * 8 + h, part[h], stat)
    return stat


def select_kernel(got_ref, back_ref, *refs):
    send_ref = refs[-1]
    tags = [got_ref[y, 64:].astype(jnp.float32)[8:, :1].astype(jnp.int32) for y in range(KVH)]
    lane = lax.broadcasted_iota(jnp.int32, (1, ROWS), 1)
    lane_key = ((lane >> 1) & 3) * 512 + ((lane >> 3) & 7) * 64 + (lane >> 6) * 2 + (lane & 1)
    tag = jnp.concatenate([tags[y] for y in range(KVH) for _ in range(RATIO)], axis=0)
    row_key = (lax.broadcasted_iota(jnp.int32, (256, 1), 0) >> 3) * 64 + tag
    select = (row_key == lane_key).astype(jnp.float32).astype(jnp.bfloat16)
    far = jnp.dot(select, back_ref[:, :64].reshape(ROWS, HD), preferred_element_type=jnp.float32)
    send_ref[:, :64] = far.astype(jnp.bfloat16).reshape(KVH, 64, HD)
    stats = back_ref[:, 64:].astype(jnp.float32)[:, :8].reshape(SLOTS, HD).astype(jnp.bfloat16)
    lane = lax.broadcasted_iota(jnp.int32, (1, SLOTS), 1)
    lane_key = ((lane >> 1) & 3) * 64 + (lane >> 3) * 2 + (lane & 1)
    row_key = (lax.broadcasted_iota(jnp.int32, (32, 1), 0) >> 3) * 64 + jnp.concatenate(tags, axis=0)
    select = (row_key == lane_key).astype(jnp.float32).astype(jnp.bfloat16)
    stat = jnp.dot(select, stats, preferred_element_type=jnp.float32).reshape(KVH, 8, HD)
    send_ref[:, 64:] = jnp.concatenate([stat, jnp.zeros_like(stat)], axis=1).astype(jnp.bfloat16)


def merge_kernel(back_ref, near_ref, near_lse_ref, out_ref):
    lane = lax.broadcasted_iota(jnp.int32, (HELD, HD), 1)
    for y in range(KVH):
        far = back_ref[y, :64].astype(jnp.float32)
        stat = jnp.where(lane < 24, back_ref[y, 64:].astype(jnp.float32)[:8], 0.0)
        for h in range(RATIO):
            head = y * RATIO + h
            far_lse = jnp.sum(jnp.where((lane & 7) == h, stat, 0.0), axis=1, keepdims=True)
            near_lse = near_lse_ref[head]
            top = jnp.maximum(far_lse, near_lse)
            far_scale = jnp.exp(far_lse - top)
            near_scale = jnp.exp(near_lse - top)
            merged = far[h * 8 : (h + 1) * 8] * far_scale + near_ref[head] * near_scale
            out_ref[:, head * HD : (head + 1) * HD] = (merged / (far_scale + near_scale)).astype(
                jnp.bfloat16
            )


VMEM = pl.BlockSpec(memory_space=pltpu.VMEM)
SMEM = pl.BlockSpec(memory_space=pltpu.SMEM)
ANY = pl.BlockSpec(memory_space=pl.ANY)
HBM = pl.BlockSpec(memory_space=pltpu.HBM)


def params(mib):
    return pltpu.CompilerParams(vmem_limit_bytes=mib << 20)


def shards(
    prompt_of,
    suffix_len,
    query,
    new_key,
    new_value,
    suffix_key,
    suffix_value,
    prefix_key,
    prefix_value,
):
    place = lax.axis_index(NEAR).astype(jnp.int32).reshape(1)
    sent, *cuts = pl.pallas_call(
        prep_kernel,
        out_shape=[jax.ShapeDtypeStruct((KVH, 80, HD), jnp.bfloat16)]
        + [jax.ShapeDtypeStruct((2, PIECE, HD), jnp.bfloat16)] * 8,
        in_specs=[SMEM, HBM, HBM, HBM, HBM],
        out_specs=[VMEM] * 9,
        scratch_shapes=[
            pltpu.SMEM((HELD,), jnp.int32),
            pltpu.VMEM((HELD, HEADS * HD), jnp.bfloat16),
            pltpu.SemaphoreType.DMA((2,)),
            pltpu.SemaphoreType.DMA((8, 2)),
        ],
        compiler_params=params(12),
        name="prep",
    )(place, prompt_of, query, prefix_key, prefix_value)
    held = [cuts[0]]
    for step in range(1, 8):
        held.append(lax.ppermute(cuts[step], NEAR, [(i, i ^ step) for i in range(8)]))
    swapped = [lax.ppermute(piece, "c", [(0, 1), (1, 0)]) for piece in held]
    got = lax.all_to_all(sent, "y", 0, 0, tiled=True)
    outgoing = pl.pallas_call(
        pack_kernel,
        out_shape=jax.ShapeDtypeStruct((ROWS, HD), jnp.bfloat16),
        in_specs=[VMEM] + [ANY] * 4,
        out_specs=VMEM,
        compiler_params=params(8),
        name="pack",
    )(got, *held[4:])
    arrived = lax.all_to_all(outgoing.reshape(PROMPTS, 64, HD), FAR, 0, 0, tiled=True)

    near_out, near_lse = pl.pallas_call(
        near_kernel,
        grid=(HELD,),
        out_shape=[jax.ShapeDtypeStruct((HEADS, HELD, HD), jnp.float32)] * 2,
        in_specs=[
            SMEM,
            pl.BlockSpec((HELD, HEADS * HD), lambda i: (0, 0)),
            pl.BlockSpec((HELD, KVH * HD), lambda i: (0, 0)),
            pl.BlockSpec((HELD, KVH * HD), lambda i: (0, 0)),
            pl.BlockSpec((1, SUF, KVH * HD), lambda i: (i, 0, 0)),
            pl.BlockSpec((1, SUF, KVH * HD), lambda i: (i, 0, 0)),
        ],
        out_specs=[pl.BlockSpec((HEADS, HELD, HD), lambda i: (0, 0, 0))] * 2,
        scratch_shapes=[pltpu.VMEM((HEADS, HELD, HD), jnp.float32)],
        compiler_params=params(12),
        cost_estimate=pl.CostEstimate(flops=300_000_000, bytes_accessed=4_500_000, transcendentals=65536),
        name="near",
    )(
        suffix_len,
        query,
        new_key,
        new_value,
        suffix_key,
        suffix_value,
    )

    parcel = pl.pallas_call(
        far_kernel,
        out_shape=jax.ShapeDtypeStruct((PROMPTS, 80, HD), jnp.bfloat16),
        in_specs=[VMEM] + [ANY] * 16,
        out_specs=VMEM,
        scratch_shapes=[
            pltpu.VMEM((16, 256, PIECE), jnp.float32),
            pltpu.VMEM((RATIO, SLOTS, HD), jnp.bfloat16),
            pltpu.VMEM((RATIO, SLOTS, HD), jnp.bfloat16),
            pltpu.VMEM((SLOTS, HD), jnp.bfloat16),
            pltpu.VMEM((16, 2, PIECE, HD), jnp.bfloat16),
            pltpu.SemaphoreType.DMA((16,)),
        ],
        compiler_params=params(60),
        name="far",
    )(arrived.reshape(ROWS, HD), *held, *swapped)
    back = lax.all_to_all(parcel, FAR, 0, 0, tiled=True)
    chosen = pl.pallas_call(
        select_kernel,
        out_shape=jax.ShapeDtypeStruct((KVH, 80, HD), jnp.bfloat16),
        in_specs=[VMEM] * 2 + [ANY] * 2,
        out_specs=VMEM,
        compiler_params=params(8),
        name="select",
    )(got, back, near_out, near_lse)
    final = lax.all_to_all(chosen, "y", 0, 0, tiled=True)
    return pl.pallas_call(
        merge_kernel,
        out_shape=jax.ShapeDtypeStruct((HELD, HEADS * HD), jnp.bfloat16),
        in_specs=[VMEM] * 3,
        out_specs=VMEM,
        compiler_params=params(12),
        name="merge",
    )(final, near_out, near_lse)


def solution(mesh):
    fine = Mesh(mesh.devices.reshape(2, 8, 2, 4, 2), ALL)
    grp = ("xh", "z")
    blk = ("xl", "y", "c")
    in_specs = (
        P(ALL),
        P(ALL),
        P(ALL, None),
        P(ALL, None),
        P(ALL, None),
        P(ALL, None, None),
        P(ALL, None, None),
        P(grp, blk, None),
        P(grp, blk, None),
    )
    return jax.shard_map(
        shards, mesh=fine, in_specs=in_specs, out_specs=P(ALL, None), check_vma=False
    )
```

```python
import math

import jax
import jax.numpy as jnp
from jax import lax
from jax.experimental import pallas as pl
from jax.experimental.pallas import tpu as pltpu
from jax.sharding import Mesh, PartitionSpec as P

HD = 128
CAP = 2
HELD = 8
HEADS = 32
KVH = 4
RATIO = 8
PROMPTS = 32
SUF = 256
PIECE = 256
SLOTS = 256
ROWS = SLOTS * RATIO
NEG = -1e30
SCALE = HD ** (-0.5)
LOG2E = 1.4426950408889634
ALL = ("xh", "z", "xl", "y", "c")
NEAR = ("xl", "y")
FAR = ("xh", "z", "xl")


def slots_of(prompt_ref):
    prompts = [prompt_ref[i] for i in range(HELD)]
    slots = []
    for i in range(HELD):
        rank = jnp.int32(0)
        for j in range(i):
            rank = rank + jnp.where(prompts[j] == prompts[i], 1, 0)
        slots.append(prompts[i] * CAP + rank)
    return slots


def spread(values, index):
    picked = jnp.zeros(index.shape, jnp.int32)
    for i, value in enumerate(values):
        picked = jnp.where(index == i, value, picked)
    return picked


def prep_kernel(place_ref, prompt_hbm, query_hbm, key_ref, value_ref, out_ref, tag_ref, *refs):
    cut_refs = refs[:8]
    prompt_ref, query_ref, small_sem, cut_sem = refs[8:]
    small = [
        pltpu.make_async_copy(prompt_hbm, prompt_ref, small_sem.at[0]),
        pltpu.make_async_copy(query_hbm, query_ref, small_sem.at[1]),
    ]
    for copy in small:
        copy.start()
    place = place_ref[0]
    copies = []
    for step, cut_ref in enumerate(cut_refs):
        target = place ^ step
        prompt = target >> 2
        column = pl.multiple_of((target & 3) * HD, HD)
        for n, cache in enumerate((key_ref, value_ref)):
            copies.append(
                pltpu.make_async_copy(
                    cache.at[prompt, :, pl.ds(column, HD)], cut_ref.at[n], cut_sem.at[step, n]
                )
            )
            copies[-1].start()
    for copy in small:
        copy.wait()
    slots = slots_of(prompt_ref)
    row = lax.broadcasted_iota(jnp.int32, (16, HD), 0)
    tag_ref[...] = spread(slots, row & 7).astype(jnp.float32).astype(jnp.bfloat16)
    held = jnp.concatenate(
        [query_ref[:, h * HD : (h + 1) * HD].astype(jnp.float32) for h in range(HEADS)], axis=0
    ).astype(jnp.bfloat16)
    lane = lax.broadcasted_iota(jnp.int32, (1, HEADS * HELD), 1)
    lane_key = (lane >> 3) * 64 + spread(slots, lane & 7)
    chunk = 512
    for start in range(0, ROWS, chunk):
        row = lax.broadcasted_iota(jnp.int32, (chunk, 1), 0) + start
        row_key = (((row >> 4) & 3) * 8 + (row & 7)) * 64 + (row >> 6) * 2 + ((row >> 3) & 1)
        select = (row_key == lane_key).astype(jnp.float32).astype(jnp.bfloat16)
        out_ref[start : start + chunk, :] = jnp.dot(
            select, held, preferred_element_type=jnp.float32
        ).astype(jnp.bfloat16)
    for copy in copies:
        copy.wait()


def near_kernel(
    len_ref, query_ref, new_key_ref, new_value_ref, key_ref, value_ref, out_ref, lse_ref, heads_ref
):
    step = pl.program_id(0)

    @pl.when(step == 0)
    def _():
        for h in range(HEADS):
            heads_ref[h] = query_ref[:, h * HD : (h + 1) * HD].astype(jnp.float32)

    length = len_ref[step]
    query = heads_ref[:, pl.ds(step, 1), :].reshape(HEADS, HD)
    keys = key_ref[0]
    values = value_ref[0]
    held_row = lax.broadcasted_iota(jnp.int32, (HELD, 1), 0)

    def row_of(ref):
        rows = jnp.where(held_row == step, ref[...].astype(jnp.float32), 0.0)
        return jnp.sum(rows, axis=0, keepdims=True)

    new_key = row_of(new_key_ref)
    new_value = row_of(new_value_ref)

    def spread_heads(row):
        return jnp.concatenate(
            [jnp.broadcast_to(row[:, k * HD : (k + 1) * HD], (RATIO, HD)) for k in range(KVH)], axis=0
        )

    scores = jnp.concatenate(
        [
            lax.dot_general(
                query.astype(jnp.bfloat16),
                keys[:, k * HD : (k + 1) * HD],
                (((1,), (1,)), ((), ())),
                preferred_element_type=jnp.float32,
            )[k * RATIO : (k + 1) * RATIO]
            for k in range(KVH)
        ],
        axis=0,
    ) * SCALE
    own = jnp.sum(query * spread_heads(new_key), axis=1, keepdims=True) * SCALE
    live = lax.broadcasted_iota(jnp.int32, (1, SUF), 1) < length
    scores = jnp.where(live, scores, NEG)
    top = jnp.maximum(jnp.max(scores, axis=1, keepdims=True), own)
    weights = jnp.where(live, jnp.exp(scores - top), 0.0)
    own_weight = jnp.exp(own - top)
    total = jnp.sum(weights, axis=1, keepdims=True) + own_weight
    rounded = weights.astype(jnp.bfloat16)
    mixed = jnp.concatenate(
        [
            jnp.dot(rounded, values[:, k * HD : (k + 1) * HD], preferred_element_type=jnp.float32)[
                k * RATIO : (k + 1) * RATIO
            ]
            for k in range(KVH)
        ],
        axis=0,
    )
    mixed = mixed + own_weight.astype(jnp.bfloat16).astype(jnp.float32) * spread_heads(new_value)
    out_ref[:, pl.ds(step, 1), :] = (mixed / total).reshape(HEADS, 1, HD)
    lse_ref[:, pl.ds(step, 1), :] = jnp.broadcast_to(top + jnp.log(total), (HEADS, HD)).reshape(
        HEADS, 1, HD
    )


def far_kernel(query_ref, *refs):
    sources = refs[:16]
    out_ref, score_ref, wide_scr, query_scr, mixed_scr, stat_scr, cache_ref, sems = refs[16:]
    copies = [
        pltpu.make_async_copy(source, cache_ref.at[n], sems.at[n]) for n, source in enumerate(sources)
    ]
    for copy in copies:
        copy.start()
    pieces = [cache_ref.at[n] for n in range(16)]
    span = 32
    block = span * RATIO
    tokens = 16 * PIECE
    wide_scr[...] = query_ref[...].astype(jnp.float32)
    queries = [wide_scr[pl.ds(h, SLOTS, RATIO), :] for h in range(RATIO)]
    biggest = jnp.abs(queries[0])
    for h in range(1, RATIO):
        biggest = jnp.maximum(biggest, jnp.abs(queries[h]))
    biggest = jnp.max(biggest, axis=1, keepdims=True)
    valid = (biggest > 0).astype(jnp.float32)
    row = lax.broadcasted_iota(jnp.int32, (SLOTS, SLOTS), 0)
    lane = lax.broadcasted_iota(jnp.int32, (SLOTS, SLOTS), 1)
    wide = jnp.broadcast_to(valid, (SLOTS, SLOTS)).astype(jnp.bfloat16)
    before = jnp.dot(
        (lane < row).astype(jnp.float32).astype(jnp.bfloat16), wide, preferred_element_type=jnp.float32
    )
    order = jnp.where(valid > 0, before, -1.0).astype(jnp.int32)
    gather = (order == lane).astype(jnp.float32).astype(jnp.bfloat16)
    count = jnp.sum(valid).astype(jnp.int32)
    for h in range(RATIO):
        query_scr[h] = lax.dot_general(
            gather,
            queries[h].astype(jnp.bfloat16),
            (((0,), (0,)), ((), ())),
            preferred_element_type=jnp.float32,
        ).astype(jnp.bfloat16)
    mixed_scr[...] = jnp.zeros_like(mixed_scr)
    stat_scr[...] = jnp.zeros_like(stat_scr)
    for copy in copies:
        copy.wait()

    @pl.loop(0, (count + span - 1) // span)
    def _(index):
        start = pl.multiple_of(index * span, span)
        query = query_scr[:, pl.ds(start, span), :].reshape(block, HD)
        peak = jnp.full((block, HD), -jnp.inf, jnp.float32)
        for n, piece in enumerate(pieces):
            scores = lax.dot_general(
                query, piece[0], (((1,), (1,)), ((), ())), preferred_element_type=jnp.float32
            )
            score_ref[n] = scores
            peak = jnp.maximum(peak, jnp.maximum(scores[:, :HD], scores[:, HD:]))
        peak = jnp.max(peak, axis=1, keepdims=True)
        total = jnp.zeros((block, HD), jnp.float32)
        mixed = jnp.zeros((block, HD), jnp.float32)
        for n, piece in enumerate(pieces):
            weights = jnp.exp2((score_ref[n] - peak) * (SCALE * LOG2E))
            total = total + (weights[:, :HD] + weights[:, HD:])
            mixed = mixed + jnp.dot(
                weights.astype(jnp.bfloat16), piece[1], preferred_element_type=jnp.float32
            )
        total = jnp.sum(total, axis=1, keepdims=True)
        mixed_scr[:, pl.ds(start, span), :] = (mixed / total).astype(jnp.bfloat16).reshape(RATIO, span, HD)
        lse = peak * SCALE + jnp.log(total)
        stat_scr[pl.ds(start, span), :] = split_stat(lse.reshape(RATIO, span, 1), span).astype(jnp.bfloat16)

    idle = 1.0 - valid
    mean = sum(piece[1].astype(jnp.float32).reshape(PIECE // 8, 8, HD).sum(axis=0) for piece in pieces)
    mean = jnp.sum(mean, axis=0, keepdims=True) / tokens
    heads = []
    for h in range(RATIO):
        spread_out = jnp.dot(gather, mixed_scr[h], preferred_element_type=jnp.float32) + idle * mean
        heads.append(spread_out.reshape(32, 8, HD))
    for h in range(0, RATIO, 2):
        out_ref[:, h * 8 : h * 8 + 16] = jnp.concatenate(heads[h : h + 2], axis=1).astype(jnp.bfloat16)
    even = split_stat(jnp.full((RATIO, SLOTS, 1), math.log(tokens), jnp.float32), SLOTS)
    stat = jnp.dot(gather, stat_scr[...], preferred_element_type=jnp.float32) + idle * even
    stat = stat.reshape(32, 8, HD)
    out_ref[:, 64:] = jnp.concatenate([stat, jnp.zeros_like(stat)], axis=1).astype(jnp.bfloat16)


def split_stat(lse, span):
    high = lse.astype(jnp.bfloat16).astype(jnp.float32)
    rest = lse - high
    middle = rest.astype(jnp.bfloat16).astype(jnp.float32)
    low = rest - middle
    lane = lax.broadcasted_iota(jnp.int32, (span, HD), 1)
    stat = jnp.zeros((span, HD), jnp.float32)
    for h in range(RATIO):
        for n, part in enumerate((high, middle, low)):
            stat = jnp.where(lane == n * 8 + h, part[h], stat)
    return stat


def select_kernel(place_ref, back_ref, *refs):
    tag_refs = refs[:4]
    send_ref = refs[-1]
    sources = [(place_ref[0] & 3) ^ step for step in range(4)]
    tags = [tag_ref[...].astype(jnp.float32)[:8, :1].astype(jnp.int32) for tag_ref in tag_refs]
    lane = lax.broadcasted_iota(jnp.int32, (1, ROWS), 1)
    lane_key = ((lane >> 1) & 3) * 512 + ((lane >> 3) & 7) * 64 + (lane >> 6) * 2 + (lane & 1)
    row_key = jnp.concatenate(
        [tags[s] + (sources[s] * 512 + h * 64) for s in range(4) for h in range(RATIO)], axis=0
    )
    select = (row_key == lane_key).astype(jnp.float32).astype(jnp.bfloat16)
    far = jnp.dot(select, back_ref[:, :64].reshape(ROWS, HD), preferred_element_type=jnp.float32)
    for s in range(4):
        send_ref[sources[s], :64] = far[s * 64 : (s + 1) * 64].astype(jnp.bfloat16)
    stats = back_ref[:, 64:].astype(jnp.float32)[:, :8].reshape(SLOTS, HD).astype(jnp.bfloat16)
    lane = lax.broadcasted_iota(jnp.int32, (1, SLOTS), 1)
    lane_key = ((lane >> 1) & 3) * 64 + (lane >> 3) * 2 + (lane & 1)
    row_key = jnp.concatenate([tags[s] + sources[s] * 64 for s in range(4)], axis=0)
    select = (row_key == lane_key).astype(jnp.float32).astype(jnp.bfloat16)
    stat = jnp.dot(select, stats, preferred_element_type=jnp.float32)
    for s in range(4):
        mine = stat[s * 8 : (s + 1) * 8]
        send_ref[sources[s], 64:] = jnp.concatenate([mine, jnp.zeros_like(mine)], axis=0).astype(
            jnp.bfloat16
        )


def merge_kernel(back_ref, near_ref, near_lse_ref, out_ref):
    lane = lax.broadcasted_iota(jnp.int32, (HELD, HD), 1)
    for y in range(KVH):
        far = back_ref[y, :64].astype(jnp.float32)
        stat = jnp.where(lane < 24, back_ref[y, 64:].astype(jnp.float32)[:8], 0.0)
        for h in range(RATIO):
            head = y * RATIO + h
            far_lse = jnp.sum(jnp.where((lane & 7) == h, stat, 0.0), axis=1, keepdims=True)
            near_lse = near_lse_ref[head]
            top = jnp.maximum(far_lse, near_lse)
            far_scale = jnp.exp(far_lse - top)
            near_scale = jnp.exp(near_lse - top)
            merged = far[h * 8 : (h + 1) * 8] * far_scale + near_ref[head] * near_scale
            out_ref[:, head * HD : (head + 1) * HD] = (merged / (far_scale + near_scale)).astype(
                jnp.bfloat16
            )


VMEM = pl.BlockSpec(memory_space=pltpu.VMEM)
SMEM = pl.BlockSpec(memory_space=pltpu.SMEM)
ANY = pl.BlockSpec(memory_space=pl.ANY)


def params(mib):
    return pltpu.CompilerParams(vmem_limit_bytes=mib << 20)


def shards(
    prompt_of,
    suffix_len,
    query,
    new_key,
    new_value,
    suffix_key,
    suffix_value,
    prefix_key,
    prefix_value,
):
    place = lax.axis_index(NEAR).astype(jnp.int32).reshape(1)
    outgoing, tag, *cuts = pl.pallas_call(
        prep_kernel,
        out_shape=[
            jax.ShapeDtypeStruct((ROWS, HD), jnp.bfloat16),
            jax.ShapeDtypeStruct((16, HD), jnp.bfloat16),
        ]
        + [jax.ShapeDtypeStruct((2, PIECE, HD), jnp.bfloat16)] * 8,
        in_specs=[SMEM, ANY, ANY, ANY, ANY],
        out_specs=[VMEM] * 2 + [ANY] * 8,
        scratch_shapes=[
            pltpu.SMEM((HELD,), jnp.int32),
            pltpu.VMEM((HELD, HEADS * HD), jnp.bfloat16),
            pltpu.SemaphoreType.DMA((2,)),
            pltpu.SemaphoreType.DMA((8, 2)),
        ],
        compiler_params=params(60),
        name="prep",
    )(place, prompt_of, query, prefix_key, prefix_value)
    arrived = lax.all_to_all(outgoing.reshape(128, 16, HD), FAR + ("y",), 0, 0, tiled=True)
    held = [cuts[0]]
    for step in range(1, 8):
        held.append(lax.ppermute(cuts[step], NEAR, [(i, i ^ step) for i in range(8)]))
    swapped = [lax.ppermute(piece, "c", [(0, 1), (1, 0)]) for piece in held]
    tags = [tag]
    for step in range(1, 4):
        tags.append(lax.ppermute(tag, "y", [(i, i ^ step) for i in range(4)]))

    near_out, near_lse = pl.pallas_call(
        near_kernel,
        grid=(HELD,),
        out_shape=[jax.ShapeDtypeStruct((HEADS, HELD, HD), jnp.float32)] * 2,
        in_specs=[
            SMEM,
            pl.BlockSpec((HELD, HEADS * HD), lambda i: (0, 0)),
            pl.BlockSpec((HELD, KVH * HD), lambda i: (0, 0)),
            pl.BlockSpec((HELD, KVH * HD), lambda i: (0, 0)),
            pl.BlockSpec((1, SUF, KVH * HD), lambda i: (i, 0, 0)),
            pl.BlockSpec((1, SUF, KVH * HD), lambda i: (i, 0, 0)),
        ],
        out_specs=[pl.BlockSpec((HEADS, HELD, HD), lambda i: (0, 0, 0))] * 2,
        scratch_shapes=[pltpu.VMEM((HEADS, HELD, HD), jnp.float32)],
        compiler_params=params(12),
        cost_estimate=pl.CostEstimate(flops=300_000_000, bytes_accessed=4_500_000, transcendentals=65536),
        name="near",
    )(
        suffix_len,
        query,
        new_key,
        new_value,
        suffix_key,
        suffix_value,
    )

    parcel = pl.pallas_call(
        far_kernel,
        out_shape=jax.ShapeDtypeStruct((PROMPTS, 80, HD), jnp.bfloat16),
        in_specs=[VMEM] + [ANY] * 16,
        out_specs=VMEM,
        scratch_shapes=[
            pltpu.VMEM((16, 256, PIECE), jnp.float32),
            pltpu.VMEM((ROWS, HD), jnp.float32),
            pltpu.VMEM((RATIO, SLOTS, HD), jnp.bfloat16),
            pltpu.VMEM((RATIO, SLOTS, HD), jnp.bfloat16),
            pltpu.VMEM((SLOTS, HD), jnp.bfloat16),
            pltpu.VMEM((16, 2, PIECE, HD), jnp.bfloat16),
            pltpu.SemaphoreType.DMA((16,)),
        ],
        compiler_params=params(60),
        name="far",
    )(arrived.reshape(ROWS, HD), *held, *swapped)
    back = lax.all_to_all(parcel, FAR, 0, 0, tiled=True)
    chosen = pl.pallas_call(
        select_kernel,
        out_shape=jax.ShapeDtypeStruct((KVH, 80, HD), jnp.bfloat16),
        in_specs=[SMEM] + [VMEM] * 5 + [ANY] * 2,
        out_specs=VMEM,
        compiler_params=params(8),
        name="select",
    )(place, back, *tags, near_out, near_lse)
    final = lax.all_to_all(chosen, "y", 0, 0, tiled=True)
    return pl.pallas_call(
        merge_kernel,
        out_shape=jax.ShapeDtypeStruct((HELD, HEADS * HD), jnp.bfloat16),
        in_specs=[VMEM] * 3,
        out_specs=VMEM,
        compiler_params=params(12),
        name="merge",
    )(final, near_out, near_lse)


def solution(mesh):
    fine = Mesh(mesh.devices.reshape(2, 8, 2, 4, 2), ALL)
    grp = ("xh", "z")
    blk = ("xl", "y", "c")
    in_specs = (
        P(ALL),
        P(ALL),
        P(ALL, None),
        P(ALL, None),
        P(ALL, None),
        P(ALL, None, None),
        P(ALL, None, None),
        P(grp, blk, None),
        P(grp, blk, None),
    )
    return jax.shard_map(
        shards, mesh=fine, in_specs=in_specs, out_specs=P(ALL, None), check_vma=False
    )
```

```python
import math

import jax
import jax.numpy as jnp
from jax import lax
from jax.experimental import pallas as pl
from jax.experimental.pallas import tpu as pltpu
from jax.sharding import Mesh, PartitionSpec as P

HD = 128
CAP = 2
HELD = 8
HEADS = 32
KVH = 4
RATIO = 8
PROMPTS = 32
SUF = 256
PIECE = 256
SLOTS = 256
ROWS = SLOTS * RATIO
NEG = -1e30
SCALE = HD ** (-0.5)
LOG2E = 1.4426950408889634
ALL = ("xh", "z", "xl", "y", "c")
NEAR = ("xl", "y")
FAR = ("xh", "z", "xl")


def slots_of(prompt_ref):
    prompts = [prompt_ref[i] for i in range(HELD)]
    slots = []
    for i in range(HELD):
        rank = jnp.int32(0)
        for j in range(i):
            rank = rank + jnp.where(prompts[j] == prompts[i], 1, 0)
        slots.append(prompts[i] * CAP + rank)
    return slots


def spread(values, index):
    picked = jnp.zeros(index.shape, jnp.int32)
    for i, value in enumerate(values):
        picked = jnp.where(index == i, value, picked)
    return picked


def prep_kernel(place_ref, prompt_hbm, query_hbm, key_ref, value_ref, *refs):
    send_refs = refs[:4]
    cut_refs = refs[4:12]
    prompt_ref, query_ref, small_sem, cut_sem = refs[12:]
    small = [
        pltpu.make_async_copy(prompt_hbm, prompt_ref, small_sem.at[0]),
        pltpu.make_async_copy(query_hbm, query_ref, small_sem.at[1]),
    ]
    for copy in small:
        copy.start()
    place = place_ref[0]
    copies = []
    for step, cut_ref in enumerate(cut_refs):
        target = place ^ step
        prompt = target >> 2
        column = pl.multiple_of((target & 3) * HD, HD)
        for n, cache in enumerate((key_ref, value_ref)):
            copies.append(
                pltpu.make_async_copy(
                    cache.at[prompt, :, pl.ds(column, HD)], cut_ref.at[n], cut_sem.at[step, n]
                )
            )
            copies[-1].start()
    for copy in small:
        copy.wait()
    slots = slots_of(prompt_ref)
    lane = lax.broadcasted_iota(jnp.int32, (HELD, HD), 1)
    row = lax.broadcasted_iota(jnp.int32, (HELD, HD), 0)
    tags = jnp.concatenate(
        [spread(slots, lane & 7).astype(jnp.float32), spread(slots, row).astype(jnp.float32)], axis=0
    ).astype(jnp.bfloat16)
    for step, send_ref in enumerate(send_refs):
        first = pl.multiple_of(((place & 3) ^ step) * RATIO * HD, RATIO * HD)
        mine = query_ref[:, pl.ds(first, RATIO * HD)].astype(jnp.float32)
        send_ref[:64] = jnp.concatenate(
            [mine[:, h * HD : (h + 1) * HD] for h in range(RATIO)], axis=0
        ).astype(jnp.bfloat16)
        send_ref[64:] = tags
    for copy in copies:
        copy.wait()


def sources_of(place_ref):
    return [(place_ref[0] & 3) ^ step for step in range(4)]


def pack_kernel(place_ref, *refs):
    got_refs = refs[:4]
    out_ref = refs[-1]
    sources = sources_of(place_ref)
    held = jnp.concatenate([got_ref[:64] for got_ref in got_refs], axis=0)
    tags = [got_ref[64:].astype(jnp.float32)[:1].astype(jnp.int32) for got_ref in got_refs]
    tags = [tags[s] + sources[s] * 512 for s in range(4)]
    half = lax.broadcasted_iota(jnp.int32, (1, HD), 1) < 64
    tag = jnp.concatenate([jnp.where(half, tags[0], tags[1]), jnp.where(half, tags[2], tags[3])], axis=1)
    lane_key = ((lax.broadcasted_iota(jnp.int32, (1, 256), 1) >> 3) & 7) * 64 + tag
    chunk = 512
    for start in range(0, ROWS, chunk):
        row = lax.broadcasted_iota(jnp.int32, (chunk, 1), 0) + start
        row_key = ((row >> 1) & 3) * 512 + ((row >> 3) & 7) * 64 + (row >> 6) * 2 + (row & 1)
        select = (row_key == lane_key).astype(jnp.float32).astype(jnp.bfloat16)
        out_ref[start : start + chunk, :] = jnp.dot(
            select, held, preferred_element_type=jnp.float32
        ).astype(jnp.bfloat16)


def near_kernel(
    len_ref, query_ref, new_key_ref, new_value_ref, key_ref, value_ref, out_ref, lse_ref, heads_ref
):
    step = pl.program_id(0)

    @pl.when(step == 0)
    def _():
        for h in range(HEADS):
            heads_ref[h] = query_ref[:, h * HD : (h + 1) * HD].astype(jnp.float32)

    length = len_ref[step]
    query = heads_ref[:, pl.ds(step, 1), :].reshape(HEADS, HD)
    keys = key_ref[0]
    values = value_ref[0]
    held_row = lax.broadcasted_iota(jnp.int32, (HELD, 1), 0)

    def row_of(ref):
        rows = jnp.where(held_row == step, ref[...].astype(jnp.float32), 0.0)
        return jnp.sum(rows, axis=0, keepdims=True)

    new_key = row_of(new_key_ref)
    new_value = row_of(new_value_ref)

    def spread_heads(row):
        return jnp.concatenate(
            [jnp.broadcast_to(row[:, k * HD : (k + 1) * HD], (RATIO, HD)) for k in range(KVH)], axis=0
        )

    scores = jnp.concatenate(
        [
            lax.dot_general(
                query.astype(jnp.bfloat16),
                keys[:, k * HD : (k + 1) * HD],
                (((1,), (1,)), ((), ())),
                preferred_element_type=jnp.float32,
            )[k * RATIO : (k + 1) * RATIO]
            for k in range(KVH)
        ],
        axis=0,
    ) * SCALE
    own = jnp.sum(query * spread_heads(new_key), axis=1, keepdims=True) * SCALE
    live = lax.broadcasted_iota(jnp.int32, (1, SUF), 1) < length
    scores = jnp.where(live, scores, NEG)
    top = jnp.maximum(jnp.max(scores, axis=1, keepdims=True), own)
    weights = jnp.where(live, jnp.exp(scores - top), 0.0)
    own_weight = jnp.exp(own - top)
    total = jnp.sum(weights, axis=1, keepdims=True) + own_weight
    rounded = weights.astype(jnp.bfloat16)
    mixed = jnp.concatenate(
        [
            jnp.dot(rounded, values[:, k * HD : (k + 1) * HD], preferred_element_type=jnp.float32)[
                k * RATIO : (k + 1) * RATIO
            ]
            for k in range(KVH)
        ],
        axis=0,
    )
    mixed = mixed + own_weight.astype(jnp.bfloat16).astype(jnp.float32) * spread_heads(new_value)
    out_ref[:, pl.ds(step, 1), :] = (mixed / total).reshape(HEADS, 1, HD)
    lse_ref[:, pl.ds(step, 1), :] = jnp.broadcast_to(top + jnp.log(total), (HEADS, HD)).reshape(
        HEADS, 1, HD
    )


def far_kernel(query_ref, *refs):
    pieces = refs[:16]
    out_ref, score_ref, query_scr, mixed_scr, stat_scr = refs[16:]
    span = 32
    block = span * RATIO
    tokens = 16 * PIECE
    queries = query_ref[...].astype(jnp.float32).reshape(32, RATIO, 8, HD)
    biggest = jnp.max(jnp.max(jnp.abs(queries), axis=1).reshape(SLOTS, HD), axis=1, keepdims=True)
    valid = (biggest > 0).astype(jnp.float32)
    row = lax.broadcasted_iota(jnp.int32, (SLOTS, SLOTS), 0)
    lane = lax.broadcasted_iota(jnp.int32, (SLOTS, SLOTS), 1)
    wide = jnp.broadcast_to(valid, (SLOTS, SLOTS)).astype(jnp.bfloat16)
    before = jnp.dot(
        (lane < row).astype(jnp.float32).astype(jnp.bfloat16), wide, preferred_element_type=jnp.float32
    )
    order = jnp.where(valid > 0, before, -1.0).astype(jnp.int32)
    gather = (order == lane).astype(jnp.float32).astype(jnp.bfloat16)
    count = jnp.sum(valid).astype(jnp.int32)
    for h in range(RATIO):
        query_scr[h] = lax.dot_general(
            gather,
            queries[:, h].reshape(SLOTS, HD).astype(jnp.bfloat16),
            (((0,), (0,)), ((), ())),
            preferred_element_type=jnp.float32,
        ).astype(jnp.bfloat16)
    mixed_scr[...] = jnp.zeros_like(mixed_scr)
    stat_scr[...] = jnp.zeros_like(stat_scr)

    @pl.loop(0, (count + span - 1) // span)
    def _(index):
        start = pl.multiple_of(index * span, span)
        query = query_scr[:, pl.ds(start, span), :].reshape(block, HD)
        peak = jnp.full((block, HD), -jnp.inf, jnp.float32)
        for n, piece in enumerate(pieces):
            scores = lax.dot_general(
                query, piece[0], (((1,), (1,)), ((), ())), preferred_element_type=jnp.float32
            )
            score_ref[n] = scores
            peak = jnp.maximum(peak, jnp.maximum(scores[:, :HD], scores[:, HD:]))
        peak = jnp.max(peak, axis=1, keepdims=True)
        total = jnp.zeros((block, HD), jnp.float32)
        mixed = jnp.zeros((block, HD), jnp.float32)
        for n, piece in enumerate(pieces):
            weights = jnp.exp2((score_ref[n] - peak) * (SCALE * LOG2E))
            total = total + (weights[:, :HD] + weights[:, HD:])
            mixed = mixed + jnp.dot(
                weights.astype(jnp.bfloat16), piece[1], preferred_element_type=jnp.float32
            )
        total = jnp.sum(total, axis=1, keepdims=True)
        mixed_scr[:, pl.ds(start, span), :] = (mixed / total).astype(jnp.bfloat16).reshape(RATIO, span, HD)
        lse = peak * SCALE + jnp.log(total)
        stat_scr[pl.ds(start, span), :] = split_stat(lse.reshape(RATIO, span, 1), span).astype(jnp.bfloat16)

    idle = 1.0 - valid
    mean = sum(piece[1].astype(jnp.float32).reshape(PIECE // 8, 8, HD).sum(axis=0) for piece in pieces)
    mean = jnp.sum(mean, axis=0, keepdims=True) / tokens
    heads = []
    for h in range(RATIO):
        spread_out = jnp.dot(gather, mixed_scr[h], preferred_element_type=jnp.float32) + idle * mean
        heads.append(spread_out.reshape(32, 8, HD))
    for h in range(0, RATIO, 2):
        out_ref[:, h * 8 : h * 8 + 16] = jnp.concatenate(heads[h : h + 2], axis=1).astype(jnp.bfloat16)
    even = split_stat(jnp.full((RATIO, SLOTS, 1), math.log(tokens), jnp.float32), SLOTS)
    stat = jnp.dot(gather, stat_scr[...], preferred_element_type=jnp.float32) + idle * even
    stat = stat.reshape(32, 8, HD)
    out_ref[:, 64:] = jnp.concatenate([stat, jnp.zeros_like(stat)], axis=1).astype(jnp.bfloat16)


def split_stat(lse, span):
    high = lse.astype(jnp.bfloat16).astype(jnp.float32)
    rest = lse - high
    middle = rest.astype(jnp.bfloat16).astype(jnp.float32)
    low = rest - middle
    lane = lax.broadcasted_iota(jnp.int32, (span, HD), 1)
    stat = jnp.zeros((span, HD), jnp.float32)
    for h in range(RATIO):
        for n, part in enumerate((high, middle, low)):
            stat = jnp.where(lane == n * 8 + h, part[h], stat)
    return stat


def select_kernel(place_ref, back_ref, *refs):
    got_refs = refs[:4]
    send_refs = refs[4:]
    sources = sources_of(place_ref)
    tags = [got_ref[64:].astype(jnp.float32)[8:, :1].astype(jnp.int32) for got_ref in got_refs]
    lane = lax.broadcasted_iota(jnp.int32, (1, ROWS), 1)
    lane_key = ((lane >> 1) & 3) * 512 + ((lane >> 3) & 7) * 64 + (lane >> 6) * 2 + (lane & 1)
    row_key = jnp.concatenate(
        [tags[s] + (sources[s] * 512 + h * 64) for s in range(4) for h in range(RATIO)], axis=0
    )
    select = (row_key == lane_key).astype(jnp.float32).astype(jnp.bfloat16)
    far = jnp.dot(select, back_ref[:, :64].reshape(ROWS, HD), preferred_element_type=jnp.float32)
    for s in range(4):
        send_refs[s][:64] = far[s * 64 : (s + 1) * 64].astype(jnp.bfloat16)
    stats = back_ref[:, 64:].astype(jnp.float32)[:, :8].reshape(SLOTS, HD).astype(jnp.bfloat16)
    lane = lax.broadcasted_iota(jnp.int32, (1, SLOTS), 1)
    lane_key = ((lane >> 1) & 3) * 64 + (lane >> 3) * 2 + (lane & 1)
    row_key = jnp.concatenate([tags[s] + sources[s] * 64 for s in range(4)], axis=0)
    select = (row_key == lane_key).astype(jnp.float32).astype(jnp.bfloat16)
    stat = jnp.dot(select, stats, preferred_element_type=jnp.float32)
    for s in range(4):
        mine = stat[s * 8 : (s + 1) * 8]
        send_refs[s][64:] = jnp.concatenate([mine, jnp.zeros_like(mine)], axis=0).astype(
            jnp.bfloat16
        )


def merge_kernel(place_ref, *refs):
    back_refs = refs[:4]
    near_ref, near_lse_ref, out_ref = refs[4:]
    lane = lax.broadcasted_iota(jnp.int32, (HELD, HD), 1)
    for source, back_ref in zip(sources_of(place_ref), back_refs):
        far = back_ref[:64].astype(jnp.float32)
        stat = jnp.where(lane < 24, back_ref[64:].astype(jnp.float32)[:8], 0.0)
        for h in range(RATIO):
            head = source * RATIO + h
            far_lse = jnp.sum(jnp.where((lane & 7) == h, stat, 0.0), axis=1, keepdims=True)
            near_lse = near_lse_ref[head]
            top = jnp.maximum(far_lse, near_lse)
            far_scale = jnp.exp(far_lse - top)
            near_scale = jnp.exp(near_lse - top)
            merged = far[h * 8 : (h + 1) * 8] * far_scale + near_ref[head] * near_scale
            out_ref[:, pl.ds(pl.multiple_of(head * HD, HD), HD)] = (
                merged / (far_scale + near_scale)
            ).astype(jnp.bfloat16)


VMEM = pl.BlockSpec(memory_space=pltpu.VMEM)
SMEM = pl.BlockSpec(memory_space=pltpu.SMEM)
ANY = pl.BlockSpec(memory_space=pl.ANY)


def params(mib):
    return pltpu.CompilerParams(vmem_limit_bytes=mib << 20)


def shards(
    prompt_of,
    suffix_len,
    query,
    new_key,
    new_value,
    suffix_key,
    suffix_value,
    prefix_key,
    prefix_value,
):
    place = lax.axis_index(NEAR).astype(jnp.int32).reshape(1)
    def along_y(pieces):
        moved = [lax.ppermute(pieces[step], "y", [(i, i ^ step) for i in range(4)]) for step in range(1, 4)]
        return [pieces[0]] + moved

    made = pl.pallas_call(
        prep_kernel,
        out_shape=[jax.ShapeDtypeStruct((80, HD), jnp.bfloat16)] * 4
        + [jax.ShapeDtypeStruct((2, PIECE, HD), jnp.bfloat16)] * 8,
        in_specs=[SMEM, ANY, ANY, ANY, ANY],
        out_specs=[VMEM] * 12,
        scratch_shapes=[
            pltpu.SMEM((HELD,), jnp.int32),
            pltpu.VMEM((HELD, HEADS * HD), jnp.bfloat16),
            pltpu.SemaphoreType.DMA((2,)),
            pltpu.SemaphoreType.DMA((8, 2)),
        ],
        compiler_params=params(12),
        name="prep",
    )(place, prompt_of, query, prefix_key, prefix_value)
    got = along_y(made[:4])
    cuts = made[4:]
    held = [cuts[0]]
    for step in range(1, 8):
        held.append(lax.ppermute(cuts[step], NEAR, [(i, i ^ step) for i in range(8)]))
    swapped = [lax.ppermute(piece, "c", [(0, 1), (1, 0)]) for piece in held]

    near_out, near_lse = pl.pallas_call(
        near_kernel,
        grid=(HELD,),
        out_shape=[jax.ShapeDtypeStruct((HEADS, HELD, HD), jnp.float32)] * 2,
        in_specs=[
            SMEM,
            pl.BlockSpec((HELD, HEADS * HD), lambda i: (0, 0)),
            pl.BlockSpec((HELD, KVH * HD), lambda i: (0, 0)),
            pl.BlockSpec((HELD, KVH * HD), lambda i: (0, 0)),
            pl.BlockSpec((1, SUF, KVH * HD), lambda i: (i, 0, 0)),
            pl.BlockSpec((1, SUF, KVH * HD), lambda i: (i, 0, 0)),
        ],
        out_specs=[pl.BlockSpec((HEADS, HELD, HD), lambda i: (0, 0, 0))] * 2,
        scratch_shapes=[pltpu.VMEM((HEADS, HELD, HD), jnp.float32)],
        compiler_params=params(12),
        cost_estimate=pl.CostEstimate(flops=300_000_000, bytes_accessed=4_500_000, transcendentals=65536),
        name="near",
    )(
        suffix_len,
        query,
        new_key,
        new_value,
        suffix_key,
        suffix_value,
    )

    first = held + swapped + [near_out, near_lse]
    outgoing = pl.pallas_call(
        pack_kernel,
        out_shape=jax.ShapeDtypeStruct((ROWS, HD), jnp.bfloat16),
        in_specs=[SMEM] + [VMEM] * 4 + [ANY] * len(first),
        out_specs=VMEM,
        compiler_params=params(8),
        name="pack",
    )(place, *got, *first)
    arrived = lax.all_to_all(outgoing.reshape(PROMPTS, 64, HD), FAR, 0, 0, tiled=True)

    parcel = pl.pallas_call(
        far_kernel,
        out_shape=jax.ShapeDtypeStruct((PROMPTS, 80, HD), jnp.bfloat16),
        in_specs=[VMEM] * 17,
        out_specs=VMEM,
        scratch_shapes=[
            pltpu.VMEM((16, 256, PIECE), jnp.float32),
            pltpu.VMEM((RATIO, SLOTS, HD), jnp.bfloat16),
            pltpu.VMEM((RATIO, SLOTS, HD), jnp.bfloat16),
            pltpu.VMEM((SLOTS, HD), jnp.bfloat16),
        ],
        compiler_params=params(16),
        name="far",
    )(arrived.reshape(ROWS, HD), *held, *swapped)
    back = lax.all_to_all(parcel, FAR, 0, 0, tiled=True)
    chosen = pl.pallas_call(
        select_kernel,
        out_shape=[jax.ShapeDtypeStruct((80, HD), jnp.bfloat16)] * 4,
        in_specs=[SMEM] + [VMEM] * 5,
        out_specs=[VMEM] * 4,
        compiler_params=params(8),
        name="select",
    )(place, back, *got)
    return pl.pallas_call(
        merge_kernel,
        out_shape=jax.ShapeDtypeStruct((HELD, HEADS * HD), jnp.bfloat16),
        in_specs=[SMEM] + [VMEM] * 6,
        out_specs=VMEM,
        compiler_params=params(12),
        name="merge",
    )(place, *along_y(chosen), near_out, near_lse)


def solution(mesh):
    fine = Mesh(mesh.devices.reshape(2, 8, 2, 4, 2), ALL)
    grp = ("xh", "z")
    blk = ("xl", "y", "c")
    in_specs = (
        P(ALL),
        P(ALL),
        P(ALL, None),
        P(ALL, None),
        P(ALL, None),
        P(ALL, None, None),
        P(ALL, None, None),
        P(grp, blk, None),
        P(grp, blk, None),
    )
    return jax.shard_map(
        shards, mesh=fine, in_specs=in_specs, out_specs=P(ALL, None), check_vma=False
    )
```

```python
import math

import jax
import jax.numpy as jnp
from jax import lax
from jax.experimental import pallas as pl
from jax.experimental.pallas import tpu as pltpu
from jax.sharding import Mesh, PartitionSpec as P

HD = 128
CAP = 2
HELD = 8
HEADS = 32
KVH = 4
RATIO = 8
PROMPTS = 32
SUF = 256
PIECE = 256
SLOTS = 256
ROWS = SLOTS * RATIO
NEG = -1e30
SCALE = HD ** (-0.5)
LOG2E = 1.4426950408889634
ALL = ("xh", "z", "xl", "y", "c")
NEAR = ("xl", "y")
FAR = ("xh", "z", "xl")


def slots_of(prompt_ref):
    prompts = [prompt_ref[i] for i in range(HELD)]
    slots = []
    for i in range(HELD):
        rank = jnp.int32(0)
        for j in range(i):
            rank = rank + jnp.where(prompts[j] == prompts[i], 1, 0)
        slots.append(prompts[i] * CAP + rank)
    return slots


def spread(values, index):
    picked = jnp.zeros(index.shape, jnp.int32)
    for i, value in enumerate(values):
        picked = jnp.where(index == i, value, picked)
    return picked


def prep_kernel(place_ref, prompt_hbm, query_hbm, key_ref, value_ref, *refs):
    send_refs = refs[:4]
    cut_refs = refs[4:12]
    prompt_ref, query_ref, small_sem, cut_sem = refs[12:]
    small = [
        pltpu.make_async_copy(prompt_hbm, prompt_ref, small_sem.at[0]),
        pltpu.make_async_copy(query_hbm, query_ref, small_sem.at[1]),
    ]
    for copy in small:
        copy.start()
    place = place_ref[0]
    copies = []
    for step, cut_ref in enumerate(cut_refs):
        target = place ^ step
        prompt = target >> 2
        column = pl.multiple_of((target & 3) * HD, HD)
        for n, cache in enumerate((key_ref, value_ref)):
            copies.append(
                pltpu.make_async_copy(
                    cache.at[prompt, :, pl.ds(column, HD)], cut_ref.at[n], cut_sem.at[step, n]
                )
            )
            copies[-1].start()
    for copy in small:
        copy.wait()
    slots = slots_of(prompt_ref)
    lane = lax.broadcasted_iota(jnp.int32, (HELD, HD), 1)
    row = lax.broadcasted_iota(jnp.int32, (HELD, HD), 0)
    tags = jnp.concatenate(
        [spread(slots, lane & 7).astype(jnp.float32), spread(slots, row).astype(jnp.float32)], axis=0
    ).astype(jnp.bfloat16)
    for step, send_ref in enumerate(send_refs):
        first = pl.multiple_of(((place & 3) ^ step) * RATIO * HD, RATIO * HD)
        mine = query_ref[:, pl.ds(first, RATIO * HD)].astype(jnp.float32)
        send_ref[:64] = jnp.concatenate(
            [mine[:, h * HD : (h + 1) * HD] for h in range(RATIO)], axis=0
        ).astype(jnp.bfloat16)
        send_ref[64:] = tags
    for copy in copies:
        copy.wait()


def sources_of(place_ref):
    return [(place_ref[0] & 3) ^ step for step in range(4)]


def pack_kernel(place_ref, *refs):
    got_refs = refs[:4]
    out_ref = refs[-1]
    sources = sources_of(place_ref)
    held = jnp.concatenate([got_ref[:64] for got_ref in got_refs], axis=0)
    tags = [got_ref[64:].astype(jnp.float32)[:1].astype(jnp.int32) for got_ref in got_refs]
    tags = [tags[s] + sources[s] * 512 for s in range(4)]
    half = lax.broadcasted_iota(jnp.int32, (1, HD), 1) < 64
    tag = jnp.concatenate([jnp.where(half, tags[0], tags[1]), jnp.where(half, tags[2], tags[3])], axis=1)
    lane_key = ((lax.broadcasted_iota(jnp.int32, (1, 256), 1) >> 3) & 7) * 64 + tag
    chunk = 512
    for start in range(0, ROWS, chunk):
        row = lax.broadcasted_iota(jnp.int32, (chunk, 1), 0) + start
        row_key = ((row >> 1) & 3) * 512 + ((row >> 3) & 7) * 64 + (row >> 6) * 2 + (row & 1)
        select = (row_key == lane_key).astype(jnp.float32).astype(jnp.bfloat16)
        out_ref[start : start + chunk, :] = jnp.dot(
            select, held, preferred_element_type=jnp.float32
        ).astype(jnp.bfloat16)


def near_kernel(
    len_ref, query_ref, new_key_ref, new_value_ref, key_ref, value_ref, out_ref, lse_ref, heads_ref
):
    step = pl.program_id(0)

    @pl.when(step == 0)
    def _():
        for h in range(HEADS):
            heads_ref[h] = query_ref[:, h * HD : (h + 1) * HD].astype(jnp.float32)

    length = len_ref[step]
    query = heads_ref[:, pl.ds(step, 1), :].reshape(HEADS, HD)
    keys = key_ref[0]
    values = value_ref[0]
    held_row = lax.broadcasted_iota(jnp.int32, (HELD, 1), 0)

    def row_of(ref):
        rows = jnp.where(held_row == step, ref[...].astype(jnp.float32), 0.0)
        return jnp.sum(rows, axis=0, keepdims=True)

    new_key = row_of(new_key_ref)
    new_value = row_of(new_value_ref)

    def spread_heads(row):
        return jnp.concatenate(
            [jnp.broadcast_to(row[:, k * HD : (k + 1) * HD], (RATIO, HD)) for k in range(KVH)], axis=0
        )

    scores = jnp.concatenate(
        [
            lax.dot_general(
                query.astype(jnp.bfloat16),
                keys[:, k * HD : (k + 1) * HD],
                (((1,), (1,)), ((), ())),
                preferred_element_type=jnp.float32,
            )[k * RATIO : (k + 1) * RATIO]
            for k in range(KVH)
        ],
        axis=0,
    ) * SCALE
    own = jnp.sum(query * spread_heads(new_key), axis=1, keepdims=True) * SCALE
    live = lax.broadcasted_iota(jnp.int32, (1, SUF), 1) < length
    scores = jnp.where(live, scores, NEG)
    top = jnp.maximum(jnp.max(scores, axis=1, keepdims=True), own)
    weights = jnp.where(live, jnp.exp(scores - top), 0.0)
    own_weight = jnp.exp(own - top)
    total = jnp.sum(weights, axis=1, keepdims=True) + own_weight
    rounded = weights.astype(jnp.bfloat16)
    mixed = jnp.concatenate(
        [
            jnp.dot(rounded, values[:, k * HD : (k + 1) * HD], preferred_element_type=jnp.float32)[
                k * RATIO : (k + 1) * RATIO
            ]
            for k in range(KVH)
        ],
        axis=0,
    )
    mixed = mixed + own_weight.astype(jnp.bfloat16).astype(jnp.float32) * spread_heads(new_value)
    out_ref[:, pl.ds(step, 1), :] = (mixed / total).reshape(HEADS, 1, HD)
    lse_ref[:, pl.ds(step, 1), :] = jnp.broadcast_to(top + jnp.log(total), (HEADS, HD)).reshape(
        HEADS, 1, HD
    )


def far_kernel(query_ref, *refs):
    sources = refs[:16]
    out_ref, score_ref, query_scr, mixed_scr, stat_scr, cache_ref, sems = refs[16:]
    copies = [
        [pltpu.make_async_copy(source.at[k], cache_ref.at[n, k], sems.at[n, k]) for n, source in enumerate(sources)]
        for k in range(2)
    ]
    for copy in copies[0] + copies[1]:
        copy.start()
    pieces = [cache_ref.at[n] for n in range(16)]
    span = 32
    block = span * RATIO
    tokens = 16 * PIECE
    queries = query_ref[...].astype(jnp.float32).reshape(32, RATIO, 8, HD)
    biggest = jnp.max(jnp.max(jnp.abs(queries), axis=1).reshape(SLOTS, HD), axis=1, keepdims=True)
    valid = (biggest > 0).astype(jnp.float32)
    row = lax.broadcasted_iota(jnp.int32, (SLOTS, SLOTS), 0)
    lane = lax.broadcasted_iota(jnp.int32, (SLOTS, SLOTS), 1)
    wide = jnp.broadcast_to(valid, (SLOTS, SLOTS)).astype(jnp.bfloat16)
    before = jnp.dot(
        (lane < row).astype(jnp.float32).astype(jnp.bfloat16), wide, preferred_element_type=jnp.float32
    )
    order = jnp.where(valid > 0, before, -1.0).astype(jnp.int32)
    gather = (order == lane).astype(jnp.float32).astype(jnp.bfloat16)
    count = jnp.sum(valid).astype(jnp.int32)
    for h in range(RATIO):
        query_scr[h] = lax.dot_general(
            gather,
            queries[:, h].reshape(SLOTS, HD).astype(jnp.bfloat16),
            (((0,), (0,)), ((), ())),
            preferred_element_type=jnp.float32,
        ).astype(jnp.bfloat16)
    mixed_scr[...] = jnp.zeros_like(mixed_scr)
    stat_scr[...] = jnp.zeros_like(stat_scr)
    for copy in copies[0]:
        copy.wait()

    @pl.loop(0, (count + span - 1) // span)
    def _(index):
        start = pl.multiple_of(index * span, span)
        query = query_scr[:, pl.ds(start, span), :].reshape(block, HD)
        peak = jnp.full((block, HD), -jnp.inf, jnp.float32)
        for n, piece in enumerate(pieces):
            scores = lax.dot_general(
                query, piece[0], (((1,), (1,)), ((), ())), preferred_element_type=jnp.float32
            )
            score_ref[n] = scores
            peak = jnp.maximum(peak, jnp.maximum(scores[:, :HD], scores[:, HD:]))
        peak = jnp.max(peak, axis=1, keepdims=True)

        @pl.when(index == 0)
        def _():
            for copy in copies[1]:
                copy.wait()

        total = jnp.zeros((block, HD), jnp.float32)
        mixed = jnp.zeros((block, HD), jnp.float32)
        for n, piece in enumerate(pieces):
            weights = jnp.exp2((score_ref[n] - peak) * (SCALE * LOG2E))
            total = total + (weights[:, :HD] + weights[:, HD:])
            mixed = mixed + jnp.dot(
                weights.astype(jnp.bfloat16), piece[1], preferred_element_type=jnp.float32
            )
        total = jnp.sum(total, axis=1, keepdims=True)
        mixed_scr[:, pl.ds(start, span), :] = (mixed / total).astype(jnp.bfloat16).reshape(RATIO, span, HD)
        lse = peak * SCALE + jnp.log(total)
        stat_scr[pl.ds(start, span), :] = split_stat(lse.reshape(RATIO, span, 1), span).astype(jnp.bfloat16)

    @pl.when(count == 0)
    def _():
        for copy in copies[1]:
            copy.wait()

    idle = 1.0 - valid
    mean = sum(piece[1].astype(jnp.float32).reshape(PIECE // 8, 8, HD).sum(axis=0) for piece in pieces)
    mean = jnp.sum(mean, axis=0, keepdims=True) / tokens
    heads = []
    for h in range(RATIO):
        spread_out = jnp.dot(gather, mixed_scr[h], preferred_element_type=jnp.float32) + idle * mean
        heads.append(spread_out.reshape(32, 8, HD))
    for h in range(0, RATIO, 2):
        out_ref[:, h * 8 : h * 8 + 16] = jnp.concatenate(heads[h : h + 2], axis=1).astype(jnp.bfloat16)
    even = split_stat(jnp.full((RATIO, SLOTS, 1), math.log(tokens), jnp.float32), SLOTS)
    stat = jnp.dot(gather, stat_scr[...], preferred_element_type=jnp.float32) + idle * even
    stat = stat.reshape(32, 8, HD)
    out_ref[:, 64:] = jnp.concatenate([stat, jnp.zeros_like(stat)], axis=1).astype(jnp.bfloat16)


def split_stat(lse, span):
    high = lse.astype(jnp.bfloat16).astype(jnp.float32)
    rest = lse - high
    middle = rest.astype(jnp.bfloat16).astype(jnp.float32)
    low = rest - middle
    lane = lax.broadcasted_iota(jnp.int32, (span, HD), 1)
    stat = jnp.zeros((span, HD), jnp.float32)
    for h in range(RATIO):
        for n, part in enumerate((high, middle, low)):
            stat = jnp.where(lane == n * 8 + h, part[h], stat)
    return stat


def select_kernel(place_ref, back_ref, *refs):
    got_refs = refs[:4]
    send_refs = refs[-4:]
    sources = sources_of(place_ref)
    tags = [got_ref[64:].astype(jnp.float32)[8:, :1].astype(jnp.int32) for got_ref in got_refs]
    lane = lax.broadcasted_iota(jnp.int32, (1, ROWS), 1)
    lane_key = ((lane >> 1) & 3) * 512 + ((lane >> 3) & 7) * 64 + (lane >> 6) * 2 + (lane & 1)
    row_key = jnp.concatenate(
        [tags[s] + (sources[s] * 512 + h * 64) for s in range(4) for h in range(RATIO)], axis=0
    )
    select = (row_key == lane_key).astype(jnp.float32).astype(jnp.bfloat16)
    far = jnp.dot(select, back_ref[:, :64].reshape(ROWS, HD), preferred_element_type=jnp.float32)
    for s in range(4):
        send_refs[s][:64] = far[s * 64 : (s + 1) * 64].astype(jnp.bfloat16)
    stats = back_ref[:, 64:].astype(jnp.float32)[:, :8].reshape(SLOTS, HD).astype(jnp.bfloat16)
    lane = lax.broadcasted_iota(jnp.int32, (1, SLOTS), 1)
    lane_key = ((lane >> 1) & 3) * 64 + (lane >> 3) * 2 + (lane & 1)
    row_key = jnp.concatenate([tags[s] + sources[s] * 64 for s in range(4)], axis=0)
    select = (row_key == lane_key).astype(jnp.float32).astype(jnp.bfloat16)
    stat = jnp.dot(select, stats, preferred_element_type=jnp.float32)
    for s in range(4):
        mine = stat[s * 8 : (s + 1) * 8]
        send_refs[s][64:] = jnp.concatenate([mine, jnp.zeros_like(mine)], axis=0).astype(
            jnp.bfloat16
        )


def merge_kernel(place_ref, *refs):
    back_refs = refs[:4]
    near_ref, near_lse_ref, out_ref = refs[4:]
    lane = lax.broadcasted_iota(jnp.int32, (HELD, HD), 1)
    for source, back_ref in zip(sources_of(place_ref), back_refs):
        far = back_ref[:64].astype(jnp.float32)
        stat = jnp.where(lane < 24, back_ref[64:].astype(jnp.float32)[:8], 0.0)
        for h in range(RATIO):
            head = source * RATIO + h
            far_lse = jnp.sum(jnp.where((lane & 7) == h, stat, 0.0), axis=1, keepdims=True)
            near_lse = near_lse_ref[head]
            top = jnp.maximum(far_lse, near_lse)
            far_scale = jnp.exp(far_lse - top)
            near_scale = jnp.exp(near_lse - top)
            merged = far[h * 8 : (h + 1) * 8] * far_scale + near_ref[head] * near_scale
            out_ref[:, pl.ds(pl.multiple_of(head * HD, HD), HD)] = (
                merged / (far_scale + near_scale)
            ).astype(jnp.bfloat16)


VMEM = pl.BlockSpec(memory_space=pltpu.VMEM)
SMEM = pl.BlockSpec(memory_space=pltpu.SMEM)
ANY = pl.BlockSpec(memory_space=pl.ANY)


def params(mib):
    return pltpu.CompilerParams(vmem_limit_bytes=mib << 20)


def shards(
    prompt_of,
    suffix_len,
    query,
    new_key,
    new_value,
    suffix_key,
    suffix_value,
    prefix_key,
    prefix_value,
):
    place = lax.axis_index(NEAR).astype(jnp.int32).reshape(1)
    def along_y(pieces):
        moved = [lax.ppermute(pieces[step], "y", [(i, i ^ step) for i in range(4)]) for step in range(1, 4)]
        return [pieces[0]] + moved

    made = pl.pallas_call(
        prep_kernel,
        out_shape=[jax.ShapeDtypeStruct((80, HD), jnp.bfloat16)] * 4
        + [jax.ShapeDtypeStruct((2, PIECE, HD), jnp.bfloat16)] * 8,
        in_specs=[SMEM, ANY, ANY, ANY, ANY],
        out_specs=[VMEM] * 12,
        scratch_shapes=[
            pltpu.SMEM((HELD,), jnp.int32),
            pltpu.VMEM((HELD, HEADS * HD), jnp.bfloat16),
            pltpu.SemaphoreType.DMA((2,)),
            pltpu.SemaphoreType.DMA((8, 2)),
        ],
        compiler_params=params(60),
        name="prep",
    )(place, prompt_of, query, prefix_key, prefix_value)
    got = along_y(made[:4])
    cuts = made[4:]
    held = [cuts[0]]
    for step in range(1, 8):
        held.append(lax.ppermute(cuts[step], NEAR, [(i, i ^ step) for i in range(8)]))
    swapped = [lax.ppermute(piece, "c", [(0, 1), (1, 0)]) for piece in held]

    near_out, near_lse = pl.pallas_call(
        near_kernel,
        grid=(HELD,),
        out_shape=[jax.ShapeDtypeStruct((HEADS, HELD, HD), jnp.float32)] * 2,
        in_specs=[
            SMEM,
            pl.BlockSpec((HELD, HEADS * HD), lambda i: (0, 0)),
            pl.BlockSpec((HELD, KVH * HD), lambda i: (0, 0)),
            pl.BlockSpec((HELD, KVH * HD), lambda i: (0, 0)),
            pl.BlockSpec((1, SUF, KVH * HD), lambda i: (i, 0, 0)),
            pl.BlockSpec((1, SUF, KVH * HD), lambda i: (i, 0, 0)),
        ],
        out_specs=[pl.BlockSpec((HEADS, HELD, HD), lambda i: (0, 0, 0))] * 2,
        scratch_shapes=[pltpu.VMEM((HEADS, HELD, HD), jnp.float32)],
        compiler_params=params(12),
        cost_estimate=pl.CostEstimate(flops=300_000_000, bytes_accessed=4_500_000, transcendentals=65536),
        name="near",
    )(
        suffix_len,
        query,
        new_key,
        new_value,
        suffix_key,
        suffix_value,
    )

    first = held[4:]
    outgoing = pl.pallas_call(
        pack_kernel,
        out_shape=jax.ShapeDtypeStruct((ROWS, HD), jnp.bfloat16),
        in_specs=[SMEM] + [VMEM] * 4 + [ANY] * len(first),
        out_specs=VMEM,
        compiler_params=params(8),
        name="pack",
    )(place, *got, *first)
    arrived = lax.all_to_all(outgoing.reshape(PROMPTS, 64, HD), FAR, 0, 0, tiled=True)

    parcel = pl.pallas_call(
        far_kernel,
        out_shape=jax.ShapeDtypeStruct((PROMPTS, 80, HD), jnp.bfloat16),
        in_specs=[VMEM] + [ANY] * 16,
        out_specs=VMEM,
        scratch_shapes=[
            pltpu.VMEM((16, 256, PIECE), jnp.float32),
            pltpu.VMEM((RATIO, SLOTS, HD), jnp.bfloat16),
            pltpu.VMEM((RATIO, SLOTS, HD), jnp.bfloat16),
            pltpu.VMEM((SLOTS, HD), jnp.bfloat16),
            pltpu.VMEM((16, 2, PIECE, HD), jnp.bfloat16),
            pltpu.SemaphoreType.DMA((16, 2)),
        ],
        compiler_params=params(60),
        name="far",
    )(arrived.reshape(ROWS, HD), *held, *swapped)
    back = lax.all_to_all(parcel, FAR, 0, 0, tiled=True)
    chosen = pl.pallas_call(
        select_kernel,
        out_shape=[jax.ShapeDtypeStruct((80, HD), jnp.bfloat16)] * 4,
        in_specs=[SMEM] + [VMEM] * 5 + [ANY] * 2,
        out_specs=[VMEM] * 4,
        compiler_params=params(8),
        name="select",
    )(place, back, *got, near_out, near_lse)
    return pl.pallas_call(
        merge_kernel,
        out_shape=jax.ShapeDtypeStruct((HELD, HEADS * HD), jnp.bfloat16),
        in_specs=[SMEM] + [VMEM] * 6,
        out_specs=VMEM,
        compiler_params=params(12),
        name="merge",
    )(place, *along_y(chosen), near_out, near_lse)


def solution(mesh):
    fine = Mesh(mesh.devices.reshape(2, 8, 2, 4, 2), ALL)
    grp = ("xh", "z")
    blk = ("xl", "y", "c")
    in_specs = (
        P(ALL),
        P(ALL),
        P(ALL, None),
        P(ALL, None),
        P(ALL, None),
        P(ALL, None, None),
        P(ALL, None, None),
        P(grp, blk, None),
        P(grp, blk, None),
    )
    return jax.shard_map(
        shards, mesh=fine, in_specs=in_specs, out_specs=P(ALL, None), check_vma=False
    )
```

```python
import math

import jax
import jax.numpy as jnp
from jax import lax
from jax.experimental import pallas as pl
from jax.experimental.pallas import tpu as pltpu
from jax.sharding import Mesh, PartitionSpec as P

HD = 128
CAP = 2
HELD = 8
HEADS = 32
KVH = 4
RATIO = 8
PROMPTS = 32
SUF = 256
PIECE = 256
SLOTS = 256
ROWS = SLOTS * RATIO
NEG = -1e30
SCALE = HD ** (-0.5)
LOG2E = 1.4426950408889634
ALL = ("xh", "z", "xl", "y", "c")
NEAR = ("xl", "y")
FAR = ("xh", "z", "xl")


def slots_of(prompt_ref):
    prompts = [prompt_ref[i] for i in range(HELD)]
    slots = []
    for i in range(HELD):
        rank = jnp.int32(0)
        for j in range(i):
            rank = rank + jnp.where(prompts[j] == prompts[i], 1, 0)
        slots.append(prompts[i] * CAP + rank)
    return slots


def spread(values, index):
    picked = jnp.zeros(index.shape, jnp.int32)
    for i, value in enumerate(values):
        picked = jnp.where(index == i, value, picked)
    return picked


def prep_kernel(place_ref, prompt_hbm, query_hbm, key_ref, value_ref, send_ref, *refs):
    cut_refs = refs[:8]
    prompt_ref, query_ref, small_sem, cut_sem = refs[8:]
    small = [
        pltpu.make_async_copy(prompt_hbm, prompt_ref, small_sem.at[0]),
        pltpu.make_async_copy(query_hbm, query_ref, small_sem.at[1]),
    ]
    for copy in small:
        copy.start()
    place = place_ref[0]
    copies = []
    for step, cut_ref in enumerate(cut_refs):
        target = place ^ step
        prompt = target >> 2
        column = pl.multiple_of((target & 3) * HD, HD)
        for n, cache in enumerate((key_ref, value_ref)):
            copies.append(
                pltpu.make_async_copy(
                    cache.at[prompt, :, pl.ds(column, HD)], cut_ref.at[n], cut_sem.at[step, n]
                )
            )
            copies[-1].start()
    for copy in small:
        copy.wait()
    slots = slots_of(prompt_ref)
    lane = lax.broadcasted_iota(jnp.int32, (HELD, HD), 1)
    row = lax.broadcasted_iota(jnp.int32, (HELD, HD), 0)
    tags = jnp.concatenate(
        [spread(slots, lane & 7).astype(jnp.float32), spread(slots, row).astype(jnp.float32)], axis=0
    ).astype(jnp.bfloat16)
    for y in range(KVH):
        send_ref[y, :64] = jnp.concatenate(
            [
                query_ref[:, h * HD : (h + 1) * HD].astype(jnp.float32)
                for h in range(y * RATIO, (y + 1) * RATIO)
            ],
            axis=0,
        ).astype(jnp.bfloat16)
        send_ref[y, 64:] = tags
    for copy in copies:
        copy.wait()


def pack_kernel(got_ref, *refs):
    out_ref = refs[-1]
    held = got_ref[:, :64].reshape(256, HD)
    tags = [got_ref[y, 64:].astype(jnp.float32)[:1].astype(jnp.int32) for y in range(KVH)]
    half = lax.broadcasted_iota(jnp.int32, (1, HD), 1) < 64
    tag = jnp.concatenate([jnp.where(half, tags[0], tags[1]), jnp.where(half, tags[2], tags[3])], axis=1)
    lane_key = (lax.broadcasted_iota(jnp.int32, (1, 256), 1) >> 3) * 64 + tag
    chunk = 512
    for start in range(0, ROWS, chunk):
        row = lax.broadcasted_iota(jnp.int32, (chunk, 1), 0) + start
        row_key = ((row >> 1) & 3) * 512 + ((row >> 3) & 7) * 64 + (row >> 6) * 2 + (row & 1)
        select = (row_key == lane_key).astype(jnp.float32).astype(jnp.bfloat16)
        out_ref[start : start + chunk, :] = jnp.dot(
            select, held, preferred_element_type=jnp.float32
        ).astype(jnp.bfloat16)


def near_kernel(
    len_ref, query_ref, new_key_ref, new_value_ref, key_ref, value_ref, out_ref, lse_ref, heads_ref
):
    step = pl.program_id(0)

    @pl.when(step == 0)
    def _():
        for h in range(HEADS):
            heads_ref[h] = query_ref[:, h * HD : (h + 1) * HD].astype(jnp.float32)

    length = len_ref[step]
    query = heads_ref[:, pl.ds(step, 1), :].reshape(HEADS, HD)
    keys = key_ref[0]
    values = value_ref[0]
    held_row = lax.broadcasted_iota(jnp.int32, (HELD, 1), 0)

    def row_of(ref):
        rows = jnp.where(held_row == step, ref[...].astype(jnp.float32), 0.0)
        return jnp.sum(rows, axis=0, keepdims=True)

    new_key = row_of(new_key_ref)
    new_value = row_of(new_value_ref)

    def spread_heads(row):
        return jnp.concatenate(
            [jnp.broadcast_to(row[:, k * HD : (k + 1) * HD], (RATIO, HD)) for k in range(KVH)], axis=0
        )

    scores = jnp.concatenate(
        [
            lax.dot_general(
                query.astype(jnp.bfloat16),
                keys[:, k * HD : (k + 1) * HD],
                (((1,), (1,)), ((), ())),
                preferred_element_type=jnp.float32,
            )[k * RATIO : (k + 1) * RATIO]
            for k in range(KVH)
        ],
        axis=0,
    ) * SCALE
    own = jnp.sum(query * spread_heads(new_key), axis=1, keepdims=True) * SCALE
    live = lax.broadcasted_iota(jnp.int32, (1, SUF), 1) < length
    scores = jnp.where(live, scores, NEG)
    top = jnp.maximum(jnp.max(scores, axis=1, keepdims=True), own)
    weights = jnp.where(live, jnp.exp(scores - top), 0.0)
    own_weight = jnp.exp(own - top)
    total = jnp.sum(weights, axis=1, keepdims=True) + own_weight
    rounded = weights.astype(jnp.bfloat16)
    mixed = jnp.concatenate(
        [
            jnp.dot(rounded, values[:, k * HD : (k + 1) * HD], preferred_element_type=jnp.float32)[
                k * RATIO : (k + 1) * RATIO
            ]
            for k in range(KVH)
        ],
        axis=0,
    )
    mixed = mixed + own_weight.astype(jnp.bfloat16).astype(jnp.float32) * spread_heads(new_value)
    out_ref[:, pl.ds(step, 1), :] = (mixed / total).reshape(HEADS, 1, HD)
    lse_ref[:, pl.ds(step, 1), :] = jnp.broadcast_to(top + jnp.log(total), (HEADS, HD)).reshape(
        HEADS, 1, HD
    )


def far_kernel(query_ref, *refs):
    sources = refs[:16]
    out_ref, score_ref, query_scr, mixed_scr, stat_scr, cache_ref, sems = refs[16:]
    copies = [
        [
            pltpu.make_async_copy(source.at[k], cache_ref.at[n, k], sems.at[n, k])
            for n, source in enumerate(sources)
        ]
        for k in range(2)
    ]
    for copy in copies[0] + copies[1]:
        copy.start()
    pieces = [cache_ref.at[n] for n in range(16)]
    span = 32
    block = span * RATIO
    tokens = 16 * PIECE
    queries = query_ref[...].astype(jnp.float32).reshape(32, RATIO, 8, HD)
    biggest = jnp.max(jnp.max(jnp.abs(queries), axis=1).reshape(SLOTS, HD), axis=1, keepdims=True)
    valid = (biggest > 0).astype(jnp.float32)
    row = lax.broadcasted_iota(jnp.int32, (SLOTS, SLOTS), 0)
    lane = lax.broadcasted_iota(jnp.int32, (SLOTS, SLOTS), 1)
    wide = jnp.broadcast_to(valid, (SLOTS, SLOTS)).astype(jnp.bfloat16)
    before = jnp.dot(
        (lane < row).astype(jnp.float32).astype(jnp.bfloat16), wide, preferred_element_type=jnp.float32
    )
    order = jnp.where(valid > 0, before, -1.0).astype(jnp.int32)
    gather = (order == lane).astype(jnp.float32).astype(jnp.bfloat16)
    count = jnp.sum(valid).astype(jnp.int32)
    for h in range(RATIO):
        query_scr[h] = lax.dot_general(
            gather,
            queries[:, h].reshape(SLOTS, HD).astype(jnp.bfloat16),
            (((0,), (0,)), ((), ())),
            preferred_element_type=jnp.float32,
        ).astype(jnp.bfloat16)
    mixed_scr[...] = jnp.zeros_like(mixed_scr)
    stat_scr[...] = jnp.zeros_like(stat_scr)
    for copy in copies[0]:
        copy.wait()

    @pl.loop(0, (count + span - 1) // span)
    def _(index):
        start = pl.multiple_of(index * span, span)
        query = query_scr[:, pl.ds(start, span), :].reshape(block, HD)
        peak = jnp.full((block, HD), -jnp.inf, jnp.float32)
        for n, piece in enumerate(pieces):
            scores = lax.dot_general(
                query, piece[0], (((1,), (1,)), ((), ())), preferred_element_type=jnp.float32
            )
            score_ref[n] = scores
            peak = jnp.maximum(peak, jnp.maximum(scores[:, :HD], scores[:, HD:]))
        peak = jnp.max(peak, axis=1, keepdims=True)

        @pl.when(index == 0)
        def _():
            for copy in copies[1]:
                copy.wait()

        total = jnp.zeros((block, HD), jnp.float32)
        mixed = jnp.zeros((block, HD), jnp.float32)
        for n, piece in enumerate(pieces):
            weights = jnp.exp2((score_ref[n] - peak) * (SCALE * LOG2E))
            total = total + (weights[:, :HD] + weights[:, HD:])
            mixed = mixed + jnp.dot(
                weights.astype(jnp.bfloat16), piece[1], preferred_element_type=jnp.float32
            )
        total = jnp.sum(total, axis=1, keepdims=True)
        mixed_scr[:, pl.ds(start, span), :] = (mixed / total).astype(jnp.bfloat16).reshape(RATIO, span, HD)
        lse = peak * SCALE + jnp.log(total)
        stat_scr[pl.ds(start, span), :] = split_stat(lse.reshape(RATIO, span, 1), span).astype(jnp.bfloat16)

    @pl.when(count == 0)
    def _():
        for copy in copies[1]:
            copy.wait()

    idle = 1.0 - valid
    mean = sum(piece[1].astype(jnp.float32).reshape(PIECE // 8, 8, HD).sum(axis=0) for piece in pieces)
    mean = jnp.sum(mean, axis=0, keepdims=True) / tokens
    heads = []
    for h in range(RATIO):
        spread_out = jnp.dot(gather, mixed_scr[h], preferred_element_type=jnp.float32) + idle * mean
        heads.append(spread_out.reshape(32, 8, HD))
    for h in range(0, RATIO, 2):
        out_ref[:, h * 8 : h * 8 + 16] = jnp.concatenate(heads[h : h + 2], axis=1).astype(jnp.bfloat16)
    even = split_stat(jnp.full((RATIO, SLOTS, 1), math.log(tokens), jnp.float32), SLOTS)
    stat = jnp.dot(gather, stat_scr[...], preferred_element_type=jnp.float32) + idle * even
    stat = stat.reshape(32, 8, HD)
    out_ref[:, 64:] = jnp.concatenate([stat, jnp.zeros_like(stat)], axis=1).astype(jnp.bfloat16)


def split_stat(lse, span):
    high = lse.astype(jnp.bfloat16).astype(jnp.float32)
    rest = lse - high
    middle = rest.astype(jnp.bfloat16).astype(jnp.float32)
    low = rest - middle
    lane = lax.broadcasted_iota(jnp.int32, (span, HD), 1)
    stat = jnp.zeros((span, HD), jnp.float32)
    for h in range(RATIO):
        for n, part in enumerate((high, middle, low)):
            stat = jnp.where(lane == n * 8 + h, part[h], stat)
    return stat


def select_kernel(got_ref, back_ref, *refs):
    send_ref = refs[-1]
    tags = [got_ref[y, 64:].astype(jnp.float32)[8:, :1].astype(jnp.int32) for y in range(KVH)]
    lane = lax.broadcasted_iota(jnp.int32, (1, ROWS), 1)
    lane_key = ((lane >> 1) & 3) * 512 + ((lane >> 3) & 7) * 64 + (lane >> 6) * 2 + (lane & 1)
    tag = jnp.concatenate([tags[y] for y in range(KVH) for _ in range(RATIO)], axis=0)
    row_key = (lax.broadcasted_iota(jnp.int32, (256, 1), 0) >> 3) * 64 + tag
    select = (row_key == lane_key).astype(jnp.float32).astype(jnp.bfloat16)
    far = jnp.dot(select, back_ref[:, :64].reshape(ROWS, HD), preferred_element_type=jnp.float32)
    send_ref[:, :64] = far.astype(jnp.bfloat16).reshape(KVH, 64, HD)
    stats = back_ref[:, 64:].astype(jnp.float32)[:, :8].reshape(SLOTS, HD).astype(jnp.bfloat16)
    lane = lax.broadcasted_iota(jnp.int32, (1, SLOTS), 1)
    lane_key = ((lane >> 1) & 3) * 64 + (lane >> 3) * 2 + (lane & 1)
    row_key = (lax.broadcasted_iota(jnp.int32, (32, 1), 0) >> 3) * 64 + jnp.concatenate(tags, axis=0)
    select = (row_key == lane_key).astype(jnp.float32).astype(jnp.bfloat16)
    stat = jnp.dot(select, stats, preferred_element_type=jnp.float32).reshape(KVH, 8, HD)
    send_ref[:, 64:] = jnp.concatenate([stat, jnp.zeros_like(stat)], axis=1).astype(jnp.bfloat16)


def merge_kernel(back_ref, near_ref, near_lse_ref, out_ref):
    lane = lax.broadcasted_iota(jnp.int32, (HELD, HD), 1)
    for y in range(KVH):
        far = back_ref[y, :64].astype(jnp.float32)
        stat = jnp.where(lane < 24, back_ref[y, 64:].astype(jnp.float32)[:8], 0.0)
        for h in range(RATIO):
            head = y * RATIO + h
            far_lse = jnp.sum(jnp.where((lane & 7) == h, stat, 0.0), axis=1, keepdims=True)
            near_lse = near_lse_ref[head]
            top = jnp.maximum(far_lse, near_lse)
            far_scale = jnp.exp(far_lse - top)
            near_scale = jnp.exp(near_lse - top)
            merged = far[h * 8 : (h + 1) * 8] * far_scale + near_ref[head] * near_scale
            out_ref[:, head * HD : (head + 1) * HD] = (merged / (far_scale + near_scale)).astype(
                jnp.bfloat16
            )


VMEM = pl.BlockSpec(memory_space=pltpu.VMEM)
SMEM = pl.BlockSpec(memory_space=pltpu.SMEM)
ANY = pl.BlockSpec(memory_space=pl.ANY)


def params(mib):
    return pltpu.CompilerParams(vmem_limit_bytes=mib << 20)


def shards(
    prompt_of,
    suffix_len,
    query,
    new_key,
    new_value,
    suffix_key,
    suffix_value,
    prefix_key,
    prefix_value,
):
    place = lax.axis_index(NEAR).astype(jnp.int32).reshape(1)
    sent, *cuts = pl.pallas_call(
        prep_kernel,
        out_shape=[jax.ShapeDtypeStruct((KVH, 80, HD), jnp.bfloat16)]
        + [jax.ShapeDtypeStruct((2, PIECE, HD), jnp.bfloat16)] * 8,
        in_specs=[SMEM, ANY, ANY, ANY, ANY],
        out_specs=[VMEM] * 9,
        scratch_shapes=[
            pltpu.SMEM((HELD,), jnp.int32),
            pltpu.VMEM((HELD, HEADS * HD), jnp.bfloat16),
            pltpu.SemaphoreType.DMA((2,)),
            pltpu.SemaphoreType.DMA((8, 2)),
        ],
        compiler_params=params(60),
        name="prep",
    )(place, prompt_of, query, prefix_key, prefix_value)
    held = [cuts[0]]
    for step in range(1, 8):
        held.append(lax.ppermute(cuts[step], NEAR, [(i, i ^ step) for i in range(8)]))
    swapped = [lax.ppermute(piece, "c", [(0, 1), (1, 0)]) for piece in held]
    got = lax.all_to_all(sent, "y", 0, 0, tiled=True)
    outgoing = pl.pallas_call(
        pack_kernel,
        out_shape=jax.ShapeDtypeStruct((ROWS, HD), jnp.bfloat16),
        in_specs=[VMEM] + [ANY] * 2,
        out_specs=VMEM,
        compiler_params=params(8),
        name="pack",
    )(got, *held[4:6])
    arrived = lax.all_to_all(outgoing.reshape(PROMPTS, 64, HD), FAR, 0, 0, tiled=True)

    near_out, near_lse = pl.pallas_call(
        near_kernel,
        grid=(HELD,),
        out_shape=[jax.ShapeDtypeStruct((HEADS, HELD, HD), jnp.float32)] * 2,
        in_specs=[
            SMEM,
            pl.BlockSpec((HELD, HEADS * HD), lambda i: (0, 0)),
            pl.BlockSpec((HELD, KVH * HD), lambda i: (0, 0)),
            pl.BlockSpec((HELD, KVH * HD), lambda i: (0, 0)),
            pl.BlockSpec((1, SUF, KVH * HD), lambda i: (i, 0, 0)),
            pl.BlockSpec((1, SUF, KVH * HD), lambda i: (i, 0, 0)),
        ],
        out_specs=[pl.BlockSpec((HEADS, HELD, HD), lambda i: (0, 0, 0))] * 2,
        scratch_shapes=[pltpu.VMEM((HEADS, HELD, HD), jnp.float32)],
        compiler_params=params(12),
        cost_estimate=pl.CostEstimate(flops=300_000_000, bytes_accessed=4_500_000, transcendentals=65536),
        name="near",
    )(
        suffix_len,
        query,
        new_key,
        new_value,
        suffix_key,
        suffix_value,
    )

    parcel = pl.pallas_call(
        far_kernel,
        out_shape=jax.ShapeDtypeStruct((PROMPTS, 80, HD), jnp.bfloat16),
        in_specs=[VMEM] + [ANY] * 16,
        out_specs=VMEM,
        scratch_shapes=[
            pltpu.VMEM((16, 256, PIECE), jnp.float32),
            pltpu.VMEM((RATIO, SLOTS, HD), jnp.bfloat16),
            pltpu.VMEM((RATIO, SLOTS, HD), jnp.bfloat16),
            pltpu.VMEM((SLOTS, HD), jnp.bfloat16),
            pltpu.VMEM((16, 2, PIECE, HD), jnp.bfloat16),
            pltpu.SemaphoreType.DMA((16, 2)),
        ],
        compiler_params=params(60),
        name="far",
    )(arrived.reshape(ROWS, HD), *held, *swapped)
    back = lax.all_to_all(parcel, FAR, 0, 0, tiled=True)
    chosen = pl.pallas_call(
        select_kernel,
        out_shape=jax.ShapeDtypeStruct((KVH, 80, HD), jnp.bfloat16),
        in_specs=[VMEM] * 2 + [ANY] * 2,
        out_specs=VMEM,
        compiler_params=params(8),
        name="select",
    )(got, back, near_out, near_lse)
    final = lax.all_to_all(chosen, "y", 0, 0, tiled=True)
    return pl.pallas_call(
        merge_kernel,
        out_shape=jax.ShapeDtypeStruct((HELD, HEADS * HD), jnp.bfloat16),
        in_specs=[VMEM] * 3,
        out_specs=VMEM,
        compiler_params=params(12),
        name="merge",
    )(final, near_out, near_lse)


def solution(mesh):
    fine = Mesh(mesh.devices.reshape(2, 8, 2, 4, 2), ALL)
    grp = ("xh", "z")
    blk = ("xl", "y", "c")
    in_specs = (
        P(ALL),
        P(ALL),
        P(ALL, None),
        P(ALL, None),
        P(ALL, None),
        P(ALL, None, None),
        P(ALL, None, None),
        P(grp, blk, None),
        P(grp, blk, None),
    )
    return jax.shard_map(
        shards, mesh=fine, in_specs=in_specs, out_specs=P(ALL, None), check_vma=False
    )
```

```python
import math

import jax
import jax.numpy as jnp
from jax import lax
from jax.experimental import pallas as pl
from jax.experimental.pallas import tpu as pltpu
from jax.sharding import Mesh, PartitionSpec as P

HD = 128
CAP = 2
HELD = 8
HEADS = 32
KVH = 4
RATIO = 8
PROMPTS = 32
SUF = 256
PIECE = 256
SLOTS = 256
ROWS = SLOTS * RATIO
NEG = -1e30
SCALE = HD ** (-0.5)
LOG2E = 1.4426950408889634
ALL = ("xh", "z", "xl", "y", "c")
NEAR = ("xl", "y")
FAR = ("xh", "z", "xl")


def slots_of(prompt_ref):
    prompts = [prompt_ref[i] for i in range(HELD)]
    slots = []
    for i in range(HELD):
        rank = jnp.int32(0)
        for j in range(i):
            rank = rank + jnp.where(prompts[j] == prompts[i], 1, 0)
        slots.append(prompts[i] * CAP + rank)
    return slots


def spread(values, index):
    picked = jnp.zeros(index.shape, jnp.int32)
    for i, value in enumerate(values):
        picked = jnp.where(index == i, value, picked)
    return picked


def prep_kernel(place_ref, prompt_hbm, query_hbm, key_ref, value_ref, send_ref, *refs):
    cut_refs = refs[:8]
    prompt_ref, query_ref, small_sem, cut_sem = refs[8:]
    small = [
        pltpu.make_async_copy(prompt_hbm, prompt_ref, small_sem.at[0]),
        pltpu.make_async_copy(query_hbm, query_ref, small_sem.at[1]),
    ]
    for copy in small:
        copy.start()
    place = place_ref[0]
    copies = []
    for step, cut_ref in enumerate(cut_refs):
        target = place ^ step
        prompt = target >> 2
        column = pl.multiple_of((target & 3) * HD, HD)
        for n, cache in enumerate((key_ref, value_ref)):
            copies.append(
                pltpu.make_async_copy(
                    cache.at[prompt, :, pl.ds(column, HD)], cut_ref.at[n], cut_sem.at[step, n]
                )
            )
            copies[-1].start()
    for copy in small:
        copy.wait()
    slots = slots_of(prompt_ref)
    lane = lax.broadcasted_iota(jnp.int32, (HELD, HD), 1)
    row = lax.broadcasted_iota(jnp.int32, (HELD, HD), 0)
    tags = jnp.concatenate(
        [spread(slots, lane & 7).astype(jnp.float32), spread(slots, row).astype(jnp.float32)], axis=0
    ).astype(jnp.bfloat16)
    for y in range(KVH):
        send_ref[y, :64] = jnp.concatenate(
            [
                query_ref[:, h * HD : (h + 1) * HD].astype(jnp.float32)
                for h in range(y * RATIO, (y + 1) * RATIO)
            ],
            axis=0,
        ).astype(jnp.bfloat16)
        send_ref[y, 64:] = tags
    for copy in copies:
        copy.wait()


def pack_kernel(got_ref, *refs):
    out_ref = refs[-1]
    held = got_ref[:, :64].reshape(256, HD)
    tags = [got_ref[y, 64:].astype(jnp.float32)[:1].astype(jnp.int32) for y in range(KVH)]
    half = lax.broadcasted_iota(jnp.int32, (1, HD), 1) < 64
    tag = jnp.concatenate([jnp.where(half, tags[0], tags[1]), jnp.where(half, tags[2], tags[3])], axis=1)
    lane_key = (lax.broadcasted_iota(jnp.int32, (1, 256), 1) >> 3) * 64 + tag
    chunk = 512
    for start in range(0, ROWS, chunk):
        row = lax.broadcasted_iota(jnp.int32, (chunk, 1), 0) + start
        row_key = ((row >> 1) & 3) * 512 + ((row >> 3) & 7) * 64 + (row >> 6) * 2 + (row & 1)
        select = (row_key == lane_key).astype(jnp.float32).astype(jnp.bfloat16)
        out_ref[start : start + chunk, :] = jnp.dot(
            select, held, preferred_element_type=jnp.float32
        ).astype(jnp.bfloat16)


def near_kernel(
    len_ref, query_ref, new_key_ref, new_value_ref, key_ref, value_ref, out_ref, heads_ref
):
    step = pl.program_id(0)

    @pl.when(step == 0)
    def _():
        for h in range(HEADS):
            heads_ref[h] = query_ref[:, h * HD : (h + 1) * HD].astype(jnp.float32)

    length = len_ref[step]
    query = heads_ref[:, pl.ds(step, 1), :].reshape(HEADS, HD)
    keys = key_ref[0]
    values = value_ref[0]
    held_row = lax.broadcasted_iota(jnp.int32, (HELD, 1), 0)

    def row_of(ref):
        rows = jnp.where(held_row == step, ref[...].astype(jnp.float32), 0.0)
        return jnp.sum(rows, axis=0, keepdims=True)

    new_key = row_of(new_key_ref)
    new_value = row_of(new_value_ref)

    def spread_heads(row):
        return jnp.concatenate(
            [jnp.broadcast_to(row[:, k * HD : (k + 1) * HD], (RATIO, HD)) for k in range(KVH)], axis=0
        )

    scores = jnp.concatenate(
        [
            lax.dot_general(
                query.astype(jnp.bfloat16),
                keys[:, k * HD : (k + 1) * HD],
                (((1,), (1,)), ((), ())),
                preferred_element_type=jnp.float32,
            )[k * RATIO : (k + 1) * RATIO]
            for k in range(KVH)
        ],
        axis=0,
    ) * SCALE
    own = jnp.sum(query * spread_heads(new_key), axis=1, keepdims=True) * SCALE
    live = lax.broadcasted_iota(jnp.int32, (1, SUF), 1) < length
    scores = jnp.where(live, scores, NEG)
    top = jnp.maximum(jnp.max(scores, axis=1, keepdims=True), own)
    weights = jnp.where(live, jnp.exp(scores - top), 0.0)
    own_weight = jnp.exp(own - top)
    total = jnp.sum(weights, axis=1, keepdims=True) + own_weight
    rounded = weights.astype(jnp.bfloat16)
    mixed = jnp.concatenate(
        [
            jnp.dot(rounded, values[:, k * HD : (k + 1) * HD], preferred_element_type=jnp.float32)[
                k * RATIO : (k + 1) * RATIO
            ]
            for k in range(KVH)
        ],
        axis=0,
    )
    mixed = mixed + own_weight.astype(jnp.bfloat16).astype(jnp.float32) * spread_heads(new_value)
    out_ref[:HEADS, pl.ds(step, 1), :] = (mixed / total).reshape(HEADS, 1, HD)
    out_ref[HEADS:, pl.ds(step, 1), :] = jnp.broadcast_to(top + jnp.log(total), (HEADS, HD)).reshape(
        HEADS, 1, HD
    )


def far_kernel(query_ref, *refs):
    pieces = refs[:16]
    out_ref, score_ref, query_scr, mixed_scr, stat_scr = refs[16:]
    span = 32
    block = span * RATIO
    tokens = 16 * PIECE
    queries = query_ref[...].astype(jnp.float32).reshape(32, RATIO, 8, HD)
    biggest = jnp.max(jnp.max(jnp.abs(queries), axis=1).reshape(SLOTS, HD), axis=1, keepdims=True)
    valid = (biggest > 0).astype(jnp.float32)
    row = lax.broadcasted_iota(jnp.int32, (SLOTS, SLOTS), 0)
    lane = lax.broadcasted_iota(jnp.int32, (SLOTS, SLOTS), 1)
    wide = jnp.broadcast_to(valid, (SLOTS, SLOTS)).astype(jnp.bfloat16)
    before = jnp.dot(
        (lane < row).astype(jnp.float32).astype(jnp.bfloat16), wide, preferred_element_type=jnp.float32
    )
    order = jnp.where(valid > 0, before, -1.0).astype(jnp.int32)
    gather = (order == lane).astype(jnp.float32).astype(jnp.bfloat16)
    count = jnp.sum(valid).astype(jnp.int32)
    for h in range(RATIO):
        query_scr[h] = lax.dot_general(
            gather,
            queries[:, h].reshape(SLOTS, HD).astype(jnp.bfloat16),
            (((0,), (0,)), ((), ())),
            preferred_element_type=jnp.float32,
        ).astype(jnp.bfloat16)
    mixed_scr[...] = jnp.zeros_like(mixed_scr)
    stat_scr[...] = jnp.zeros_like(stat_scr)

    @pl.loop(0, (count + span - 1) // span)
    def _(index):
        start = pl.multiple_of(index * span, span)
        query = query_scr[:, pl.ds(start, span), :].reshape(block, HD)
        peak = jnp.full((block, HD), -jnp.inf, jnp.float32)
        for n, piece in enumerate(pieces):
            scores = lax.dot_general(
                query, piece[0], (((1,), (1,)), ((), ())), preferred_element_type=jnp.float32
            )
            score_ref[n] = scores
            peak = jnp.maximum(peak, jnp.maximum(scores[:, :HD], scores[:, HD:]))
        peak = jnp.max(peak, axis=1, keepdims=True)
        total = jnp.zeros((block, HD), jnp.float32)
        mixed = jnp.zeros((block, HD), jnp.float32)
        for n, piece in enumerate(pieces):
            weights = jnp.exp2((score_ref[n] - peak) * (SCALE * LOG2E))
            total = total + (weights[:, :HD] + weights[:, HD:])
            mixed = mixed + jnp.dot(
                weights.astype(jnp.bfloat16), piece[1], preferred_element_type=jnp.float32
            )
        total = jnp.sum(total, axis=1, keepdims=True)
        mixed_scr[:, pl.ds(start, span), :] = (mixed / total).astype(jnp.bfloat16).reshape(RATIO, span, HD)
        lse = peak * SCALE + jnp.log(total)
        stat_scr[pl.ds(start, span), :] = split_stat(lse.reshape(RATIO, span, 1), span).astype(jnp.bfloat16)

    idle = 1.0 - valid
    mean = sum(piece[1].astype(jnp.float32).reshape(PIECE // 8, 8, HD).sum(axis=0) for piece in pieces)
    mean = jnp.sum(mean, axis=0, keepdims=True) / tokens
    heads = []
    for h in range(RATIO):
        spread_out = jnp.dot(gather, mixed_scr[h], preferred_element_type=jnp.float32) + idle * mean
        heads.append(spread_out.reshape(32, 8, HD))
    for h in range(0, RATIO, 2):
        out_ref[:, h * 8 : h * 8 + 16] = jnp.concatenate(heads[h : h + 2], axis=1).astype(jnp.bfloat16)
    even = split_stat(jnp.full((RATIO, SLOTS, 1), math.log(tokens), jnp.float32), SLOTS)
    stat = jnp.dot(gather, stat_scr[...], preferred_element_type=jnp.float32) + idle * even
    stat = stat.reshape(32, 8, HD)
    out_ref[:, 64:] = jnp.concatenate([stat, jnp.zeros_like(stat)], axis=1).astype(jnp.bfloat16)


def split_stat(lse, span):
    high = lse.astype(jnp.bfloat16).astype(jnp.float32)
    rest = lse - high
    middle = rest.astype(jnp.bfloat16).astype(jnp.float32)
    low = rest - middle
    lane = lax.broadcasted_iota(jnp.int32, (span, HD), 1)
    stat = jnp.zeros((span, HD), jnp.float32)
    for h in range(RATIO):
        for n, part in enumerate((high, middle, low)):
            stat = jnp.where(lane == n * 8 + h, part[h], stat)
    return stat


def select_kernel(got_ref, back_ref, *refs):
    send_ref = refs[-1]
    tags = [got_ref[y, 64:].astype(jnp.float32)[8:, :1].astype(jnp.int32) for y in range(KVH)]
    lane = lax.broadcasted_iota(jnp.int32, (1, ROWS), 1)
    lane_key = ((lane >> 1) & 3) * 512 + ((lane >> 3) & 7) * 64 + (lane >> 6) * 2 + (lane & 1)
    tag = jnp.concatenate([tags[y] for y in range(KVH) for _ in range(RATIO)], axis=0)
    row_key = (lax.broadcasted_iota(jnp.int32, (256, 1), 0) >> 3) * 64 + tag
    select = (row_key == lane_key).astype(jnp.float32).astype(jnp.bfloat16)
    far = jnp.dot(select, back_ref[:, :64].reshape(ROWS, HD), preferred_element_type=jnp.float32)
    send_ref[:, :64] = far.astype(jnp.bfloat16).reshape(KVH, 64, HD)
    stats = back_ref[:, 64:].astype(jnp.float32)[:, :8].reshape(SLOTS, HD).astype(jnp.bfloat16)
    lane = lax.broadcasted_iota(jnp.int32, (1, SLOTS), 1)
    lane_key = ((lane >> 1) & 3) * 64 + (lane >> 3) * 2 + (lane & 1)
    row_key = (lax.broadcasted_iota(jnp.int32, (32, 1), 0) >> 3) * 64 + jnp.concatenate(tags, axis=0)
    select = (row_key == lane_key).astype(jnp.float32).astype(jnp.bfloat16)
    stat = jnp.dot(select, stats, preferred_element_type=jnp.float32).reshape(KVH, 8, HD)
    send_ref[:, 64:] = jnp.concatenate([stat, jnp.zeros_like(stat)], axis=1).astype(jnp.bfloat16)


def merge_kernel(back_ref, near_ref, out_ref):
    lane = lax.broadcasted_iota(jnp.int32, (HELD, HD), 1)
    for y in range(KVH):
        far = back_ref[y, :64].astype(jnp.float32)
        stat = jnp.where(lane < 24, back_ref[y, 64:].astype(jnp.float32)[:8], 0.0)
        for h in range(RATIO):
            head = y * RATIO + h
            far_lse = jnp.sum(jnp.where((lane & 7) == h, stat, 0.0), axis=1, keepdims=True)
            near_lse = near_ref[HEADS + head]
            top = jnp.maximum(far_lse, near_lse)
            far_scale = jnp.exp(far_lse - top)
            near_scale = jnp.exp(near_lse - top)
            merged = far[h * 8 : (h + 1) * 8] * far_scale + near_ref[head] * near_scale
            out_ref[:, head * HD : (head + 1) * HD] = (merged / (far_scale + near_scale)).astype(
                jnp.bfloat16
            )


VMEM = pl.BlockSpec(memory_space=pltpu.VMEM)
SMEM = pl.BlockSpec(memory_space=pltpu.SMEM)
ANY = pl.BlockSpec(memory_space=pl.ANY)


def params(mib):
    return pltpu.CompilerParams(vmem_limit_bytes=mib << 20)


def shards(
    prompt_of,
    suffix_len,
    query,
    new_key,
    new_value,
    suffix_key,
    suffix_value,
    prefix_key,
    prefix_value,
):
    place = lax.axis_index(NEAR).astype(jnp.int32).reshape(1)
    sent, *cuts = pl.pallas_call(
        prep_kernel,
        out_shape=[jax.ShapeDtypeStruct((KVH, 80, HD), jnp.bfloat16)]
        + [jax.ShapeDtypeStruct((2, PIECE, HD), jnp.bfloat16)] * 8,
        in_specs=[SMEM, ANY, ANY, ANY, ANY],
        out_specs=[VMEM] * 9,
        scratch_shapes=[
            pltpu.SMEM((HELD,), jnp.int32),
            pltpu.VMEM((HELD, HEADS * HD), jnp.bfloat16),
            pltpu.SemaphoreType.DMA((2,)),
            pltpu.SemaphoreType.DMA((8, 2)),
        ],
        compiler_params=params(60),
        name="prep",
    )(place, prompt_of, query, prefix_key, prefix_value)
    held = [cuts[0]]
    for step in range(1, 8):
        held.append(lax.ppermute(cuts[step], NEAR, [(i, i ^ step) for i in range(8)]))
    swapped = [lax.ppermute(piece, "c", [(0, 1), (1, 0)]) for piece in held]
    got = lax.all_to_all(sent, "y", 0, 0, tiled=True)
    outgoing = pl.pallas_call(
        pack_kernel,
        out_shape=jax.ShapeDtypeStruct((ROWS, HD), jnp.bfloat16),
        in_specs=[VMEM] + [ANY] * 3,
        out_specs=VMEM,
        compiler_params=params(8),
        name="pack",
    )(got, *held[4:7])
    arrived = lax.all_to_all(outgoing.reshape(PROMPTS, 64, HD), FAR, 0, 0, tiled=True)

    near = pl.pallas_call(
        near_kernel,
        grid=(HELD,),
        out_shape=jax.ShapeDtypeStruct((2 * HEADS, HELD, HD), jnp.float32),
        in_specs=[
            SMEM,
            pl.BlockSpec((HELD, HEADS * HD), lambda i: (0, 0)),
            pl.BlockSpec((HELD, KVH * HD), lambda i: (0, 0)),
            pl.BlockSpec((HELD, KVH * HD), lambda i: (0, 0)),
            pl.BlockSpec((1, SUF, KVH * HD), lambda i: (i, 0, 0)),
            pl.BlockSpec((1, SUF, KVH * HD), lambda i: (i, 0, 0)),
        ],
        out_specs=pl.BlockSpec((2 * HEADS, HELD, HD), lambda i: (0, 0, 0)),
        scratch_shapes=[pltpu.VMEM((HEADS, HELD, HD), jnp.float32)],
        compiler_params=params(60),
        cost_estimate=pl.CostEstimate(flops=300_000_000, bytes_accessed=4_500_000, transcendentals=65536),
        name="near",
    )(
        suffix_len,
        query,
        new_key,
        new_value,
        suffix_key,
        suffix_value,
    )

    parcel = pl.pallas_call(
        far_kernel,
        out_shape=jax.ShapeDtypeStruct((PROMPTS, 80, HD), jnp.bfloat16),
        in_specs=[VMEM] * 17,
        out_specs=VMEM,
        scratch_shapes=[
            pltpu.VMEM((16, 256, PIECE), jnp.float32),
            pltpu.VMEM((RATIO, SLOTS, HD), jnp.bfloat16),
            pltpu.VMEM((RATIO, SLOTS, HD), jnp.bfloat16),
            pltpu.VMEM((SLOTS, HD), jnp.bfloat16),
        ],
        compiler_params=params(16),
        name="far",
    )(arrived.reshape(ROWS, HD), *held, *swapped)
    back = lax.all_to_all(parcel, FAR, 0, 0, tiled=True)
    chosen = pl.pallas_call(
        select_kernel,
        out_shape=jax.ShapeDtypeStruct((KVH, 80, HD), jnp.bfloat16),
        in_specs=[VMEM] * 2,
        out_specs=VMEM,
        compiler_params=params(8),
        name="select",
    )(got, back)
    final = lax.all_to_all(chosen, "y", 0, 0, tiled=True)
    return pl.pallas_call(
        merge_kernel,
        out_shape=jax.ShapeDtypeStruct((HELD, HEADS * HD), jnp.bfloat16),
        in_specs=[VMEM] * 2,
        out_specs=VMEM,
        compiler_params=params(12),
        name="merge",
    )(final, near)


def solution(mesh):
    fine = Mesh(mesh.devices.reshape(2, 8, 2, 4, 2), ALL)
    grp = ("xh", "z")
    blk = ("xl", "y", "c")
    in_specs = (
        P(ALL),
        P(ALL),
        P(ALL, None),
        P(ALL, None),
        P(ALL, None),
        P(ALL, None, None),
        P(ALL, None, None),
        P(grp, blk, None),
        P(grp, blk, None),
    )
    return jax.shard_map(
        shards, mesh=fine, in_specs=in_specs, out_specs=P(ALL, None), check_vma=False
    )
```

```python
import math

import jax
import jax.numpy as jnp
from jax import lax
from jax.experimental import pallas as pl
from jax.experimental.pallas import tpu as pltpu
from jax.sharding import Mesh, PartitionSpec as P

HD = 128
CAP = 2
HELD = 8
HEADS = 32
KVH = 4
RATIO = 8
PROMPTS = 32
SUF = 256
PIECE = 256
SLOTS = 256
ROWS = SLOTS * RATIO
NEG = -1e30
SCALE = HD ** (-0.5)
LOG2E = 1.4426950408889634
ALL = ("xh", "z", "xl", "y", "c")
NEAR = ("xl", "y")
FAR = ("xh", "z", "xl")


def slots_of(prompt_ref):
    prompts = [prompt_ref[i] for i in range(HELD)]
    slots = []
    for i in range(HELD):
        rank = jnp.int32(0)
        for j in range(i):
            rank = rank + jnp.where(prompts[j] == prompts[i], 1, 0)
        slots.append(prompts[i] * CAP + rank)
    return slots


def spread(values, index):
    picked = jnp.zeros(index.shape, jnp.int32)
    for i, value in enumerate(values):
        picked = jnp.where(index == i, value, picked)
    return picked


def prep_kernel(place_ref, prompt_hbm, query_hbm, key_ref, value_ref, send_ref, *refs):
    cut_refs = refs[:8]
    prompt_ref, query_ref, small_sem, cut_sem = refs[8:]
    small = [
        pltpu.make_async_copy(prompt_hbm, prompt_ref, small_sem.at[0]),
        pltpu.make_async_copy(query_hbm, query_ref, small_sem.at[1]),
    ]
    for copy in small:
        copy.start()
    place = place_ref[0]
    copies = []
    for step, cut_ref in enumerate(cut_refs):
        target = place ^ step
        prompt = target >> 2
        column = pl.multiple_of((target & 3) * HD, HD)
        for n, cache in enumerate((key_ref, value_ref)):
            copies.append(
                pltpu.make_async_copy(
                    cache.at[prompt, :, pl.ds(column, HD)], cut_ref.at[n], cut_sem.at[step, n]
                )
            )
            copies[-1].start()
    for copy in small:
        copy.wait()
    slots = slots_of(prompt_ref)
    lane = lax.broadcasted_iota(jnp.int32, (HELD, HD), 1)
    row = lax.broadcasted_iota(jnp.int32, (HELD, HD), 0)
    tags = jnp.concatenate(
        [spread(slots, lane & 7).astype(jnp.float32), spread(slots, row).astype(jnp.float32)], axis=0
    ).astype(jnp.bfloat16)
    for y in range(KVH):
        send_ref[y, :64] = jnp.concatenate(
            [
                query_ref[:, h * HD : (h + 1) * HD].astype(jnp.float32)
                for h in range(y * RATIO, (y + 1) * RATIO)
            ],
            axis=0,
        ).astype(jnp.bfloat16)
        send_ref[y, 64:] = tags
    for copy in copies:
        copy.wait()


def pack_kernel(got_ref, *refs):
    out_ref = refs[-1]
    held = got_ref[:, :64].reshape(256, HD)
    tags = [got_ref[y, 64:].astype(jnp.float32)[:1].astype(jnp.int32) for y in range(KVH)]
    half = lax.broadcasted_iota(jnp.int32, (1, HD), 1) < 64
    tag = jnp.concatenate([jnp.where(half, tags[0], tags[1]), jnp.where(half, tags[2], tags[3])], axis=1)
    lane_key = (lax.broadcasted_iota(jnp.int32, (1, 256), 1) >> 3) * 64 + tag
    chunk = 512
    for start in range(0, ROWS, chunk):
        row = lax.broadcasted_iota(jnp.int32, (chunk, 1), 0) + start
        row_key = ((row >> 1) & 3) * 512 + ((row >> 3) & 7) * 64 + (row >> 6) * 2 + (row & 1)
        select = (row_key == lane_key).astype(jnp.float32).astype(jnp.bfloat16)
        out_ref[start : start + chunk, :] = jnp.dot(
            select, held, preferred_element_type=jnp.float32
        ).astype(jnp.bfloat16)


def near_kernel(
    len_ref, query_ref, new_key_ref, new_value_ref, key_ref, value_ref, out_ref, heads_ref
):
    step = pl.program_id(0)

    @pl.when(step == 0)
    def _():
        for h in range(HEADS):
            heads_ref[h] = query_ref[:, h * HD : (h + 1) * HD].astype(jnp.float32)

    length = len_ref[step]
    query = heads_ref[:, pl.ds(step, 1), :].reshape(HEADS, HD)
    keys = key_ref[0]
    values = value_ref[0]
    held_row = lax.broadcasted_iota(jnp.int32, (HELD, 1), 0)

    def row_of(ref):
        rows = jnp.where(held_row == step, ref[...].astype(jnp.float32), 0.0)
        return jnp.sum(rows, axis=0, keepdims=True)

    new_key = row_of(new_key_ref)
    new_value = row_of(new_value_ref)

    def spread_heads(row):
        return jnp.concatenate(
            [jnp.broadcast_to(row[:, k * HD : (k + 1) * HD], (RATIO, HD)) for k in range(KVH)], axis=0
        )

    scores = jnp.concatenate(
        [
            lax.dot_general(
                query.astype(jnp.bfloat16),
                keys[:, k * HD : (k + 1) * HD],
                (((1,), (1,)), ((), ())),
                preferred_element_type=jnp.float32,
            )[k * RATIO : (k + 1) * RATIO]
            for k in range(KVH)
        ],
        axis=0,
    ) * SCALE
    own = jnp.sum(query * spread_heads(new_key), axis=1, keepdims=True) * SCALE
    live = lax.broadcasted_iota(jnp.int32, (1, SUF), 1) < length
    scores = jnp.where(live, scores, NEG)
    top = jnp.maximum(jnp.max(scores, axis=1, keepdims=True), own)
    weights = jnp.where(live, jnp.exp(scores - top), 0.0)
    own_weight = jnp.exp(own - top)
    total = jnp.sum(weights, axis=1, keepdims=True) + own_weight
    rounded = weights.astype(jnp.bfloat16)
    mixed = jnp.concatenate(
        [
            jnp.dot(rounded, values[:, k * HD : (k + 1) * HD], preferred_element_type=jnp.float32)[
                k * RATIO : (k + 1) * RATIO
            ]
            for k in range(KVH)
        ],
        axis=0,
    )
    mixed = mixed + own_weight.astype(jnp.bfloat16).astype(jnp.float32) * spread_heads(new_value)
    out_ref[:HEADS, pl.ds(step, 1), :] = (mixed / total).reshape(HEADS, 1, HD)
    out_ref[HEADS:, pl.ds(step, 1), :] = jnp.broadcast_to(top + jnp.log(total), (HEADS, HD)).reshape(
        HEADS, 1, HD
    )


def far_kernel(query_ref, *refs):
    pieces = refs[:16]
    out_ref, score_ref, query_scr, mixed_scr, stat_scr = refs[16:]
    tokens = 16 * PIECE
    queries = query_ref[...].astype(jnp.float32).reshape(32, RATIO, 8, HD)
    biggest = jnp.max(jnp.max(jnp.abs(queries), axis=1).reshape(SLOTS, HD), axis=1, keepdims=True)
    valid = (biggest > 0).astype(jnp.float32)
    row = lax.broadcasted_iota(jnp.int32, (SLOTS, SLOTS), 0)
    lane = lax.broadcasted_iota(jnp.int32, (SLOTS, SLOTS), 1)
    wide = jnp.broadcast_to(valid, (SLOTS, SLOTS)).astype(jnp.bfloat16)
    before = jnp.dot(
        (lane < row).astype(jnp.float32).astype(jnp.bfloat16), wide, preferred_element_type=jnp.float32
    )
    order = jnp.where(valid > 0, before, -1.0).astype(jnp.int32)
    gather = (order == lane).astype(jnp.float32).astype(jnp.bfloat16)
    count = jnp.sum(valid).astype(jnp.int32)
    for h in range(RATIO):
        query_scr[h] = lax.dot_general(
            gather,
            queries[:, h].reshape(SLOTS, HD).astype(jnp.bfloat16),
            (((0,), (0,)), ((), ())),
            preferred_element_type=jnp.float32,
        ).astype(jnp.bfloat16)
    mixed_scr[...] = jnp.zeros_like(mixed_scr)
    stat_scr[...] = jnp.zeros_like(stat_scr)

    def work(start, span):
        block = span * RATIO
        query = query_scr[:, pl.ds(start, span), :].reshape(block, HD)
        peak = jnp.full((block, HD), -jnp.inf, jnp.float32)
        for n, piece in enumerate(pieces):
            scores = lax.dot_general(
                query, piece[0], (((1,), (1,)), ((), ())), preferred_element_type=jnp.float32
            )
            score_ref[n, :block] = scores
            peak = jnp.maximum(peak, jnp.maximum(scores[:, :HD], scores[:, HD:]))
        peak = jnp.max(peak, axis=1, keepdims=True)
        total = jnp.zeros((block, HD), jnp.float32)
        mixed = jnp.zeros((block, HD), jnp.float32)
        for n, piece in enumerate(pieces):
            weights = jnp.exp2((score_ref[n, :block] - peak) * (SCALE * LOG2E))
            total = total + (weights[:, :HD] + weights[:, HD:])
            mixed = mixed + jnp.dot(
                weights.astype(jnp.bfloat16), piece[1], preferred_element_type=jnp.float32
            )
        total = jnp.sum(total, axis=1, keepdims=True)
        mixed_scr[:, pl.ds(start, span), :] = (mixed / total).astype(jnp.bfloat16).reshape(RATIO, span, HD)
        lse = peak * SCALE + jnp.log(total)
        stat_scr[pl.ds(start, span), :] = split_stat(lse.reshape(RATIO, span, 1), span).astype(jnp.bfloat16)

    halves = (count + 15) // 16

    @pl.loop(0, halves // 2)
    def _(index):
        work(pl.multiple_of(index * 32, 32), 32)

    @pl.when(halves % 2 == 1)
    def _():
        work(pl.multiple_of((halves - 1) * 16, 16), 16)

    idle = 1.0 - valid
    mean = sum(piece[1].astype(jnp.float32).reshape(PIECE // 8, 8, HD).sum(axis=0) for piece in pieces)
    mean = jnp.sum(mean, axis=0, keepdims=True) / tokens
    heads = []
    for h in range(RATIO):
        spread_out = jnp.dot(gather, mixed_scr[h], preferred_element_type=jnp.float32) + idle * mean
        heads.append(spread_out.reshape(32, 8, HD))
    for h in range(0, RATIO, 2):
        out_ref[:, h * 8 : h * 8 + 16] = jnp.concatenate(heads[h : h + 2], axis=1).astype(jnp.bfloat16)
    even = split_stat(jnp.full((RATIO, SLOTS, 1), math.log(tokens), jnp.float32), SLOTS)
    stat = jnp.dot(gather, stat_scr[...], preferred_element_type=jnp.float32) + idle * even
    stat = stat.reshape(32, 8, HD)
    out_ref[:, 64:] = jnp.concatenate([stat, jnp.zeros_like(stat)], axis=1).astype(jnp.bfloat16)


def split_stat(lse, span):
    high = lse.astype(jnp.bfloat16).astype(jnp.float32)
    rest = lse - high
    middle = rest.astype(jnp.bfloat16).astype(jnp.float32)
    low = rest - middle
    lane = lax.broadcasted_iota(jnp.int32, (span, HD), 1)
    stat = jnp.zeros((span, HD), jnp.float32)
    for h in range(RATIO):
        for n, part in enumerate((high, middle, low)):
            stat = jnp.where(lane == n * 8 + h, part[h], stat)
    return stat


def select_kernel(got_ref, back_ref, *refs):
    send_ref = refs[-1]
    tags = [got_ref[y, 64:].astype(jnp.float32)[8:, :1].astype(jnp.int32) for y in range(KVH)]
    lane = lax.broadcasted_iota(jnp.int32, (1, ROWS), 1)
    lane_key = ((lane >> 1) & 3) * 512 + ((lane >> 3) & 7) * 64 + (lane >> 6) * 2 + (lane & 1)
    tag = jnp.concatenate([tags[y] for y in range(KVH) for _ in range(RATIO)], axis=0)
    row_key = (lax.broadcasted_iota(jnp.int32, (256, 1), 0) >> 3) * 64 + tag
    select = (row_key == lane_key).astype(jnp.float32).astype(jnp.bfloat16)
    far = jnp.dot(select, back_ref[:, :64].reshape(ROWS, HD), preferred_element_type=jnp.float32)
    send_ref[:, :64] = far.astype(jnp.bfloat16).reshape(KVH, 64, HD)
    stats = back_ref[:, 64:].astype(jnp.float32)[:, :8].reshape(SLOTS, HD).astype(jnp.bfloat16)
    lane = lax.broadcasted_iota(jnp.int32, (1, SLOTS), 1)
    lane_key = ((lane >> 1) & 3) * 64 + (lane >> 3) * 2 + (lane & 1)
    row_key = (lax.broadcasted_iota(jnp.int32, (32, 1), 0) >> 3) * 64 + jnp.concatenate(tags, axis=0)
    select = (row_key == lane_key).astype(jnp.float32).astype(jnp.bfloat16)
    stat = jnp.dot(select, stats, preferred_element_type=jnp.float32).reshape(KVH, 8, HD)
    send_ref[:, 64:] = jnp.concatenate([stat, jnp.zeros_like(stat)], axis=1).astype(jnp.bfloat16)


def merge_kernel(back_ref, near_ref, out_ref):
    lane = lax.broadcasted_iota(jnp.int32, (HELD, HD), 1)
    for y in range(KVH):
        far = back_ref[y, :64].astype(jnp.float32)
        stat = jnp.where(lane < 24, back_ref[y, 64:].astype(jnp.float32)[:8], 0.0)
        for h in range(RATIO):
            head = y * RATIO + h
            far_lse = jnp.sum(jnp.where((lane & 7) == h, stat, 0.0), axis=1, keepdims=True)
            near_lse = near_ref[HEADS + head]
            top = jnp.maximum(far_lse, near_lse)
            far_scale = jnp.exp(far_lse - top)
            near_scale = jnp.exp(near_lse - top)
            merged = far[h * 8 : (h + 1) * 8] * far_scale + near_ref[head] * near_scale
            out_ref[:, head * HD : (head + 1) * HD] = (merged / (far_scale + near_scale)).astype(
                jnp.bfloat16
            )


VMEM = pl.BlockSpec(memory_space=pltpu.VMEM)
SMEM = pl.BlockSpec(memory_space=pltpu.SMEM)
ANY = pl.BlockSpec(memory_space=pl.ANY)


def params(mib):
    return pltpu.CompilerParams(vmem_limit_bytes=mib << 20)


def shards(
    prompt_of,
    suffix_len,
    query,
    new_key,
    new_value,
    suffix_key,
    suffix_value,
    prefix_key,
    prefix_value,
):
    place = lax.axis_index(NEAR).astype(jnp.int32).reshape(1)
    sent, *cuts = pl.pallas_call(
        prep_kernel,
        out_shape=[jax.ShapeDtypeStruct((KVH, 80, HD), jnp.bfloat16)]
        + [jax.ShapeDtypeStruct((2, PIECE, HD), jnp.bfloat16)] * 8,
        in_specs=[SMEM, ANY, ANY, ANY, ANY],
        out_specs=[VMEM] * 9,
        scratch_shapes=[
            pltpu.SMEM((HELD,), jnp.int32),
            pltpu.VMEM((HELD, HEADS * HD), jnp.bfloat16),
            pltpu.SemaphoreType.DMA((2,)),
            pltpu.SemaphoreType.DMA((8, 2)),
        ],
        compiler_params=params(60),
        name="prep",
    )(place, prompt_of, query, prefix_key, prefix_value)
    held = [cuts[0]]
    for step in range(1, 8):
        held.append(lax.ppermute(cuts[step], NEAR, [(i, i ^ step) for i in range(8)]))
    swapped = [lax.ppermute(piece, "c", [(0, 1), (1, 0)]) for piece in held]
    got = lax.all_to_all(sent, "y", 0, 0, tiled=True)
    outgoing = pl.pallas_call(
        pack_kernel,
        out_shape=jax.ShapeDtypeStruct((ROWS, HD), jnp.bfloat16),
        in_specs=[VMEM] + [ANY] * 3,
        out_specs=VMEM,
        compiler_params=params(8),
        name="pack",
    )(got, *held[4:7])
    arrived = lax.all_to_all(outgoing.reshape(PROMPTS, 64, HD), FAR, 0, 0, tiled=True)

    near = pl.pallas_call(
        near_kernel,
        grid=(HELD,),
        out_shape=jax.ShapeDtypeStruct((2 * HEADS, HELD, HD), jnp.float32),
        in_specs=[
            SMEM,
            pl.BlockSpec((HELD, HEADS * HD), lambda i: (0, 0)),
            pl.BlockSpec((HELD, KVH * HD), lambda i: (0, 0)),
            pl.BlockSpec((HELD, KVH * HD), lambda i: (0, 0)),
            pl.BlockSpec((1, SUF, KVH * HD), lambda i: (i, 0, 0)),
            pl.BlockSpec((1, SUF, KVH * HD), lambda i: (i, 0, 0)),
        ],
        out_specs=pl.BlockSpec((2 * HEADS, HELD, HD), lambda i: (0, 0, 0)),
        scratch_shapes=[pltpu.VMEM((HEADS, HELD, HD), jnp.float32)],
        compiler_params=params(60),
        cost_estimate=pl.CostEstimate(flops=300_000_000, bytes_accessed=4_500_000, transcendentals=65536),
        name="near",
    )(
        suffix_len,
        query,
        new_key,
        new_value,
        suffix_key,
        suffix_value,
    )

    parcel = pl.pallas_call(
        far_kernel,
        out_shape=jax.ShapeDtypeStruct((PROMPTS, 80, HD), jnp.bfloat16),
        in_specs=[VMEM] * 17,
        out_specs=VMEM,
        scratch_shapes=[
            pltpu.VMEM((16, 256, PIECE), jnp.float32),
            pltpu.VMEM((RATIO, SLOTS, HD), jnp.bfloat16),
            pltpu.VMEM((RATIO, SLOTS, HD), jnp.bfloat16),
            pltpu.VMEM((SLOTS, HD), jnp.bfloat16),
        ],
        compiler_params=params(16),
        name="far",
    )(arrived.reshape(ROWS, HD), *held, *swapped)
    back = lax.all_to_all(parcel, FAR, 0, 0, tiled=True)
    chosen = pl.pallas_call(
        select_kernel,
        out_shape=jax.ShapeDtypeStruct((KVH, 80, HD), jnp.bfloat16),
        in_specs=[VMEM] * 2 + [ANY],
        out_specs=VMEM,
        compiler_params=params(8),
        name="select",
    )(got, back, near)
    final = lax.all_to_all(chosen, "y", 0, 0, tiled=True)
    return pl.pallas_call(
        merge_kernel,
        out_shape=jax.ShapeDtypeStruct((HELD, HEADS * HD), jnp.bfloat16),
        in_specs=[VMEM] * 2,
        out_specs=VMEM,
        compiler_params=params(12),
        name="merge",
    )(final, near)


def solution(mesh):
    fine = Mesh(mesh.devices.reshape(2, 8, 2, 4, 2), ALL)
    grp = ("xh", "z")
    blk = ("xl", "y", "c")
    in_specs = (
        P(ALL),
        P(ALL),
        P(ALL, None),
        P(ALL, None),
        P(ALL, None),
        P(ALL, None, None),
        P(ALL, None, None),
        P(grp, blk, None),
        P(grp, blk, None),
    )
    return jax.shard_map(
        shards, mesh=fine, in_specs=in_specs, out_specs=P(ALL, None), check_vma=False
    )
```

```python
import math

import jax
import jax.numpy as jnp
from jax import lax
from jax.experimental import pallas as pl
from jax.experimental.pallas import tpu as pltpu
from jax.sharding import Mesh, PartitionSpec as P

HD = 128
CAP = 2
HELD = 8
HEADS = 32
KVH = 4
RATIO = 8
PROMPTS = 32
SUF = 256
PIECE = 256
SLOTS = 256
ROWS = SLOTS * RATIO
NEG = -1e30
SCALE = HD ** (-0.5)
LOG2E = 1.4426950408889634
ALL = ("xh", "z", "xl", "y", "c")
NEAR = ("xl", "y")
FAR = ("xh", "z", "xl")


def slots_of(prompt_ref):
    prompts = [prompt_ref[i] for i in range(HELD)]
    slots = []
    for i in range(HELD):
        rank = jnp.int32(0)
        for j in range(i):
            rank = rank + jnp.where(prompts[j] == prompts[i], 1, 0)
        slots.append(prompts[i] * CAP + rank)
    return slots


def spread(values, index):
    picked = jnp.zeros(index.shape, jnp.int32)
    for i, value in enumerate(values):
        picked = jnp.where(index == i, value, picked)
    return picked


def prep_kernel(place_ref, prompt_hbm, query_hbm, key_ref, value_ref, send_ref, *refs):
    cut_refs = refs[:8]
    prompt_ref, query_ref, small_sem, cut_sem = refs[8:]
    small = [
        pltpu.make_async_copy(prompt_hbm, prompt_ref, small_sem.at[0]),
        pltpu.make_async_copy(query_hbm, query_ref, small_sem.at[1]),
    ]
    for copy in small:
        copy.start()
    place = place_ref[0]
    copies = []
    for step, cut_ref in enumerate(cut_refs):
        target = place ^ step
        prompt = target >> 2
        column = pl.multiple_of((target & 3) * HD, HD)
        for n, cache in enumerate((key_ref, value_ref)):
            copies.append(
                pltpu.make_async_copy(
                    cache.at[prompt, :, pl.ds(column, HD)], cut_ref.at[n], cut_sem.at[step, n]
                )
            )
            copies[-1].start()
    for copy in small:
        copy.wait()
    slots = slots_of(prompt_ref)
    lane = lax.broadcasted_iota(jnp.int32, (HELD, HD), 1)
    row = lax.broadcasted_iota(jnp.int32, (HELD, HD), 0)
    tags = jnp.concatenate(
        [spread(slots, lane & 7).astype(jnp.float32), spread(slots, row).astype(jnp.float32)], axis=0
    ).astype(jnp.bfloat16)
    for y in range(KVH):
        send_ref[y, :64] = jnp.concatenate(
            [
                query_ref[:, h * HD : (h + 1) * HD].astype(jnp.float32)
                for h in range(y * RATIO, (y + 1) * RATIO)
            ],
            axis=0,
        ).astype(jnp.bfloat16)
        send_ref[y, 64:] = tags
    for copy in copies:
        copy.wait()


def pack_kernel(got_ref, *refs):
    out_ref = refs[-1]
    held = got_ref[:, :64].reshape(256, HD)
    tags = [got_ref[y, 64:].astype(jnp.float32)[:1].astype(jnp.int32) for y in range(KVH)]
    half = lax.broadcasted_iota(jnp.int32, (1, HD), 1) < 64
    tag = jnp.concatenate([jnp.where(half, tags[0], tags[1]), jnp.where(half, tags[2], tags[3])], axis=1)
    lane_key = (lax.broadcasted_iota(jnp.int32, (1, 256), 1) >> 3) * 64 + tag
    chunk = 512
    for start in range(0, ROWS, chunk):
        row = lax.broadcasted_iota(jnp.int32, (chunk, 1), 0) + start
        row_key = ((row >> 1) & 3) * 512 + ((row >> 3) & 7) * 64 + (row >> 6) * 2 + (row & 1)
        select = (row_key == lane_key).astype(jnp.float32).astype(jnp.bfloat16)
        out_ref[start : start + chunk, :] = jnp.dot(
            select, held, preferred_element_type=jnp.float32
        ).astype(jnp.bfloat16)


def near_kernel(
    len_ref, query_ref, new_key_ref, new_value_ref, key_ref, value_ref, out_ref, heads_ref
):
    step = pl.program_id(0)

    @pl.when(step == 0)
    def _():
        for h in range(HEADS):
            heads_ref[h] = query_ref[:, h * HD : (h + 1) * HD].astype(jnp.float32)

    length = len_ref[step]
    query = heads_ref[:, pl.ds(step, 1), :].reshape(HEADS, HD)
    keys = key_ref[0]
    values = value_ref[0]
    held_row = lax.broadcasted_iota(jnp.int32, (HELD, 1), 0)

    def row_of(ref):
        rows = jnp.where(held_row == step, ref[...].astype(jnp.float32), 0.0)
        return jnp.sum(rows, axis=0, keepdims=True)

    new_key = row_of(new_key_ref)
    new_value = row_of(new_value_ref)

    def spread_heads(row):
        return jnp.concatenate(
            [jnp.broadcast_to(row[:, k * HD : (k + 1) * HD], (RATIO, HD)) for k in range(KVH)], axis=0
        )

    scores = jnp.concatenate(
        [
            lax.dot_general(
                query.astype(jnp.bfloat16),
                keys[:, k * HD : (k + 1) * HD],
                (((1,), (1,)), ((), ())),
                preferred_element_type=jnp.float32,
            )[k * RATIO : (k + 1) * RATIO]
            for k in range(KVH)
        ],
        axis=0,
    ) * SCALE
    own = jnp.sum(query * spread_heads(new_key), axis=1, keepdims=True) * SCALE
    live = lax.broadcasted_iota(jnp.int32, (1, SUF), 1) < length
    scores = jnp.where(live, scores, NEG)
    top = jnp.maximum(jnp.max(scores, axis=1, keepdims=True), own)
    weights = jnp.where(live, jnp.exp(scores - top), 0.0)
    own_weight = jnp.exp(own - top)
    total = jnp.sum(weights, axis=1, keepdims=True) + own_weight
    rounded = weights.astype(jnp.bfloat16)
    mixed = jnp.concatenate(
        [
            jnp.dot(rounded, values[:, k * HD : (k + 1) * HD], preferred_element_type=jnp.float32)[
                k * RATIO : (k + 1) * RATIO
            ]
            for k in range(KVH)
        ],
        axis=0,
    )
    mixed = mixed + own_weight.astype(jnp.bfloat16).astype(jnp.float32) * spread_heads(new_value)
    out_ref[:HEADS, pl.ds(step, 1), :] = (mixed / total).reshape(HEADS, 1, HD)
    out_ref[HEADS:, pl.ds(step, 1), :] = jnp.broadcast_to(top + jnp.log(total), (HEADS, HD)).reshape(
        HEADS, 1, HD
    )


def far_kernel(query_ref, *refs):
    pieces = refs[:16]
    out_ref, score_ref, query_scr, mixed_scr, stat_scr = refs[16:]
    tokens = 16 * PIECE
    queries = query_ref[...].astype(jnp.float32).reshape(32, RATIO, 8, HD)
    biggest = jnp.max(jnp.max(jnp.abs(queries), axis=1).reshape(SLOTS, HD), axis=1, keepdims=True)
    valid = (biggest > 0).astype(jnp.float32)
    row = lax.broadcasted_iota(jnp.int32, (SLOTS, SLOTS), 0)
    lane = lax.broadcasted_iota(jnp.int32, (SLOTS, SLOTS), 1)
    wide = jnp.broadcast_to(valid, (SLOTS, SLOTS)).astype(jnp.bfloat16)
    before = jnp.dot(
        (lane < row).astype(jnp.float32).astype(jnp.bfloat16), wide, preferred_element_type=jnp.float32
    )
    order = jnp.where(valid > 0, before, -1.0).astype(jnp.int32)
    gather = (order == lane).astype(jnp.float32).astype(jnp.bfloat16)
    count = jnp.sum(valid).astype(jnp.int32)
    for h in range(RATIO):
        query_scr[h] = lax.dot_general(
            gather,
            queries[:, h].reshape(SLOTS, HD).astype(jnp.bfloat16),
            (((0,), (0,)), ((), ())),
            preferred_element_type=jnp.float32,
        ).astype(jnp.bfloat16)
    mixed_scr[...] = jnp.zeros_like(mixed_scr)
    stat_scr[...] = jnp.zeros_like(stat_scr)

    def work(start, span):
        block = span * RATIO
        query = query_scr[:, pl.ds(start, span), :].reshape(block, HD)
        peak = jnp.full((block, HD), -jnp.inf, jnp.float32)
        for n, piece in enumerate(pieces):
            scores = lax.dot_general(
                query, piece[0], (((1,), (1,)), ((), ())), preferred_element_type=jnp.float32
            )
            score_ref[n, :block] = scores
            peak = jnp.maximum(peak, jnp.maximum(scores[:, :HD], scores[:, HD:]))
        peak = jnp.max(peak, axis=1, keepdims=True)
        total = jnp.zeros((block, HD), jnp.float32)
        mixed = jnp.zeros((block, HD), jnp.float32)
        for n, piece in enumerate(pieces):
            weights = jnp.exp2((score_ref[n, :block] - peak) * (SCALE * LOG2E))
            total = total + (weights[:, :HD] + weights[:, HD:])
            mixed = mixed + jnp.dot(
                weights.astype(jnp.bfloat16), piece[1], preferred_element_type=jnp.float32
            )
        total = jnp.sum(total, axis=1, keepdims=True)
        mixed_scr[:, pl.ds(start, span), :] = (mixed / total).astype(jnp.bfloat16).reshape(RATIO, span, HD)
        lse = peak * SCALE + jnp.log(total)
        stat_scr[pl.ds(start, span), :] = split_stat(lse.reshape(RATIO, span, 1), span).astype(jnp.bfloat16)

    halves = (count + 15) // 16

    @pl.loop(0, halves // 2)
    def _(index):
        work(pl.multiple_of(index * 32, 32), 32)

    @pl.when(halves % 2 == 1)
    def _():
        work(pl.multiple_of((halves - 1) * 16, 16), 16)

    idle = 1.0 - valid
    mean = sum(piece[1].astype(jnp.float32).reshape(PIECE // 8, 8, HD).sum(axis=0) for piece in pieces)
    mean = jnp.sum(mean, axis=0, keepdims=True) / tokens
    for h in range(RATIO):
        out_ref[h] = (
            jnp.dot(gather, mixed_scr[h], preferred_element_type=jnp.float32) + idle * mean
        ).astype(jnp.bfloat16)
    even = split_stat(jnp.full((RATIO, SLOTS, 1), math.log(tokens), jnp.float32), SLOTS)
    stat = jnp.dot(gather, stat_scr[...], preferred_element_type=jnp.float32) + idle * even
    out_ref[RATIO] = stat.astype(jnp.bfloat16)


def split_stat(lse, span):
    high = lse.astype(jnp.bfloat16).astype(jnp.float32)
    rest = lse - high
    middle = rest.astype(jnp.bfloat16).astype(jnp.float32)
    low = rest - middle
    lane = lax.broadcasted_iota(jnp.int32, (span, HD), 1)
    stat = jnp.zeros((span, HD), jnp.float32)
    for h in range(RATIO):
        for n, part in enumerate((high, middle, low)):
            stat = jnp.where(lane == n * 8 + h, part[h], stat)
    return stat


def merge_kernel(prompt_ref, back_ref, near_ref, out_ref):
    slots = slots_of(prompt_ref)
    count = HEADS * HELD
    row = lax.broadcasted_iota(jnp.int32, (count, 1), 0)
    slot = spread(slots, row & 7)
    head = row >> 3
    row_key = (head & 7) * SLOTS + (slot >> 1) * 8 + (head >> 3) * 2 + (slot & 1)
    select = (row_key == lax.broadcasted_iota(jnp.int32, (1, ROWS), 1)).astype(jnp.float32)
    far = jnp.dot(select.astype(jnp.bfloat16), back_ref[:ROWS, :], preferred_element_type=jnp.float32)
    row = lax.broadcasted_iota(jnp.int32, (KVH * HELD, 1), 0)
    slot = spread(slots, row & 7)
    row_key = (slot >> 1) * 8 + (row >> 3) * 2 + (slot & 1)
    select = (row_key == lax.broadcasted_iota(jnp.int32, (1, SLOTS), 1)).astype(jnp.float32)
    stats = jnp.dot(select.astype(jnp.bfloat16), back_ref[ROWS:, :], preferred_element_type=jnp.float32)
    lane = lax.broadcasted_iota(jnp.int32, (HELD, HD), 1)
    for y in range(KVH):
        stat = jnp.where(lane < 24, stats[y * HELD : (y + 1) * HELD], 0.0)
        for h in range(RATIO):
            head = y * RATIO + h
            far_lse = jnp.sum(jnp.where((lane & 7) == h, stat, 0.0), axis=1, keepdims=True)
            near_lse = near_ref[HEADS + head]
            top = jnp.maximum(far_lse, near_lse)
            far_scale = jnp.exp(far_lse - top)
            near_scale = jnp.exp(near_lse - top)
            merged = far[head * HELD : (head + 1) * HELD] * far_scale + near_ref[head] * near_scale
            out_ref[:, head * HD : (head + 1) * HD] = (merged / (far_scale + near_scale)).astype(
                jnp.bfloat16
            )


VMEM = pl.BlockSpec(memory_space=pltpu.VMEM)
SMEM = pl.BlockSpec(memory_space=pltpu.SMEM)
ANY = pl.BlockSpec(memory_space=pl.ANY)


def params(mib):
    return pltpu.CompilerParams(vmem_limit_bytes=mib << 20)


def shards(
    prompt_of,
    suffix_len,
    query,
    new_key,
    new_value,
    suffix_key,
    suffix_value,
    prefix_key,
    prefix_value,
):
    place = lax.axis_index(NEAR).astype(jnp.int32).reshape(1)
    sent, *cuts = pl.pallas_call(
        prep_kernel,
        out_shape=[jax.ShapeDtypeStruct((KVH, 80, HD), jnp.bfloat16)]
        + [jax.ShapeDtypeStruct((2, PIECE, HD), jnp.bfloat16)] * 8,
        in_specs=[SMEM, ANY, ANY, ANY, ANY],
        out_specs=[VMEM] * 9,
        scratch_shapes=[
            pltpu.SMEM((HELD,), jnp.int32),
            pltpu.VMEM((HELD, HEADS * HD), jnp.bfloat16),
            pltpu.SemaphoreType.DMA((2,)),
            pltpu.SemaphoreType.DMA((8, 2)),
        ],
        compiler_params=params(60),
        name="prep",
    )(place, prompt_of, query, prefix_key, prefix_value)
    held = [cuts[0]]
    for step in range(1, 8):
        held.append(lax.ppermute(cuts[step], NEAR, [(i, i ^ step) for i in range(8)]))
    swapped = [lax.ppermute(piece, "c", [(0, 1), (1, 0)]) for piece in held]
    got = lax.all_to_all(sent, "y", 0, 0, tiled=True)
    outgoing = pl.pallas_call(
        pack_kernel,
        out_shape=jax.ShapeDtypeStruct((ROWS, HD), jnp.bfloat16),
        in_specs=[VMEM] + [ANY] * 3,
        out_specs=VMEM,
        compiler_params=params(8),
        name="pack",
    )(got, *held[4:7])
    arrived = lax.all_to_all(outgoing.reshape(PROMPTS, 64, HD), FAR, 0, 0, tiled=True)

    near = pl.pallas_call(
        near_kernel,
        grid=(HELD,),
        out_shape=jax.ShapeDtypeStruct((2 * HEADS, HELD, HD), jnp.float32),
        in_specs=[
            SMEM,
            pl.BlockSpec((HELD, HEADS * HD), lambda i: (0, 0)),
            pl.BlockSpec((HELD, KVH * HD), lambda i: (0, 0)),
            pl.BlockSpec((HELD, KVH * HD), lambda i: (0, 0)),
            pl.BlockSpec((1, SUF, KVH * HD), lambda i: (i, 0, 0)),
            pl.BlockSpec((1, SUF, KVH * HD), lambda i: (i, 0, 0)),
        ],
        out_specs=pl.BlockSpec((2 * HEADS, HELD, HD), lambda i: (0, 0, 0)),
        scratch_shapes=[pltpu.VMEM((HEADS, HELD, HD), jnp.float32)],
        compiler_params=params(60),
        cost_estimate=pl.CostEstimate(flops=300_000_000, bytes_accessed=4_500_000, transcendentals=65536),
        name="near",
    )(
        suffix_len,
        query,
        new_key,
        new_value,
        suffix_key,
        suffix_value,
    )

    parcel = pl.pallas_call(
        far_kernel,
        out_shape=jax.ShapeDtypeStruct((RATIO + 1, SLOTS, HD), jnp.bfloat16),
        in_specs=[VMEM] * 17,
        out_specs=VMEM,
        scratch_shapes=[
            pltpu.VMEM((16, 256, PIECE), jnp.float32),
            pltpu.VMEM((RATIO, SLOTS, HD), jnp.bfloat16),
            pltpu.VMEM((RATIO, SLOTS, HD), jnp.bfloat16),
            pltpu.VMEM((SLOTS, HD), jnp.bfloat16),
        ],
        compiler_params=params(16),
        name="far",
    )(arrived.reshape(ROWS, HD), *held, *swapped)
    parcel = parcel.reshape(RATIO + 1, 128, CAP, HD).transpose(1, 0, 2, 3)
    back = lax.all_to_all(parcel, FAR + ("y",), 0, 0, tiled=True)
    back = back.transpose(1, 0, 2, 3).reshape((RATIO + 1) * SLOTS, HD)
    return pl.pallas_call(
        merge_kernel,
        out_shape=jax.ShapeDtypeStruct((HELD, HEADS * HD), jnp.bfloat16),
        in_specs=[SMEM] + [VMEM] * 2,
        out_specs=VMEM,
        compiler_params=params(12),
        name="merge",
    )(prompt_of, back, near)


def solution(mesh):
    fine = Mesh(mesh.devices.reshape(2, 8, 2, 4, 2), ALL)
    grp = ("xh", "z")
    blk = ("xl", "y", "c")
    in_specs = (
        P(ALL),
        P(ALL),
        P(ALL, None),
        P(ALL, None),
        P(ALL, None),
        P(ALL, None, None),
        P(ALL, None, None),
        P(grp, blk, None),
        P(grp, blk, None),
    )
    return jax.shard_map(
        shards, mesh=fine, in_specs=in_specs, out_specs=P(ALL, None), check_vma=False
    )
```

```python
import math

import jax
import jax.numpy as jnp
from jax import lax
from jax.experimental import pallas as pl
from jax.experimental.pallas import tpu as pltpu
from jax.sharding import Mesh, PartitionSpec as P

HD = 128
CAP = 2
HELD = 8
HEADS = 32
KVH = 4
RATIO = 8
PROMPTS = 32
SUF = 256
PIECE = 256
SLOTS = 256
ROWS = SLOTS * RATIO
NEG = -1e30
SCALE = HD ** (-0.5)
LOG2E = 1.4426950408889634
ALL = ("xh", "z", "xl", "y", "c")
NEAR = ("xl", "y")
FAR = ("xh", "z", "xl")


def slots_of(prompt_ref):
    prompts = [prompt_ref[i] for i in range(HELD)]
    slots = []
    for i in range(HELD):
        rank = jnp.int32(0)
        for j in range(i):
            rank = rank + jnp.where(prompts[j] == prompts[i], 1, 0)
        slots.append(prompts[i] * CAP + rank)
    return slots


def spread(values, index):
    picked = jnp.zeros(index.shape, jnp.int32)
    for i, value in enumerate(values):
        picked = jnp.where(index == i, value, picked)
    return picked


def prep_kernel(place_ref, prompt_hbm, query_hbm, key_ref, value_ref, *refs):
    send_refs = refs[:4]
    cut_refs = refs[4:12]
    prompt_ref, query_ref, small_sem, cut_sem = refs[12:]
    small = [
        pltpu.make_async_copy(prompt_hbm, prompt_ref, small_sem.at[0]),
        pltpu.make_async_copy(query_hbm, query_ref, small_sem.at[1]),
    ]
    for copy in small:
        copy.start()
    place = place_ref[0]
    copies = []
    for step, cut_ref in enumerate(cut_refs):
        target = place ^ step
        prompt = target >> 2
        column = pl.multiple_of((target & 3) * HD, HD)
        for n, cache in enumerate((key_ref, value_ref)):
            copies.append(
                pltpu.make_async_copy(
                    cache.at[prompt, :, pl.ds(column, HD)], cut_ref.at[n], cut_sem.at[step, n]
                )
            )
            copies[-1].start()
    for copy in small:
        copy.wait()
    slots = slots_of(prompt_ref)
    lane = lax.broadcasted_iota(jnp.int32, (HELD, HD), 1)
    row = lax.broadcasted_iota(jnp.int32, (HELD, HD), 0)
    tags = jnp.concatenate(
        [spread(slots, lane & 7).astype(jnp.float32), spread(slots, row).astype(jnp.float32)], axis=0
    ).astype(jnp.bfloat16)
    for step, send_ref in enumerate(send_refs):
        first = pl.multiple_of(((place & 3) ^ step) * RATIO * HD, RATIO * HD)
        mine = query_ref[:, pl.ds(first, RATIO * HD)].astype(jnp.float32)
        send_ref[:64] = jnp.concatenate(
            [mine[:, h * HD : (h + 1) * HD] for h in range(RATIO)], axis=0
        ).astype(jnp.bfloat16)
        send_ref[64:] = tags
    for copy in copies:
        copy.wait()


def sources_of(place_ref):
    return [(place_ref[0] & 3) ^ step for step in range(4)]


def pack_kernel(place_ref, *refs):
    got_refs = refs[:4]
    out_ref = refs[-1]
    sources = sources_of(place_ref)
    held = jnp.concatenate([got_ref[:64] for got_ref in got_refs], axis=0)
    tags = [got_ref[64:].astype(jnp.float32)[:1].astype(jnp.int32) for got_ref in got_refs]
    tags = [tags[s] + sources[s] * 512 for s in range(4)]
    half = lax.broadcasted_iota(jnp.int32, (1, HD), 1) < 64
    tag = jnp.concatenate([jnp.where(half, tags[0], tags[1]), jnp.where(half, tags[2], tags[3])], axis=1)
    lane_key = ((lax.broadcasted_iota(jnp.int32, (1, 256), 1) >> 3) & 7) * 64 + tag
    chunk = 512
    for start in range(0, ROWS, chunk):
        row = lax.broadcasted_iota(jnp.int32, (chunk, 1), 0) + start
        row_key = ((row >> 1) & 3) * 512 + ((row >> 3) & 7) * 64 + (row >> 6) * 2 + (row & 1)
        select = (row_key == lane_key).astype(jnp.float32).astype(jnp.bfloat16)
        out_ref[start : start + chunk, :] = jnp.dot(
            select, held, preferred_element_type=jnp.float32
        ).astype(jnp.bfloat16)


def near_kernel(
    len_ref, query_ref, new_key_ref, new_value_ref, key_ref, value_ref, out_ref, heads_ref
):
    step = pl.program_id(0)

    @pl.when(step == 0)
    def _():
        for h in range(HEADS):
            heads_ref[h] = query_ref[:, h * HD : (h + 1) * HD].astype(jnp.float32)

    length = len_ref[step]
    query = heads_ref[:, pl.ds(step, 1), :].reshape(HEADS, HD)
    keys = key_ref[0]
    values = value_ref[0]
    held_row = lax.broadcasted_iota(jnp.int32, (HELD, 1), 0)

    def row_of(ref):
        rows = jnp.where(held_row == step, ref[...].astype(jnp.float32), 0.0)
        return jnp.sum(rows, axis=0, keepdims=True)

    new_key = row_of(new_key_ref)
    new_value = row_of(new_value_ref)

    def spread_heads(row):
        return jnp.concatenate(
            [jnp.broadcast_to(row[:, k * HD : (k + 1) * HD], (RATIO, HD)) for k in range(KVH)], axis=0
        )

    scores = jnp.concatenate(
        [
            lax.dot_general(
                query.astype(jnp.bfloat16),
                keys[:, k * HD : (k + 1) * HD],
                (((1,), (1,)), ((), ())),
                preferred_element_type=jnp.float32,
            )[k * RATIO : (k + 1) * RATIO]
            for k in range(KVH)
        ],
        axis=0,
    ) * SCALE
    own = jnp.sum(query * spread_heads(new_key), axis=1, keepdims=True) * SCALE
    live = lax.broadcasted_iota(jnp.int32, (1, SUF), 1) < length
    scores = jnp.where(live, scores, NEG)
    top = jnp.maximum(jnp.max(scores, axis=1, keepdims=True), own)
    weights = jnp.where(live, jnp.exp(scores - top), 0.0)
    own_weight = jnp.exp(own - top)
    total = jnp.sum(weights, axis=1, keepdims=True) + own_weight
    rounded = weights.astype(jnp.bfloat16)
    mixed = jnp.concatenate(
        [
            jnp.dot(rounded, values[:, k * HD : (k + 1) * HD], preferred_element_type=jnp.float32)[
                k * RATIO : (k + 1) * RATIO
            ]
            for k in range(KVH)
        ],
        axis=0,
    )
    mixed = mixed + own_weight.astype(jnp.bfloat16).astype(jnp.float32) * spread_heads(new_value)
    out_ref[:HEADS, pl.ds(step, 1), :] = (mixed / total).reshape(HEADS, 1, HD)
    out_ref[HEADS:, pl.ds(step, 1), :] = jnp.broadcast_to(top + jnp.log(total), (HEADS, HD)).reshape(
        HEADS, 1, HD
    )


def far_kernel(query_ref, *refs):
    pieces = refs[:16]
    out_ref, score_ref, query_scr, mixed_scr, stat_scr = refs[16:]
    tokens = 16 * PIECE
    queries = query_ref[...].astype(jnp.float32).reshape(32, RATIO, 8, HD)
    biggest = jnp.max(jnp.max(jnp.abs(queries), axis=1).reshape(SLOTS, HD), axis=1, keepdims=True)
    valid = (biggest > 0).astype(jnp.float32)
    row = lax.broadcasted_iota(jnp.int32, (SLOTS, SLOTS), 0)
    lane = lax.broadcasted_iota(jnp.int32, (SLOTS, SLOTS), 1)
    wide = jnp.broadcast_to(valid, (SLOTS, SLOTS)).astype(jnp.bfloat16)
    before = jnp.dot(
        (lane < row).astype(jnp.float32).astype(jnp.bfloat16), wide, preferred_element_type=jnp.float32
    )
    order = jnp.where(valid > 0, before, -1.0).astype(jnp.int32)
    gather = (order == lane).astype(jnp.float32).astype(jnp.bfloat16)
    count = jnp.sum(valid).astype(jnp.int32)
    for h in range(RATIO):
        query_scr[h] = lax.dot_general(
            gather,
            queries[:, h].reshape(SLOTS, HD).astype(jnp.bfloat16),
            (((0,), (0,)), ((), ())),
            preferred_element_type=jnp.float32,
        ).astype(jnp.bfloat16)
    mixed_scr[...] = jnp.zeros_like(mixed_scr)
    stat_scr[...] = jnp.zeros_like(stat_scr)

    def work(start, span):
        block = span * RATIO
        query = query_scr[:, pl.ds(start, span), :].reshape(block, HD)
        peak = jnp.full((block, HD), -jnp.inf, jnp.float32)
        for n, piece in enumerate(pieces):
            scores = lax.dot_general(
                query, piece[0], (((1,), (1,)), ((), ())), preferred_element_type=jnp.float32
            )
            score_ref[n, :block] = scores
            peak = jnp.maximum(peak, jnp.maximum(scores[:, :HD], scores[:, HD:]))
        peak = jnp.max(peak, axis=1, keepdims=True)
        total = jnp.zeros((block, HD), jnp.float32)
        mixed = jnp.zeros((block, HD), jnp.float32)
        for n, piece in enumerate(pieces):
            weights = jnp.exp2((score_ref[n, :block] - peak) * (SCALE * LOG2E))
            total = total + (weights[:, :HD] + weights[:, HD:])
            mixed = mixed + jnp.dot(
                weights.astype(jnp.bfloat16), piece[1], preferred_element_type=jnp.float32
            )
        total = jnp.sum(total, axis=1, keepdims=True)
        mixed_scr[:, pl.ds(start, span), :] = (mixed / total).astype(jnp.bfloat16).reshape(RATIO, span, HD)
        lse = peak * SCALE + jnp.log(total)
        stat_scr[pl.ds(start, span), :] = split_stat(lse.reshape(RATIO, span, 1), span).astype(jnp.bfloat16)

    halves = (count + 15) // 16

    @pl.loop(0, halves // 2)
    def _(index):
        work(pl.multiple_of(index * 32, 32), 32)

    @pl.when(halves % 2 == 1)
    def _():
        work(pl.multiple_of((halves - 1) * 16, 16), 16)

    idle = 1.0 - valid
    mean = sum(piece[1].astype(jnp.float32).reshape(PIECE // 8, 8, HD).sum(axis=0) for piece in pieces)
    mean = jnp.sum(mean, axis=0, keepdims=True) / tokens
    for h in range(RATIO):
        out_ref[h] = (
            jnp.dot(gather, mixed_scr[h], preferred_element_type=jnp.float32) + idle * mean
        ).astype(jnp.bfloat16)
    even = split_stat(jnp.full((RATIO, SLOTS, 1), math.log(tokens), jnp.float32), SLOTS)
    stat = jnp.dot(gather, stat_scr[...], preferred_element_type=jnp.float32) + idle * even
    out_ref[RATIO] = stat.astype(jnp.bfloat16)


def split_stat(lse, span):
    high = lse.astype(jnp.bfloat16).astype(jnp.float32)
    rest = lse - high
    middle = rest.astype(jnp.bfloat16).astype(jnp.float32)
    low = rest - middle
    lane = lax.broadcasted_iota(jnp.int32, (span, HD), 1)
    stat = jnp.zeros((span, HD), jnp.float32)
    for h in range(RATIO):
        for n, part in enumerate((high, middle, low)):
            stat = jnp.where(lane == n * 8 + h, part[h], stat)
    return stat


def merge_kernel(prompt_ref, back_ref, near_ref, out_ref):
    slots = slots_of(prompt_ref)
    count = HEADS * HELD
    row = lax.broadcasted_iota(jnp.int32, (count, 1), 0)
    slot = spread(slots, row & 7)
    head = row >> 3
    row_key = (head & 7) * SLOTS + (slot >> 1) * 8 + (head >> 3) * 2 + (slot & 1)
    select = (row_key == lax.broadcasted_iota(jnp.int32, (1, ROWS), 1)).astype(jnp.float32)
    far = jnp.dot(select.astype(jnp.bfloat16), back_ref[:ROWS, :], preferred_element_type=jnp.float32)
    row = lax.broadcasted_iota(jnp.int32, (KVH * HELD, 1), 0)
    slot = spread(slots, row & 7)
    row_key = (slot >> 1) * 8 + (row >> 3) * 2 + (slot & 1)
    select = (row_key == lax.broadcasted_iota(jnp.int32, (1, SLOTS), 1)).astype(jnp.float32)
    stats = jnp.dot(select.astype(jnp.bfloat16), back_ref[ROWS:, :], preferred_element_type=jnp.float32)
    lane = lax.broadcasted_iota(jnp.int32, (HELD, HD), 1)
    for y in range(KVH):
        stat = jnp.where(lane < 24, stats[y * HELD : (y + 1) * HELD], 0.0)
        for h in range(RATIO):
            head = y * RATIO + h
            far_lse = jnp.sum(jnp.where((lane & 7) == h, stat, 0.0), axis=1, keepdims=True)
            near_lse = near_ref[HEADS + head]
            top = jnp.maximum(far_lse, near_lse)
            far_scale = jnp.exp(far_lse - top)
            near_scale = jnp.exp(near_lse - top)
            merged = far[head * HELD : (head + 1) * HELD] * far_scale + near_ref[head] * near_scale
            out_ref[:, head * HD : (head + 1) * HD] = (merged / (far_scale + near_scale)).astype(
                jnp.bfloat16
            )


VMEM = pl.BlockSpec(memory_space=pltpu.VMEM)
SMEM = pl.BlockSpec(memory_space=pltpu.SMEM)
ANY = pl.BlockSpec(memory_space=pl.ANY)


def params(mib):
    return pltpu.CompilerParams(vmem_limit_bytes=mib << 20)


def shards(
    prompt_of,
    suffix_len,
    query,
    new_key,
    new_value,
    suffix_key,
    suffix_value,
    prefix_key,
    prefix_value,
):
    place = lax.axis_index(NEAR).astype(jnp.int32).reshape(1)
    def along_y(pieces):
        moved = [lax.ppermute(pieces[step], "y", [(i, i ^ step) for i in range(4)]) for step in range(1, 4)]
        return [pieces[0]] + moved

    made = pl.pallas_call(
        prep_kernel,
        out_shape=[jax.ShapeDtypeStruct((80, HD), jnp.bfloat16)] * 4
        + [jax.ShapeDtypeStruct((2, PIECE, HD), jnp.bfloat16)] * 8,
        in_specs=[SMEM, ANY, ANY, ANY, ANY],
        out_specs=[VMEM] * 12,
        scratch_shapes=[
            pltpu.SMEM((HELD,), jnp.int32),
            pltpu.VMEM((HELD, HEADS * HD), jnp.bfloat16),
            pltpu.SemaphoreType.DMA((2,)),
            pltpu.SemaphoreType.DMA((8, 2)),
        ],
        compiler_params=params(60),
        name="prep",
    )(place, prompt_of, query, prefix_key, prefix_value)
    got = along_y(made[:4])
    cuts = made[4:]
    held = [cuts[0]]
    for step in range(1, 8):
        held.append(lax.ppermute(cuts[step], NEAR, [(i, i ^ step) for i in range(8)]))
    swapped = [lax.ppermute(piece, "c", [(0, 1), (1, 0)]) for piece in held]

    first = held[4:6]
    outgoing = pl.pallas_call(
        pack_kernel,
        out_shape=jax.ShapeDtypeStruct((ROWS, HD), jnp.bfloat16),
        in_specs=[SMEM] + [VMEM] * 4 + [ANY] * len(first),
        out_specs=VMEM,
        compiler_params=params(8),
        name="pack",
    )(place, *got, *first)
    arrived = lax.all_to_all(outgoing.reshape(PROMPTS, 64, HD), FAR, 0, 0, tiled=True)

    near = pl.pallas_call(
        near_kernel,
        grid=(HELD,),
        out_shape=jax.ShapeDtypeStruct((2 * HEADS, HELD, HD), jnp.float32),
        in_specs=[
            SMEM,
            pl.BlockSpec((HELD, HEADS * HD), lambda i: (0, 0)),
            pl.BlockSpec((HELD, KVH * HD), lambda i: (0, 0)),
            pl.BlockSpec((HELD, KVH * HD), lambda i: (0, 0)),
            pl.BlockSpec((1, SUF, KVH * HD), lambda i: (i, 0, 0)),
            pl.BlockSpec((1, SUF, KVH * HD), lambda i: (i, 0, 0)),
        ],
        out_specs=pl.BlockSpec((2 * HEADS, HELD, HD), lambda i: (0, 0, 0)),
        scratch_shapes=[pltpu.VMEM((HEADS, HELD, HD), jnp.float32)],
        compiler_params=params(60),
        cost_estimate=pl.CostEstimate(flops=300_000_000, bytes_accessed=4_500_000, transcendentals=65536),
        name="near",
    )(
        suffix_len,
        query,
        new_key,
        new_value,
        suffix_key,
        suffix_value,
    )

    parcel = pl.pallas_call(
        far_kernel,
        out_shape=jax.ShapeDtypeStruct((RATIO + 1, SLOTS, HD), jnp.bfloat16),
        in_specs=[VMEM] * 17,
        out_specs=VMEM,
        scratch_shapes=[
            pltpu.VMEM((16, 256, PIECE), jnp.float32),
            pltpu.VMEM((RATIO, SLOTS, HD), jnp.bfloat16),
            pltpu.VMEM((RATIO, SLOTS, HD), jnp.bfloat16),
            pltpu.VMEM((SLOTS, HD), jnp.bfloat16),
        ],
        compiler_params=params(16),
        name="far",
    )(arrived.reshape(ROWS, HD), *held, *swapped)
    parcel = parcel.reshape(RATIO + 1, 128, CAP, HD).transpose(1, 0, 2, 3)
    back = lax.all_to_all(parcel, FAR + ("y",), 0, 0, tiled=True)
    back = back.transpose(1, 0, 2, 3).reshape((RATIO + 1) * SLOTS, HD)
    return pl.pallas_call(
        merge_kernel,
        out_shape=jax.ShapeDtypeStruct((HELD, HEADS * HD), jnp.bfloat16),
        in_specs=[SMEM] + [VMEM] * 2,
        out_specs=VMEM,
        compiler_params=params(12),
        name="merge",
    )(prompt_of, back, near)


def solution(mesh):
    fine = Mesh(mesh.devices.reshape(2, 8, 2, 4, 2), ALL)
    grp = ("xh", "z")
    blk = ("xl", "y", "c")
    in_specs = (
        P(ALL),
        P(ALL),
        P(ALL, None),
        P(ALL, None),
        P(ALL, None),
        P(ALL, None, None),
        P(ALL, None, None),
        P(grp, blk, None),
        P(grp, blk, None),
    )
    return jax.shard_map(
        shards, mesh=fine, in_specs=in_specs, out_specs=P(ALL, None), check_vma=False
    )
```

```python
import math

import jax
import jax.numpy as jnp
from jax import lax
from jax.experimental import pallas as pl
from jax.experimental.pallas import tpu as pltpu
from jax.sharding import Mesh, PartitionSpec as P

HD = 128
CAP = 2
HELD = 8
HEADS = 32
KVH = 4
RATIO = 8
PROMPTS = 32
SUF = 256
PIECE = 256
SLOTS = 256
ROWS = SLOTS * RATIO
NEG = -1e30
SCALE = HD ** (-0.5)
LOG2E = 1.4426950408889634
ALL = ("xh", "z", "xl", "y", "c")
NEAR = ("xl", "y")
FAR = ("xh", "z", "xl")


def slots_of(prompt_ref):
    prompts = [prompt_ref[i] for i in range(HELD)]
    slots = []
    for i in range(HELD):
        rank = jnp.int32(0)
        for j in range(i):
            rank = rank + jnp.where(prompts[j] == prompts[i], 1, 0)
        slots.append(prompts[i] * CAP + rank)
    return slots


def spread(values, index):
    picked = jnp.zeros(index.shape, jnp.int32)
    for i, value in enumerate(values):
        picked = jnp.where(index == i, value, picked)
    return picked


def prep_kernel(place_ref, prompt_hbm, query_hbm, key_ref, value_ref, *refs):
    send_refs = refs[:4]
    cut_refs = refs[4:12]
    prompt_ref, query_ref, small_sem, cut_sem = refs[12:]
    small = [
        pltpu.make_async_copy(prompt_hbm, prompt_ref, small_sem.at[0]),
        pltpu.make_async_copy(query_hbm, query_ref, small_sem.at[1]),
    ]
    for copy in small:
        copy.start()
    place = place_ref[0]
    copies = []
    for step, cut_ref in enumerate(cut_refs):
        target = place ^ step
        prompt = target >> 2
        column = pl.multiple_of((target & 3) * HD, HD)
        for n, cache in enumerate((key_ref, value_ref)):
            copies.append(
                pltpu.make_async_copy(
                    cache.at[prompt, :, pl.ds(column, HD)], cut_ref.at[n], cut_sem.at[step, n]
                )
            )
            copies[-1].start()
    for copy in small:
        copy.wait()
    slots = slots_of(prompt_ref)
    lane = lax.broadcasted_iota(jnp.int32, (HELD, HD), 1)
    row = lax.broadcasted_iota(jnp.int32, (HELD, HD), 0)
    tags = jnp.concatenate(
        [spread(slots, lane & 7).astype(jnp.float32), spread(slots, row).astype(jnp.float32)], axis=0
    ).astype(jnp.bfloat16)
    for step, send_ref in enumerate(send_refs):
        first = pl.multiple_of(((place & 3) ^ step) * RATIO * HD, RATIO * HD)
        mine = query_ref[:, pl.ds(first, RATIO * HD)].astype(jnp.float32)
        send_ref[:64] = jnp.concatenate(
            [mine[:, h * HD : (h + 1) * HD] for h in range(RATIO)], axis=0
        ).astype(jnp.bfloat16)
        send_ref[64:] = tags
    for copy in copies:
        copy.wait()


def sources_of(place_ref):
    return [(place_ref[0] & 3) ^ step for step in range(4)]


def pack_kernel(place_ref, *refs):
    got_refs = refs[:4]
    out_ref = refs[-1]
    sources = sources_of(place_ref)
    held = jnp.concatenate([got_ref[:64] for got_ref in got_refs], axis=0)
    tags = [got_ref[64:].astype(jnp.float32)[:1].astype(jnp.int32) for got_ref in got_refs]
    tags = [tags[s] + sources[s] * 512 for s in range(4)]
    half = lax.broadcasted_iota(jnp.int32, (1, HD), 1) < 64
    tag = jnp.concatenate([jnp.where(half, tags[0], tags[1]), jnp.where(half, tags[2], tags[3])], axis=1)
    lane_key = ((lax.broadcasted_iota(jnp.int32, (1, 256), 1) >> 3) & 7) * 64 + tag
    chunk = 512
    for start in range(0, ROWS, chunk):
        row = lax.broadcasted_iota(jnp.int32, (chunk, 1), 0) + start
        row_key = ((row >> 1) & 3) * 512 + ((row >> 3) & 7) * 64 + (row >> 6) * 2 + (row & 1)
        select = (row_key == lane_key).astype(jnp.float32).astype(jnp.bfloat16)
        out_ref[start : start + chunk, :] = jnp.dot(
            select, held, preferred_element_type=jnp.float32
        ).astype(jnp.bfloat16)


def near_kernel(
    len_ref, query_ref, new_key_ref, new_value_ref, key_ref, value_ref, out_ref, heads_ref
):
    step = pl.program_id(0)

    @pl.when(step == 0)
    def _():
        for h in range(HEADS):
            heads_ref[h] = query_ref[:, h * HD : (h + 1) * HD].astype(jnp.float32)

    length = len_ref[step]
    query = heads_ref[:, pl.ds(step, 1), :].reshape(HEADS, HD)
    keys = key_ref[0]
    values = value_ref[0]
    held_row = lax.broadcasted_iota(jnp.int32, (HELD, 1), 0)

    def row_of(ref):
        rows = jnp.where(held_row == step, ref[...].astype(jnp.float32), 0.0)
        return jnp.sum(rows, axis=0, keepdims=True)

    new_key = row_of(new_key_ref)
    new_value = row_of(new_value_ref)

    def spread_heads(row):
        return jnp.concatenate(
            [jnp.broadcast_to(row[:, k * HD : (k + 1) * HD], (RATIO, HD)) for k in range(KVH)], axis=0
        )

    scores = jnp.concatenate(
        [
            lax.dot_general(
                query.astype(jnp.bfloat16),
                keys[:, k * HD : (k + 1) * HD],
                (((1,), (1,)), ((), ())),
                preferred_element_type=jnp.float32,
            )[k * RATIO : (k + 1) * RATIO]
            for k in range(KVH)
        ],
        axis=0,
    ) * SCALE
    own = jnp.sum(query * spread_heads(new_key), axis=1, keepdims=True) * SCALE
    live = lax.broadcasted_iota(jnp.int32, (1, SUF), 1) < length
    scores = jnp.where(live, scores, NEG)
    top = jnp.maximum(jnp.max(scores, axis=1, keepdims=True), own)
    weights = jnp.where(live, jnp.exp(scores - top), 0.0)
    own_weight = jnp.exp(own - top)
    total = jnp.sum(weights, axis=1, keepdims=True) + own_weight
    rounded = weights.astype(jnp.bfloat16)
    mixed = jnp.concatenate(
        [
            jnp.dot(rounded, values[:, k * HD : (k + 1) * HD], preferred_element_type=jnp.float32)[
                k * RATIO : (k + 1) * RATIO
            ]
            for k in range(KVH)
        ],
        axis=0,
    )
    mixed = mixed + own_weight.astype(jnp.bfloat16).astype(jnp.float32) * spread_heads(new_value)
    out_ref[:HEADS, pl.ds(step, 1), :] = (mixed / total).reshape(HEADS, 1, HD)
    out_ref[HEADS:, pl.ds(step, 1), :] = jnp.broadcast_to(top + jnp.log(total), (HEADS, HD)).reshape(
        HEADS, 1, HD
    )


def far_kernel(query_ref, *refs):
    pieces = refs[:16]
    out_ref, score_ref, query_scr, mixed_scr, stat_scr = refs[16:]
    tokens = 16 * PIECE
    queries = query_ref[...].astype(jnp.float32).reshape(32, RATIO, 8, HD)
    biggest = jnp.max(jnp.max(jnp.abs(queries), axis=1).reshape(SLOTS, HD), axis=1, keepdims=True)
    valid = (biggest > 0).astype(jnp.float32)
    row = lax.broadcasted_iota(jnp.int32, (SLOTS, SLOTS), 0)
    lane = lax.broadcasted_iota(jnp.int32, (SLOTS, SLOTS), 1)
    wide = jnp.broadcast_to(valid, (SLOTS, SLOTS)).astype(jnp.bfloat16)
    before = jnp.dot(
        (lane < row).astype(jnp.float32).astype(jnp.bfloat16), wide, preferred_element_type=jnp.float32
    )
    order = jnp.where(valid > 0, before, -1.0).astype(jnp.int32)
    gather = (order == lane).astype(jnp.float32).astype(jnp.bfloat16)
    count = jnp.sum(valid).astype(jnp.int32)
    for h in range(RATIO):
        query_scr[h] = lax.dot_general(
            gather,
            queries[:, h].reshape(SLOTS, HD).astype(jnp.bfloat16),
            (((0,), (0,)), ((), ())),
            preferred_element_type=jnp.float32,
        ).astype(jnp.bfloat16)
    mixed_scr[...] = jnp.zeros_like(mixed_scr)
    stat_scr[...] = jnp.zeros_like(stat_scr)

    def work(start, span):
        block = span * RATIO
        query = query_scr[:, pl.ds(start, span), :].reshape(block, HD)
        peak = jnp.full((block, HD), -jnp.inf, jnp.float32)
        for n, piece in enumerate(pieces):
            scores = lax.dot_general(
                query, piece[0], (((1,), (1,)), ((), ())), preferred_element_type=jnp.float32
            )
            score_ref[n, :block] = scores
            peak = jnp.maximum(peak, jnp.maximum(scores[:, :HD], scores[:, HD:]))
        peak = jnp.max(peak, axis=1, keepdims=True)
        total = jnp.zeros((block, HD), jnp.float32)
        mixed = jnp.zeros((block, HD), jnp.float32)
        for n, piece in enumerate(pieces):
            weights = jnp.exp2((score_ref[n, :block] - peak) * (SCALE * LOG2E))
            total = total + (weights[:, :HD] + weights[:, HD:])
            mixed = mixed + jnp.dot(
                weights.astype(jnp.bfloat16), piece[1], preferred_element_type=jnp.float32
            )
        total = jnp.sum(total, axis=1, keepdims=True)
        mixed_scr[:, pl.ds(start, span), :] = (mixed / total).astype(jnp.bfloat16).reshape(RATIO, span, HD)
        lse = peak * SCALE + jnp.log(total)
        stat_scr[pl.ds(start, span), :] = split_stat(lse.reshape(RATIO, span, 1), span).astype(jnp.bfloat16)

    halves = (count + 15) // 16

    @pl.loop(0, halves // 2)
    def _(index):
        work(pl.multiple_of(index * 32, 32), 32)

    @pl.when(halves % 2 == 1)
    def _():
        work(pl.multiple_of((halves - 1) * 16, 16), 16)

    idle = 1.0 - valid
    mean = sum(piece[1].astype(jnp.float32).reshape(PIECE // 8, 8, HD).sum(axis=0) for piece in pieces)
    mean = jnp.sum(mean, axis=0, keepdims=True) / tokens
    for h in range(RATIO):
        out_ref[h] = (
            jnp.dot(gather, mixed_scr[h], preferred_element_type=jnp.float32) + idle * mean
        ).astype(jnp.bfloat16)
    even = split_stat(jnp.full((RATIO, SLOTS, 1), math.log(tokens), jnp.float32), SLOTS)
    stat = jnp.dot(gather, stat_scr[...], preferred_element_type=jnp.float32) + idle * even
    out_ref[RATIO] = stat.astype(jnp.bfloat16)


def split_stat(lse, span):
    high = lse.astype(jnp.bfloat16).astype(jnp.float32)
    rest = lse - high
    middle = rest.astype(jnp.bfloat16).astype(jnp.float32)
    low = rest - middle
    lane = lax.broadcasted_iota(jnp.int32, (span, HD), 1)
    stat = jnp.zeros((span, HD), jnp.float32)
    for h in range(RATIO):
        for n, part in enumerate((high, middle, low)):
            stat = jnp.where(lane == n * 8 + h, part[h], stat)
    return stat


def merge_kernel(prompt_ref, back_ref, near_ref, out_ref):
    slots = slots_of(prompt_ref)
    count = HEADS * HELD
    row = lax.broadcasted_iota(jnp.int32, (count, 1), 0)
    slot = spread(slots, row & 7)
    head = row >> 3
    row_key = (head & 7) * SLOTS + (slot >> 1) * 8 + (head >> 3) * 2 + (slot & 1)
    select = (row_key == lax.broadcasted_iota(jnp.int32, (1, ROWS), 1)).astype(jnp.float32)
    far = jnp.dot(select.astype(jnp.bfloat16), back_ref[:ROWS, :], preferred_element_type=jnp.float32)
    row = lax.broadcasted_iota(jnp.int32, (KVH * HELD, 1), 0)
    slot = spread(slots, row & 7)
    row_key = (slot >> 1) * 8 + (row >> 3) * 2 + (slot & 1)
    select = (row_key == lax.broadcasted_iota(jnp.int32, (1, SLOTS), 1)).astype(jnp.float32)
    stats = jnp.dot(select.astype(jnp.bfloat16), back_ref[ROWS:, :], preferred_element_type=jnp.float32)
    lane = lax.broadcasted_iota(jnp.int32, (HELD, HD), 1)
    for y in range(KVH):
        stat = jnp.where(lane < 24, stats[y * HELD : (y + 1) * HELD], 0.0)
        for h in range(RATIO):
            head = y * RATIO + h
            far_lse = jnp.sum(jnp.where((lane & 7) == h, stat, 0.0), axis=1, keepdims=True)
            near_lse = near_ref[HEADS + head]
            top = jnp.maximum(far_lse, near_lse)
            far_scale = jnp.exp(far_lse - top)
            near_scale = jnp.exp(near_lse - top)
            merged = far[head * HELD : (head + 1) * HELD] * far_scale + near_ref[head] * near_scale
            out_ref[:, head * HD : (head + 1) * HD] = (merged / (far_scale + near_scale)).astype(
                jnp.bfloat16
            )


VMEM = pl.BlockSpec(memory_space=pltpu.VMEM)
SMEM = pl.BlockSpec(memory_space=pltpu.SMEM)
ANY = pl.BlockSpec(memory_space=pl.ANY)


def params(mib):
    return pltpu.CompilerParams(vmem_limit_bytes=mib << 20)


def shards(
    prompt_of,
    suffix_len,
    query,
    new_key,
    new_value,
    suffix_key,
    suffix_value,
    prefix_key,
    prefix_value,
):
    place = lax.axis_index(NEAR).astype(jnp.int32).reshape(1)
    def along_y(pieces):
        moved = [lax.ppermute(pieces[step], "y", [(i, i ^ step) for i in range(4)]) for step in range(1, 4)]
        return [pieces[0]] + moved

    made = pl.pallas_call(
        prep_kernel,
        out_shape=[jax.ShapeDtypeStruct((80, HD), jnp.bfloat16)] * 4
        + [jax.ShapeDtypeStruct((2, PIECE, HD), jnp.bfloat16)] * 8,
        in_specs=[SMEM, ANY, ANY, ANY, ANY],
        out_specs=[VMEM] * 12,
        scratch_shapes=[
            pltpu.SMEM((HELD,), jnp.int32),
            pltpu.VMEM((HELD, HEADS * HD), jnp.bfloat16),
            pltpu.SemaphoreType.DMA((2,)),
            pltpu.SemaphoreType.DMA((8, 2)),
        ],
        compiler_params=params(60),
        name="prep",
    )(place, prompt_of, query, prefix_key, prefix_value)
    got = along_y(made[:4])
    cuts = made[4:]
    held = [cuts[0]]
    for step in range(1, 8):
        held.append(lax.ppermute(cuts[step], NEAR, [(i, i ^ step) for i in range(8)]))
    swapped = [lax.ppermute(piece, "c", [(0, 1), (1, 0)]) for piece in held]

    first = [held[4], held[6]]
    outgoing = pl.pallas_call(
        pack_kernel,
        out_shape=jax.ShapeDtypeStruct((ROWS, HD), jnp.bfloat16),
        in_specs=[SMEM] + [VMEM] * 4 + [ANY] * len(first),
        out_specs=VMEM,
        compiler_params=params(8),
        name="pack",
    )(place, *got, *first)
    arrived = lax.all_to_all(outgoing.reshape(PROMPTS, 64, HD), FAR, 0, 0, tiled=True)

    near = pl.pallas_call(
        near_kernel,
        grid=(HELD,),
        out_shape=jax.ShapeDtypeStruct((2 * HEADS, HELD, HD), jnp.float32),
        in_specs=[
            SMEM,
            pl.BlockSpec((HELD, HEADS * HD), lambda i: (0, 0)),
            pl.BlockSpec((HELD, KVH * HD), lambda i: (0, 0)),
            pl.BlockSpec((HELD, KVH * HD), lambda i: (0, 0)),
            pl.BlockSpec((1, SUF, KVH * HD), lambda i: (i, 0, 0)),
            pl.BlockSpec((1, SUF, KVH * HD), lambda i: (i, 0, 0)),
        ],
        out_specs=pl.BlockSpec((2 * HEADS, HELD, HD), lambda i: (0, 0, 0)),
        scratch_shapes=[pltpu.VMEM((HEADS, HELD, HD), jnp.float32)],
        compiler_params=params(60),
        cost_estimate=pl.CostEstimate(flops=300_000_000, bytes_accessed=4_500_000, transcendentals=65536),
        name="near",
    )(
        suffix_len,
        query,
        new_key,
        new_value,
        suffix_key,
        suffix_value,
    )

    parcel = pl.pallas_call(
        far_kernel,
        out_shape=jax.ShapeDtypeStruct((RATIO + 1, SLOTS, HD), jnp.bfloat16),
        in_specs=[VMEM] * 17,
        out_specs=VMEM,
        scratch_shapes=[
            pltpu.VMEM((16, 256, PIECE), jnp.float32),
            pltpu.VMEM((RATIO, SLOTS, HD), jnp.bfloat16),
            pltpu.VMEM((RATIO, SLOTS, HD), jnp.bfloat16),
            pltpu.VMEM((SLOTS, HD), jnp.bfloat16),
        ],
        compiler_params=params(16),
        name="far",
    )(arrived.reshape(ROWS, HD), *held, *swapped)
    parcel = parcel.reshape(RATIO + 1, 128, CAP, HD).transpose(1, 0, 2, 3)
    back = lax.all_to_all(parcel, FAR + ("y",), 0, 0, tiled=True)
    back = back.transpose(1, 0, 2, 3).reshape((RATIO + 1) * SLOTS, HD)
    return pl.pallas_call(
        merge_kernel,
        out_shape=jax.ShapeDtypeStruct((HELD, HEADS * HD), jnp.bfloat16),
        in_specs=[SMEM] + [VMEM] * 2,
        out_specs=VMEM,
        compiler_params=params(12),
        name="merge",
    )(prompt_of, back, near)


def solution(mesh):
    fine = Mesh(mesh.devices.reshape(2, 8, 2, 4, 2), ALL)
    grp = ("xh", "z")
    blk = ("xl", "y", "c")
    in_specs = (
        P(ALL),
        P(ALL),
        P(ALL, None),
        P(ALL, None),
        P(ALL, None),
        P(ALL, None, None),
        P(ALL, None, None),
        P(grp, blk, None),
        P(grp, blk, None),
    )
    return jax.shard_map(
        shards, mesh=fine, in_specs=in_specs, out_specs=P(ALL, None), check_vma=False
    )
```

```python
import math

import jax
import jax.numpy as jnp
from jax import lax
from jax.experimental import pallas as pl
from jax.experimental.pallas import tpu as pltpu
from jax.sharding import Mesh, PartitionSpec as P

HD = 128
CAP = 2
HELD = 8
HEADS = 32
KVH = 4
RATIO = 8
PROMPTS = 32
SUF = 256
PIECE = 256
SLOTS = 256
ROWS = SLOTS * RATIO
NEG = -1e30
SCALE = HD ** (-0.5)
LOG2E = 1.4426950408889634
ALL = ("xh", "z", "xl", "y", "c")
NEAR = ("xl", "y")
FAR = ("xh", "z", "xl")


def slots_of(prompt_ref):
    prompts = [prompt_ref[i] for i in range(HELD)]
    slots = []
    for i in range(HELD):
        rank = jnp.int32(0)
        for j in range(i):
            rank = rank + jnp.where(prompts[j] == prompts[i], 1, 0)
        slots.append(prompts[i] * CAP + rank)
    return slots


def spread(values, index):
    picked = jnp.zeros(index.shape, jnp.int32)
    for i, value in enumerate(values):
        picked = jnp.where(index == i, value, picked)
    return picked


def prep_kernel(place_ref, prompt_hbm, query_hbm, key_ref, value_ref, *refs):
    send_refs = refs[:4]
    cut_refs = refs[4:12]
    prompt_ref, query_ref, small_sem, cut_sem = refs[12:]
    small = [
        pltpu.make_async_copy(prompt_hbm, prompt_ref, small_sem.at[0]),
        pltpu.make_async_copy(query_hbm, query_ref, small_sem.at[1]),
    ]
    for copy in small:
        copy.start()
    place = place_ref[0]
    copies = []
    for step, cut_ref in enumerate(cut_refs):
        target = place ^ step
        prompt = target >> 2
        column = pl.multiple_of((target & 3) * HD, HD)
        for n, cache in enumerate((key_ref, value_ref)):
            copies.append(
                pltpu.make_async_copy(
                    cache.at[prompt, :, pl.ds(column, HD)], cut_ref.at[n], cut_sem.at[step, n]
                )
            )
            copies[-1].start()
    for copy in small:
        copy.wait()
    slots = slots_of(prompt_ref)
    lane = lax.broadcasted_iota(jnp.int32, (HELD, HD), 1)
    row = lax.broadcasted_iota(jnp.int32, (HELD, HD), 0)
    tags = jnp.concatenate(
        [spread(slots, lane & 7).astype(jnp.float32), spread(slots, row).astype(jnp.float32)], axis=0
    ).astype(jnp.bfloat16)
    for step, send_ref in enumerate(send_refs):
        first = pl.multiple_of(((place & 3) ^ step) * RATIO * HD, RATIO * HD)
        mine = query_ref[:, pl.ds(first, RATIO * HD)].astype(jnp.float32)
        send_ref[:64] = jnp.concatenate(
            [mine[:, h * HD : (h + 1) * HD] for h in range(RATIO)], axis=0
        ).astype(jnp.bfloat16)
        send_ref[64:] = tags
    for copy in copies:
        copy.wait()


def sources_of(place_ref):
    return [(place_ref[0] & 3) ^ step for step in range(4)]


def pack_kernel(place_ref, *refs):
    got_refs = refs[:4]
    out_ref = refs[-1]
    sources = sources_of(place_ref)
    held = jnp.concatenate([got_ref[:64] for got_ref in got_refs], axis=0)
    tags = [got_ref[64:].astype(jnp.float32)[:1].astype(jnp.int32) for got_ref in got_refs]
    tags = [tags[s] + sources[s] * 512 for s in range(4)]
    half = lax.broadcasted_iota(jnp.int32, (1, HD), 1) < 64
    tag = jnp.concatenate([jnp.where(half, tags[0], tags[1]), jnp.where(half, tags[2], tags[3])], axis=1)
    lane_key = ((lax.broadcasted_iota(jnp.int32, (1, 256), 1) >> 3) & 7) * 64 + tag
    chunk = 512
    for start in range(0, ROWS, chunk):
        row = lax.broadcasted_iota(jnp.int32, (chunk, 1), 0) + start
        row_key = ((row >> 1) & 3) * 512 + ((row >> 3) & 7) * 64 + (row >> 6) * 2 + (row & 1)
        select = (row_key == lane_key).astype(jnp.float32).astype(jnp.bfloat16)
        out_ref[start : start + chunk, :] = jnp.dot(
            select, held, preferred_element_type=jnp.float32
        ).astype(jnp.bfloat16)


def near_kernel(
    len_ref, query_ref, new_key_ref, new_value_ref, key_ref, value_ref, out_ref, heads_ref
):
    step = pl.program_id(0)

    @pl.when(step == 0)
    def _():
        for h in range(HEADS):
            heads_ref[h] = query_ref[:, h * HD : (h + 1) * HD].astype(jnp.float32)

    length = len_ref[step]
    query = heads_ref[:, pl.ds(step, 1), :].reshape(HEADS, HD)
    keys = key_ref[0]
    values = value_ref[0]
    held_row = lax.broadcasted_iota(jnp.int32, (HELD, 1), 0)

    def row_of(ref):
        rows = jnp.where(held_row == step, ref[...].astype(jnp.float32), 0.0)
        return jnp.sum(rows, axis=0, keepdims=True)

    new_key = row_of(new_key_ref)
    new_value = row_of(new_value_ref)

    def spread_heads(row):
        return jnp.concatenate(
            [jnp.broadcast_to(row[:, k * HD : (k + 1) * HD], (RATIO, HD)) for k in range(KVH)], axis=0
        )

    scores = jnp.concatenate(
        [
            lax.dot_general(
                query.astype(jnp.bfloat16),
                keys[:, k * HD : (k + 1) * HD],
                (((1,), (1,)), ((), ())),
                preferred_element_type=jnp.float32,
            )[k * RATIO : (k + 1) * RATIO]
            for k in range(KVH)
        ],
        axis=0,
    ) * SCALE
    own = jnp.sum(query * spread_heads(new_key), axis=1, keepdims=True) * SCALE
    live = lax.broadcasted_iota(jnp.int32, (1, SUF), 1) < length
    scores = jnp.where(live, scores, NEG)
    top = jnp.maximum(jnp.max(scores, axis=1, keepdims=True), own)
    weights = jnp.where(live, jnp.exp(scores - top), 0.0)
    own_weight = jnp.exp(own - top)
    total = jnp.sum(weights, axis=1, keepdims=True) + own_weight
    rounded = weights.astype(jnp.bfloat16)
    mixed = jnp.concatenate(
        [
            jnp.dot(rounded, values[:, k * HD : (k + 1) * HD], preferred_element_type=jnp.float32)[
                k * RATIO : (k + 1) * RATIO
            ]
            for k in range(KVH)
        ],
        axis=0,
    )
    mixed = mixed + own_weight.astype(jnp.bfloat16).astype(jnp.float32) * spread_heads(new_value)
    out_ref[:HEADS, pl.ds(step, 1), :] = (mixed / total).reshape(HEADS, 1, HD)
    out_ref[HEADS:, pl.ds(step, 1), :] = jnp.broadcast_to(top + jnp.log(total), (HEADS, HD)).reshape(
        HEADS, 1, HD
    )


def far_kernel(query_ref, *refs):
    pieces = refs[:16]
    out_ref, score_ref, query_scr, mixed_scr, stat_scr = refs[16:]
    tokens = 16 * PIECE
    queries = query_ref[...].astype(jnp.float32).reshape(32, RATIO, 8, HD)
    biggest = jnp.max(jnp.max(jnp.abs(queries), axis=1).reshape(SLOTS, HD), axis=1, keepdims=True)
    valid = (biggest > 0).astype(jnp.float32)
    row = lax.broadcasted_iota(jnp.int32, (SLOTS, SLOTS), 0)
    lane = lax.broadcasted_iota(jnp.int32, (SLOTS, SLOTS), 1)
    wide = jnp.broadcast_to(valid, (SLOTS, SLOTS)).astype(jnp.bfloat16)
    before = jnp.dot(
        (lane < row).astype(jnp.float32).astype(jnp.bfloat16), wide, preferred_element_type=jnp.float32
    )
    order = jnp.where(valid > 0, before, -1.0).astype(jnp.int32)
    gather = (order == lane).astype(jnp.float32).astype(jnp.bfloat16)
    count = jnp.sum(valid).astype(jnp.int32)
    for h in range(RATIO):
        query_scr[h] = lax.dot_general(
            gather,
            queries[:, h].reshape(SLOTS, HD).astype(jnp.bfloat16),
            (((0,), (0,)), ((), ())),
            preferred_element_type=jnp.float32,
        ).astype(jnp.bfloat16)
    mixed_scr[...] = jnp.zeros_like(mixed_scr)
    stat_scr[...] = jnp.zeros_like(stat_scr)

    def work(start, span):
        block = span * RATIO
        query = query_scr[:, pl.ds(start, span), :].reshape(block, HD)
        peak = jnp.full((block, HD), -jnp.inf, jnp.float32)
        for n, piece in enumerate(pieces):
            scores = lax.dot_general(
                query, piece[0], (((1,), (1,)), ((), ())), preferred_element_type=jnp.float32
            )
            score_ref[n, :block] = scores
            peak = jnp.maximum(peak, jnp.maximum(scores[:, :HD], scores[:, HD:]))
        peak = jnp.max(peak, axis=1, keepdims=True)
        total = jnp.zeros((block, HD), jnp.float32)
        mixed = jnp.zeros((block, HD), jnp.float32)
        for n, piece in enumerate(pieces):
            weights = jnp.exp2((score_ref[n, :block] - peak) * (SCALE * LOG2E))
            total = total + (weights[:, :HD] + weights[:, HD:])
            mixed = mixed + jnp.dot(
                weights.astype(jnp.bfloat16), piece[1], preferred_element_type=jnp.float32
            )
        total = jnp.sum(total, axis=1, keepdims=True)
        mixed_scr[:, pl.ds(start, span), :] = (mixed / total).astype(jnp.bfloat16).reshape(RATIO, span, HD)
        lse = peak * SCALE + jnp.log(total)
        stat_scr[pl.ds(start, span), :] = split_stat(lse.reshape(RATIO, span, 1), span).astype(jnp.bfloat16)

    halves = (count + 15) // 16

    @pl.loop(0, halves // 2)
    def _(index):
        work(pl.multiple_of(index * 32, 32), 32)

    @pl.when(halves % 2 == 1)
    def _():
        work(pl.multiple_of((halves - 1) * 16, 16), 16)

    idle = 1.0 - valid
    mean = sum(piece[1].astype(jnp.float32).reshape(PIECE // 8, 8, HD).sum(axis=0) for piece in pieces)
    mean = jnp.sum(mean, axis=0, keepdims=True) / tokens
    for h in range(RATIO):
        out_ref[h] = (
            jnp.dot(gather, mixed_scr[h], preferred_element_type=jnp.float32) + idle * mean
        ).astype(jnp.bfloat16)
    even = split_stat(jnp.full((RATIO, SLOTS, 1), math.log(tokens), jnp.float32), SLOTS)
    stat = jnp.dot(gather, stat_scr[...], preferred_element_type=jnp.float32) + idle * even
    out_ref[RATIO] = stat.astype(jnp.bfloat16)


def split_stat(lse, span):
    high = lse.astype(jnp.bfloat16).astype(jnp.float32)
    rest = lse - high
    middle = rest.astype(jnp.bfloat16).astype(jnp.float32)
    low = rest - middle
    lane = lax.broadcasted_iota(jnp.int32, (span, HD), 1)
    stat = jnp.zeros((span, HD), jnp.float32)
    for h in range(RATIO):
        for n, part in enumerate((high, middle, low)):
            stat = jnp.where(lane == n * 8 + h, part[h], stat)
    return stat


def merge_kernel(prompt_ref, back_ref, near_ref, out_ref):
    slots = slots_of(prompt_ref)
    count = HEADS * HELD
    row = lax.broadcasted_iota(jnp.int32, (count, 1), 0)
    slot = spread(slots, row & 7)
    head = row >> 3
    row_key = (head & 7) * SLOTS + (slot >> 1) * 8 + (head >> 3) * 2 + (slot & 1)
    select = (row_key == lax.broadcasted_iota(jnp.int32, (1, ROWS), 1)).astype(jnp.float32)
    far = jnp.dot(select.astype(jnp.bfloat16), back_ref[:ROWS, :], preferred_element_type=jnp.float32)
    row = lax.broadcasted_iota(jnp.int32, (KVH * HELD, 1), 0)
    slot = spread(slots, row & 7)
    row_key = (slot >> 1) * 8 + (row >> 3) * 2 + (slot & 1)
    select = (row_key == lax.broadcasted_iota(jnp.int32, (1, SLOTS), 1)).astype(jnp.float32)
    stats = jnp.dot(select.astype(jnp.bfloat16), back_ref[ROWS:, :], preferred_element_type=jnp.float32)
    lane = lax.broadcasted_iota(jnp.int32, (HELD, HD), 1)
    for y in range(KVH):
        stat = jnp.where(lane < 24, stats[y * HELD : (y + 1) * HELD], 0.0)
        for h in range(RATIO):
            head = y * RATIO + h
            far_lse = jnp.sum(jnp.where((lane & 7) == h, stat, 0.0), axis=1, keepdims=True)
            near_lse = near_ref[HEADS + head]
            top = jnp.maximum(far_lse, near_lse)
            far_scale = jnp.exp(far_lse - top)
            near_scale = jnp.exp(near_lse - top)
            merged = far[head * HELD : (head + 1) * HELD] * far_scale + near_ref[head] * near_scale
            out_ref[:, head * HD : (head + 1) * HD] = (merged / (far_scale + near_scale)).astype(
                jnp.bfloat16
            )


VMEM = pl.BlockSpec(memory_space=pltpu.VMEM)
SMEM = pl.BlockSpec(memory_space=pltpu.SMEM)
ANY = pl.BlockSpec(memory_space=pl.ANY)


def params(mib):
    return pltpu.CompilerParams(vmem_limit_bytes=mib << 20)


def shards(
    prompt_of,
    suffix_len,
    query,
    new_key,
    new_value,
    suffix_key,
    suffix_value,
    prefix_key,
    prefix_value,
):
    place = lax.axis_index(NEAR).astype(jnp.int32).reshape(1)
    def along_y(pieces):
        moved = [lax.ppermute(pieces[step], "y", [(i, i ^ step) for i in range(4)]) for step in range(1, 4)]
        return [pieces[0]] + moved

    made = pl.pallas_call(
        prep_kernel,
        out_shape=[jax.ShapeDtypeStruct((80, HD), jnp.bfloat16)] * 4
        + [jax.ShapeDtypeStruct((2, PIECE, HD), jnp.bfloat16)] * 8,
        in_specs=[SMEM, ANY, ANY, ANY, ANY],
        out_specs=[VMEM] * 12,
        scratch_shapes=[
            pltpu.SMEM((HELD,), jnp.int32),
            pltpu.VMEM((HELD, HEADS * HD), jnp.bfloat16),
            pltpu.SemaphoreType.DMA((2,)),
            pltpu.SemaphoreType.DMA((8, 2)),
        ],
        compiler_params=params(60),
        name="prep",
    )(place, prompt_of, query, prefix_key, prefix_value)
    got = along_y(made[:4])
    cuts = made[4:]
    held = [cuts[0]]
    for step in range(1, 8):
        held.append(lax.ppermute(cuts[step], NEAR, [(i, i ^ step) for i in range(8)]))
    swapped = [lax.ppermute(piece, "c", [(0, 1), (1, 0)]) for piece in held]

    first = [held[4], held[6], swapped[0]]
    outgoing = pl.pallas_call(
        pack_kernel,
        out_shape=jax.ShapeDtypeStruct((ROWS, HD), jnp.bfloat16),
        in_specs=[SMEM] + [VMEM] * 4 + [ANY] * len(first),
        out_specs=VMEM,
        compiler_params=params(8),
        name="pack",
    )(place, *got, *first)
    arrived = lax.all_to_all(outgoing.reshape(PROMPTS, 64, HD), FAR, 0, 0, tiled=True)

    near = pl.pallas_call(
        near_kernel,
        grid=(HELD,),
        out_shape=jax.ShapeDtypeStruct((2 * HEADS, HELD, HD), jnp.float32),
        in_specs=[
            SMEM,
            pl.BlockSpec((HELD, HEADS * HD), lambda i: (0, 0)),
            pl.BlockSpec((HELD, KVH * HD), lambda i: (0, 0)),
            pl.BlockSpec((HELD, KVH * HD), lambda i: (0, 0)),
            pl.BlockSpec((1, SUF, KVH * HD), lambda i: (i, 0, 0)),
            pl.BlockSpec((1, SUF, KVH * HD), lambda i: (i, 0, 0)),
        ],
        out_specs=pl.BlockSpec((2 * HEADS, HELD, HD), lambda i: (0, 0, 0)),
        scratch_shapes=[pltpu.VMEM((HEADS, HELD, HD), jnp.float32)],
        compiler_params=params(60),
        cost_estimate=pl.CostEstimate(flops=300_000_000, bytes_accessed=4_500_000, transcendentals=65536),
        name="near",
    )(
        suffix_len,
        query,
        new_key,
        new_value,
        suffix_key,
        suffix_value,
    )

    parcel = pl.pallas_call(
        far_kernel,
        out_shape=jax.ShapeDtypeStruct((RATIO + 1, SLOTS, HD), jnp.bfloat16),
        in_specs=[VMEM] * 17,
        out_specs=VMEM,
        scratch_shapes=[
            pltpu.VMEM((16, 256, PIECE), jnp.float32),
            pltpu.VMEM((RATIO, SLOTS, HD), jnp.bfloat16),
            pltpu.VMEM((RATIO, SLOTS, HD), jnp.bfloat16),
            pltpu.VMEM((SLOTS, HD), jnp.bfloat16),
        ],
        compiler_params=params(16),
        name="far",
    )(arrived.reshape(ROWS, HD), *held, *swapped)
    parcel = parcel.reshape(RATIO + 1, 128, CAP, HD).transpose(1, 0, 2, 3)
    back = lax.all_to_all(parcel, FAR + ("y",), 0, 0, tiled=True)
    back = back.transpose(1, 0, 2, 3).reshape((RATIO + 1) * SLOTS, HD)
    return pl.pallas_call(
        merge_kernel,
        out_shape=jax.ShapeDtypeStruct((HELD, HEADS * HD), jnp.bfloat16),
        in_specs=[SMEM] + [VMEM] * 2,
        out_specs=VMEM,
        compiler_params=params(12),
        name="merge",
    )(prompt_of, back, near)


def solution(mesh):
    fine = Mesh(mesh.devices.reshape(2, 8, 2, 4, 2), ALL)
    grp = ("xh", "z")
    blk = ("xl", "y", "c")
    in_specs = (
        P(ALL),
        P(ALL),
        P(ALL, None),
        P(ALL, None),
        P(ALL, None),
        P(ALL, None, None),
        P(ALL, None, None),
        P(grp, blk, None),
        P(grp, blk, None),
    )
    return jax.shard_map(
        shards, mesh=fine, in_specs=in_specs, out_specs=P(ALL, None), check_vma=False
    )
```
